128 devices in a mesh: grp: 4 (over z), dp: 32 (over x, y, core).
Axes of the slice: x: 4, y: 4, z: 4, core: 2. Of those that a mesh axis runs over, the one named last changes fastest.
Arguments:
- caption_token_index: int32 [32, 64], P('dp'), may hold values from 0 to 32767
- lengths: int32 [32], P('dp'), may hold values from 1 to 64
- slot_image_pair: int32 [32], P('dp'), may hold values from 0 to 31, each once
- features: bfloat16 [32, 256, 1024], P('dp'), may hold values from -6 to 6
- text_table: bfloat16 [32768, 2048], P(('grp', 'dp')), may hold values from -6 to 6
- latents: bfloat16 [64, 2048], P(None, 'dp'), may hold values from -6 to 6
- sampler_gain: bfloat16 [2048], P('dp'), may hold values from 0.099609375 to 1.8984375
- sampler_query: bfloat16 [2048, 2048], P('dp', 'grp'), may hold values from -0.125 to 0.125
- sampler_source: bfloat16 [1024, 2, 2048], P('dp', None, 'grp'), may hold values from -0.25 to 0.25
- sampler_mixer: bfloat16 [2048, 2048], P('grp', 'dp'), may hold values from -1 to 1
- norm_gain_one: bfloat16 [2048], P('dp'), may hold values from 0.099609375 to 1.8984375
- attention_in: bfloat16 [2048, 3, 2048], P('dp', None, 'grp'), may hold values from -0.1875 to 0.1875
- norm_gain_two: bfloat16 [2048], P(('grp', 'dp')), may hold values from 0.099609375 to 1.8984375
- attention_out: bfloat16 [2048, 2048], P('grp', 'dp'), may hold values from -0.125 to 0.125
- norm_gain_three: bfloat16 [2048], P('dp'), may hold values from 0.099609375 to 1.8984375
- feed_up: bfloat16 [2048, 8192], P('dp', 'grp'), may hold values from -0.125 to 0.125
- norm_gain_four: bfloat16 [8192], P(('grp', 'dp')), may hold values from 0.099609375 to 1.8984375
- feed_down: bfloat16 [8192, 2048], P('grp', 'dp'), may hold values from -0.0625 to 0.0625
- cotangent: bfloat16 [32, 128, 2048], P('dp'), may hold values from -6 to 6
Outputs:
- layer_output: float32 [32, 128, 2048], P('dp')
- input_grad: float32 [32, 128, 2048], P('dp')
- table_grad: float32 [32768, 2048], P(('grp', 'dp'))
- latents_grad: float32 [64, 2048], P(None, 'dp')
- sampler_gain_grad: float32 [2048], P('dp')
- sampler_query_grad: float32 [2048, 2048], P('dp', 'grp')
- sampler_source_grad: float32 [1024, 2, 2048], P('dp', None, 'grp')
- sampler_mixer_grad: float32 [2048, 2048], P('grp', 'dp')
- gain_one_grad: float32 [2048], P('dp')
- attention_in_grad: float32 [2048, 3, 2048], P('dp', None, 'grp')
- gain_two_grad: float32 [2048], P(('grp', 'dp'))
- attention_out_grad: float32 [2048, 2048], P('grp', 'dp')
- gain_three_grad: float32 [2048], P('dp')
- feed_up_grad: float32 [2048, 8192], P('dp', 'grp')
- gain_four_grad: float32 [8192], P(('grp', 'dp'))
- feed_down_grad: float32 [8192, 2048], P('grp', 'dp')
The draws below stay inside these ranges and needn't reach their ends.
Inputs may be any that keep to these rules, and one draw needn't show every extreme that they name: `slot_image_pair`: every pair fills exactly one slot.
All inputs are finite; a program needn't handle non-finite values.
Results may differ from the reference program's by a relative error of at most 0.025.
The reference program's roundings to bfloat16 on the way count: a program that leaves them out, or rounds other values in their place, can miss the bound.
Values may be sent and summed in bfloat16 or wider, within the bound.
No kernel may reach another device: no remote copies, remote signals or barrier semaphores. Data moves between devices by JAX's collectives and lax.ppermute only.
A program may use at most 512 MiB of HBM per device.

```python
import math
import jax
import jax.numpy as jnp
import numpy as np
from jax import lax

MODEL_WIDTH = 2048
HEADS = 32
HD = 64
FF = 8192
VOCAB_ROWS = 32768
FEATURE_WIDTH = 1024
PATCH_COUNT = 256
NL = 64
RHEADS = 16
RHD = 128
SLOT_TOKENS = 128
SLOT_DP = 1
SLOT_TOTAL = 32
CAPTION_SPAN = 64
N_DP = 32


def plant(drawn, own_key, smallest, largest):
    place = [jax.random.randint(jax.random.fold_in(own_key, axis), (), 0, length) for axis, length in enumerate(drawn.shape)]
    widest = drawn.shape.index(max(drawn.shape))
    beside = place[:widest] + [(place[widest] + 1) % drawn.shape[widest]] + place[widest + 1:]
    return drawn.at[tuple(place)].set(smallest).at[tuple(beside)].set(largest)


def levels(own_key, dims, pieces, least, high):
    gain = 1.0
    for dim, blocks in pieces:
        heights = jax.random.uniform(jax.random.fold_in(jax.random.fold_in(own_key, 6), dim), (blocks,), jnp.float32, least / len(pieces), high / len(pieces))
        gain = gain * jnp.repeat(jnp.exp(heights), dims[dim] // blocks).reshape((-1,) + (1,) * (len(dims) - 1 - dim))
    return gain


def cumulative_ranks(amount, lean):
    weights = [(1 << 20) // math.isqrt(grade ** lean) + 1 for grade in range(1, amount + 1)]
    scale = 1 + sum(weights) // (1 << 30)
    return np.cumsum(np.array([max(1, weight // scale) for weight in weights]))


def ranked_ids(key, dims, count, slope):
    table = cumulative_ranks(count, slope)
    pick = jax.random.randint(jax.random.fold_in(key, 1), dims, 0, int(table[count - 1]))
    rank = jnp.searchsorted(jnp.asarray(table, jnp.int32), pick, side="right")
    return jax.random.permutation(jax.random.fold_in(key, 2), count)[rank].astype(jnp.int32)


def bell_draw(rng, extent, scale, bound, shards=(), held_as=jnp.bfloat16):
    array = scale * jax.random.normal(rng, extent, jnp.float32)
    if shards:
        array = array * levels(rng, extent, shards, -0.22, 0.18)
    return jnp.clip(array, -bound, bound).astype(held_as)


def setup_inputs(seed: int = 0) -> dict:
    keys = jax.random.split(jax.random.key(seed), 20)
    caption_token_index = plant(ranked_ids(keys[0], (SLOT_TOTAL, CAPTION_SPAN), VOCAB_ROWS, 2), jax.random.fold_in(keys[0], 3), 0, VOCAB_ROWS - 1).astype(jnp.int32)
    lengths = plant(jax.random.randint(keys[1], (SLOT_TOTAL,), 1, CAPTION_SPAN + 1), jax.random.fold_in(keys[1], 1), 1, CAPTION_SPAN).astype(jnp.int32)
    slot_image_pair = jax.random.permutation(keys[2], SLOT_TOTAL).astype(jnp.int32)
    features = bell_draw(keys[3], (SLOT_TOTAL, PATCH_COUNT, FEATURE_WIDTH), 1.0, 6.0, ((0, 32),))
    text_table = bell_draw(keys[4], (VOCAB_ROWS, MODEL_WIDTH), 1.0, 6.0, ((0, 128),))
    latents = bell_draw(keys[5], (NL, MODEL_WIDTH), 1.0, 6.0, ((1, 32),))
    sampler_gain = jnp.clip(1.0 + 0.18 * jax.random.normal(keys[6], (MODEL_WIDTH,), jnp.float32), 0.099609375, 1.8984375).astype(jnp.bfloat16)
    sampler_query = bell_draw(keys[7], (MODEL_WIDTH, MODEL_WIDTH), MODEL_WIDTH ** -0.5, 0.125, ((0, 32), (1, 4)))
    sampler_source = bell_draw(keys[8], (FEATURE_WIDTH, 2, MODEL_WIDTH), (FEATURE_WIDTH // 2) ** -0.5, 0.25, ((0, 32), (2, 4)))
    sampler_mixer = bell_draw(keys[9], (MODEL_WIDTH, MODEL_WIDTH), (MODEL_WIDTH // 64) ** -0.5, 1.0, ((0, 4), (1, 32)))
    norm_gain_one = jnp.clip(1.0 + 0.18 * jax.random.normal(keys[10], (MODEL_WIDTH,), jnp.float32), 0.099609375, 1.8984375).astype(jnp.bfloat16)
    attention_in = bell_draw(keys[11], (MODEL_WIDTH, 3, MODEL_WIDTH), (MODEL_WIDTH // 2) ** -0.5, 0.1875, ((0, 32), (2, 4)))
    norm_gain_two = jnp.clip(1.0 + 0.18 * jax.random.normal(keys[12], (MODEL_WIDTH,), jnp.float32), 0.099609375, 1.8984375).astype(jnp.bfloat16)
    attention_out = bell_draw(keys[13], (MODEL_WIDTH, MODEL_WIDTH), MODEL_WIDTH ** -0.5, 0.125, ((0, 4), (1, 32)))
    norm_gain_three = jnp.clip(1.0 + 0.18 * jax.random.normal(keys[14], (MODEL_WIDTH,), jnp.float32), 0.099609375, 1.8984375).astype(jnp.bfloat16)
    feed_up = bell_draw(keys[15], (MODEL_WIDTH, FF), MODEL_WIDTH ** -0.5, 0.125, ((0, 32), (1, 4)))
    norm_gain_four = jnp.clip(1.0 + 0.18 * jax.random.normal(keys[16], (FF,), jnp.float32), 0.099609375, 1.8984375).astype(jnp.bfloat16)
    feed_down = bell_draw(keys[17], (FF, MODEL_WIDTH), FF ** -0.5, 0.0625, ((0, 4), (1, 32)))
    cotangent = bell_draw(keys[18], (SLOT_TOTAL, SLOT_TOKENS, MODEL_WIDTH), 1.0, 6.0, ((0, 32),))
    return {"caption_token_index": caption_token_index, "lengths": lengths, "slot_image_pair": slot_image_pair, "features": features, "text_table": text_table, "latents": latents, "sampler_gain": sampler_gain, "sampler_query": sampler_query, "sampler_source": sampler_source, "sampler_mixer": sampler_mixer, "norm_gain_one": norm_gain_one, "attention_in": attention_in, "norm_gain_two": norm_gain_two, "attention_out": attention_out, "norm_gain_three": norm_gain_three, "feed_up": feed_up, "norm_gain_four": norm_gain_four, "feed_down": feed_down, "cotangent": cotangent}


EPSILON = 1e-05
NEG_FILL = -1e+30
HIGHEST = lax.Precision.HIGHEST

@jax.custom_vjp
def low(v):
    return lax.optimization_barrier(v.astype(jnp.bfloat16)).astype(jnp.float32)

@jax.custom_vjp
def low_back(v):
    return v

def low_keep(v):
    return (low(v), None)

def low_pass(kept, grad):
    return (grad,)

def back_keep(v):
    return (v, None)

def back_low(kept, grad):
    return (low(grad),)
low.defvjp(low_keep, low_pass)
low_back.defvjp(back_keep, back_low)

def layer_norm(values, scale_gain):
    center = values - lax.optimization_barrier(jnp.mean(values, axis=-1, keepdims=True))
    spread = lax.optimization_barrier(jnp.mean(center * center, axis=-1, keepdims=True))
    return center * lax.rsqrt(spread + EPSILON) * scale_gain

def sampler_pair(feature, query_heads, latents, sampler_source, sampler_mixer):
    projected = jnp.einsum('nf,fce->nce', feature, sampler_source, precision=HIGHEST)
    key_rows = low(low_back(projected[:, 0])).reshape(PATCH_COUNT, RHEADS, RHD)
    value_rows = low(low_back(projected[:, 1])).reshape(PATCH_COUNT, RHEADS, RHD)
    scores = jnp.einsum('lhe,nhe->hln', query_heads, key_rows, precision=HIGHEST) * RHD ** (-0.5)
    weights = low(jax.nn.softmax(low_back(scores), axis=-1))
    attended = jnp.einsum('hln,nhe->lhe', weights, value_rows, precision=HIGHEST)
    attended = low(low_back(attended.reshape(NL, MODEL_WIDTH)))
    embedded = latents + jnp.dot(attended, sampler_mixer, precision=HIGHEST)
    return low(low_back(embedded))

def text_block(block_rows, block_lengths, block_weights):
    gain_one, attention_in, gain_two, attention_out, gain_three, feed_up, gain_four, feed_down = block_weights
    normed = low(layer_norm(block_rows, gain_one))
    projected = jnp.einsum('bsd,dce->bsce', normed, attention_in, precision=HIGHEST)
    projected_low = low(low_back(projected))
    shape_heads = (block_rows.shape[0], SLOT_TOKENS, HEADS, HD)
    query_heads = projected_low[:, :, 0].reshape(shape_heads)
    key_heads = projected_low[:, :, 1].reshape(shape_heads)
    value_heads = projected_low[:, :, 2].reshape(shape_heads)
    scores = jnp.einsum('bqhe,bkhe->bhqk', query_heads, key_heads, precision=HIGHEST) * HD ** (-0.5)
    scores = low_back(scores)
    positions = jnp.arange(SLOT_TOKENS, dtype=jnp.int32)
    causal = (positions[None, :] <= positions[:, None])[None, None]
    present = positions[None, None, None, :] < NL + block_lengths[:, None, None, None]
    scores = jnp.where(causal & present, scores, NEG_FILL)
    weights = low(jax.nn.softmax(scores, axis=-1))
    attended = jnp.einsum('bhqk,bkhe->bqhe', weights, value_heads, precision=HIGHEST)
    attended = low_back(attended.reshape(block_rows.shape))
    branch = jnp.einsum('bsd,de->bse', low(layer_norm(attended, gain_two)), attention_out, precision=HIGHEST)
    middle = block_rows + low_back(branch)
    hidden = jnp.einsum('bsd,df->bsf', low(layer_norm(middle, gain_three)), feed_up, precision=HIGHEST)
    hidden = jax.nn.gelu(low_back(hidden), approximate=False)
    hidden = low(layer_norm(hidden, gain_four))
    return middle + low_back(jnp.einsum('bsf,fd->bsd', hidden, feed_down, precision=HIGHEST))

def forward(params, start_position, caption_token_index, lengths, slot_image_pair, feature_rows):
    text_table, latents, sampler_gain, sampler_query, sampler_source, sampler_mixer = params[:6]
    block_weights = params[6:]
    query_rows = jnp.dot(low(layer_norm(latents, sampler_gain)), sampler_query, precision=HIGHEST)
    query_heads = low(low_back(query_rows)).reshape(NL, RHEADS, RHD)

    def one_pair(feature):
        return sampler_pair(feature, query_heads, latents, sampler_source, sampler_mixer)
    images = lax.map(jax.checkpoint(one_pair), feature_rows)
    text_rows = low_back(jnp.take(text_table, caption_token_index, axis=0))
    inputs = jnp.concatenate([images[slot_image_pair], text_rows], axis=1) + start_position
    blocks = inputs.reshape(SLOT_DP, N_DP, SLOT_TOKENS, MODEL_WIDTH)
    block_lengths = lengths.reshape(SLOT_DP, N_DP)

    def one_block(operands):
        return text_block(operands[0], operands[1], block_weights)
    output_list = lax.map(jax.checkpoint(one_block), (blocks, block_lengths))
    return output_list.reshape(SLOT_TOTAL, SLOT_TOKENS, MODEL_WIDTH)

def reference(caption_token_index, lengths, slot_image_pair, features, text_table, latents, sampler_gain, sampler_query, sampler_source, sampler_mixer, norm_gain_one, attention_in, norm_gain_two, attention_out, norm_gain_three, feed_up, norm_gain_four, feed_down, cotangent):
    params = tuple((weight.astype(jnp.float32) for weight in (text_table, latents, sampler_gain, sampler_query, sampler_source, sampler_mixer, norm_gain_one, attention_in, norm_gain_two, attention_out, norm_gain_three, feed_up, norm_gain_four, feed_down)))
    feature_rows = features.astype(jnp.float32)
    start_position = jnp.zeros((SLOT_TOTAL, SLOT_TOKENS, MODEL_WIDTH), jnp.float32)

    def whole(weights, shift_rows):
        return forward(weights, shift_rows, caption_token_index, lengths, slot_image_pair, feature_rows)
    result, backward = jax.vjp(whole, params, start_position)
    grads, input_grad = backward(cotangent.astype(jnp.float32))
    return (result, input_grad, grads[0], grads[1], grads[2], grads[3], grads[4], grads[5], grads[6], grads[7], grads[8], grads[9], grads[10], grads[11], grads[12], grads[13])
```

```python
from functools import partial

import jax
import jax.numpy as jnp
from jax import lax
from jax.sharding import PartitionSpec as P

HD = 64
RHD = 128
NL = 64
EPSILON = 1e-05
NEG_FILL = -1e30
GRP = 4
XS = 4
YS = 4
CS = 2
DP = XS * YS * CS
BF = jnp.bfloat16
F32 = jnp.float32


def dot(left, right, left_dims, right_dims):
    return lax.dot_general(
        left, right, (((left_dims,), (right_dims,)), ((), ())), preferred_element_type=F32
    )


def fetch(values, step_x, step_y, step_core):
    pairs = []
    for x in range(XS):
        for y in range(YS):
            for core in range(CS):
                source = (((x + step_x) % XS) * YS + (y + step_y) % YS) * CS + (core ^ step_core)
                pairs.append((source, (x * YS + y) * CS + core))
    return lax.ppermute(values, "dp", pairs)


def coordinates():
    place = lax.axis_index("dp")
    return place // (YS * CS), place // CS % YS, place % CS


def ring(values, axis):
    steps = [(step, 0) if axis == 0 else (0, step) for step in range(4)]
    return [values] + [fetch(values, *step, 0) for step in steps[1:]]


def gather_offsets(values):
    over_y = jnp.stack(ring(values, 1))
    over_x = jnp.stack(ring(over_y, 0))
    return jnp.stack([over_x, fetch(over_x, 0, 0, 1)])


def gather_small(values):
    x, y, core = coordinates()
    rows = gather_offsets(values)
    rows = jnp.roll(rows, (core, x, y), axis=(0, 1, 2))
    rows = jnp.moveaxis(rows, 0, 2)
    return rows.reshape((DP,) + values.shape)


def dp_total(values):
    values = values + fetch(values, 0, 0, 1)
    for axis in (0, 1):
        parts = ring(values, axis)
        values = (parts[0] + parts[2]) + (parts[1] + parts[3])
    return values


def scatter_offsets(values):
    values = values[0] + fetch(values[1], 0, 0, 1)
    values = values[0] + sum(fetch(values[step], -step, 0, 0) for step in range(1, XS))
    return values[0] + sum(fetch(values[step], 0, -step, 0) for step in range(1, YS))


def grp_gather(values):
    spread = jnp.broadcast_to(values[None], (GRP,) + values.shape)
    return lax.all_to_all(spread, "grp", 0, 0)


def grp_scatter(values, sent):
    rows = values.shape[0] // GRP
    blocks = values.astype(sent).reshape(GRP, rows, values.shape[1])
    return lax.all_to_all(blocks, "grp", 0, 0).astype(F32)


def total(parts):
    return (parts[0] + parts[1]) + (parts[2] + parts[3])


def row_norm(values):
    center = values - jnp.mean(values, axis=-1, keepdims=True)
    spread = jnp.mean(center * center, axis=-1, keepdims=True)
    scale_rows = lax.rsqrt(spread + EPSILON)
    return center * scale_rows, scale_rows


def row_norm_back(grad_normed, normed, scale_rows, scale_gain):
    grad_hat = grad_normed * scale_gain
    return scale_rows * (
        grad_hat
        - jnp.mean(grad_hat, axis=-1, keepdims=True)
        - normed * jnp.mean(grad_hat * normed, axis=-1, keepdims=True)
    )


def shards(
    caption_token_index,
    lengths,
    slot_image_pair,
    features,
    text_table,
    latents,
    sampler_gain,
    sampler_query,
    sampler_source,
    sampler_mixer,
    norm_gain_one,
    attention_in,
    norm_gain_two,
    attention_out,
    norm_gain_three,
    feed_up,
    norm_gain_four,
    feed_down,
    cotangent,
):
    group = lax.axis_index("grp")
    place = lax.axis_index("dp")
    width = feed_down.shape[1] * DP
    hidden = feed_down.shape[0] * GRP
    own = width // DP
    local = attention_out.shape[0]
    local_ff = feed_up.shape[1]
    patches, feature_width = features.shape[1:]
    tokens = cotangent.shape[1]
    spans = caption_token_index.shape[1]
    own_rows = tokens // GRP

    quarter = patches // GRP
    feature_part = lax.dynamic_slice_in_dim(features[0], group * quarter, quarter, 0)
    source_part = sampler_source.reshape(own, local)
    first_part = jnp.concatenate(
        [sampler_mixer.T, source_part, feature_part, attention_out.T, attention_in.reshape(own, 3 * local)],
        axis=1,
    )
    second_part = jnp.concatenate([feed_up, feed_down.T], axis=1)
    first_all = lax.all_gather(first_part, "dp", axis=0, tiled=True)
    second_all = lax.all_gather(second_part, "dp", axis=0, tiled=True)
    mixer_t = first_all[:, :local]
    source_weight = first_all[:, local : 2 * local].reshape(feature_width, 2 * local)
    feature_all = first_all[:, 2 * local : 2 * local + feature_width].reshape(DP, quarter, feature_width)
    out_t = first_all[:, 2 * local + feature_width : 3 * local + feature_width]
    in_weight = first_all[:, 3 * local + feature_width :]
    up_weight = second_all[:, :local_ff]
    down_t = second_all[:, local_ff:]

    flat_ids = caption_token_index[0]
    gain_two_pad = jnp.pad(norm_gain_two, (0, own - norm_gain_two.shape[0]))
    small = jnp.stack(
        [
            sampler_gain,
            norm_gain_one,
            norm_gain_three,
            norm_gain_four,
            gain_two_pad,
            (flat_ids // 256).astype(BF),
            (flat_ids % 256).astype(BF),
        ],
        axis=0,
    )
    small = jnp.concatenate([latents.T, small, jnp.zeros((9, own), BF)], axis=0)
    smalls = gather_small(small)
    latent_values = jnp.moveaxis(smalls[:, :own].reshape(width, NL), 1, 0).astype(F32)
    gains = smalls[:, own:].astype(F32)
    query_gain, gain_one, gain_three = (gains[:, i].reshape(width) for i in range(3))
    gain_four = gains[:, 3].reshape(local_ff)
    gain_two = gains[:, 4, : norm_gain_two.shape[0]].reshape(local)
    all_ids = (gains[:, 5] * 256 + gains[:, 6]).astype(jnp.int32)

    latent_hat, latent_scale = row_norm(latent_values)
    query_input = (latent_hat * query_gain).astype(BF)
    query_own = lax.dynamic_slice_in_dim(query_input, place * own, own, 1)
    latent_hat_own = lax.dynamic_slice_in_dim(latent_hat, place * own, own, 1)
    gain_row = jnp.broadcast_to(sampler_gain[None], (8, own))
    query_sums = dp_total(dot(jnp.concatenate([query_own, gain_row], axis=0), sampler_query, 1, 0))
    query_rows = query_sums[:NL]
    gain_rows = query_sums[NL : NL + 1]
    sampler_heads = local // RHD
    query_heads = query_rows.astype(BF).reshape(NL, sampler_heads, RHD)

    table_rows = text_table.shape[0]
    table_block = lax.all_to_all(text_table, "grp", 1, 0, tiled=True)
    x, y, core = coordinates()
    by_offset = jnp.roll(
        jnp.moveaxis(all_ids.reshape(XS, YS, CS, spans), 2, 0), (-core, -x, -y), axis=(0, 1, 2)
    )

    def block_rows(ids):
        span = table_rows * DP
        held = ids % span // table_rows == place
        return jnp.where(held, ids // span * table_rows + ids % table_rows, -1)

    def one_hot(ids):
        return (block_rows(ids)[:, None] == jnp.arange(GRP * table_rows, dtype=jnp.int32)[None]).astype(BF)

    picked = dot(one_hot(by_offset.reshape(-1)), table_block, 1, 0).astype(BF)
    text_cols = scatter_offsets(picked.reshape(CS, XS, YS, spans, local))
    text_rows = jnp.moveaxis(grp_gather(text_cols), 0, 1).reshape(spans, width)

    pair_part = lax.dynamic_index_in_dim(feature_all, slot_image_pair[0], 0, keepdims=False)
    pair_rows = grp_gather(pair_part).reshape(patches, feature_width)
    sources = dot(pair_rows, source_weight, 1, 0).astype(BF)
    key_heads = sources[:, :local].reshape(patches, sampler_heads, RHD)
    value_heads = sources[:, local:].reshape(patches, sampler_heads, RHD)
    sampler_factor = RHD ** (-0.5)
    scores = (
        jnp.einsum("lhe,nhe->hln", query_heads, key_heads, preferred_element_type=F32) * sampler_factor
    )
    exponent = jnp.exp(scores - jnp.max(scores, axis=-1, keepdims=True))
    sampler_prob = exponent / jnp.sum(exponent, axis=-1, keepdims=True)
    sampler_low = sampler_prob.astype(BF)
    sampled = jnp.einsum("hln,nhe->lhe", sampler_low, value_heads, preferred_element_type=F32)
    sampled = sampled.reshape(NL, local).astype(BF)
    mixed = total(grp_scatter(dot(sampled, mixer_t, 1, 1), F32))
    latent_rows = lax.dynamic_slice_in_dim(latent_values, group * (NL // GRP), NL // GRP, 0)
    image_rows = grp_gather((latent_rows + mixed).astype(BF)).reshape(NL, width)

    inputs = jnp.concatenate([image_rows, text_rows], axis=0).astype(F32)
    first_hat, first_scale = row_norm(inputs)
    first_input = (first_hat * gain_one).astype(BF)

    def own_of(values):
        return lax.dynamic_slice_in_dim(values, group * own_rows, own_rows, 0)

    projected = dot(first_input, in_weight, 1, 0).astype(BF)
    heads_here = local // HD
    query_text, key_text, value_text = (
        projected[:, i * local : (i + 1) * local].reshape(tokens, heads_here, HD) for i in range(3)
    )
    positions = jnp.arange(tokens, dtype=jnp.int32)
    allowed = (positions[None, :] <= positions[:, None]) & (positions[None, :] < NL + lengths[0])
    text_factor = HD ** (-0.5)
    scores = jnp.einsum("qhe,khe->hqk", query_text, key_text, preferred_element_type=F32) * text_factor
    scores = jnp.where(allowed[None], scores, NEG_FILL)
    exponent = jnp.exp(scores - jnp.max(scores, axis=-1, keepdims=True))
    probability = exponent / jnp.sum(exponent, axis=-1, keepdims=True)
    weights_low = probability.astype(BF)
    attended = jnp.einsum("hqk,khe->qhe", weights_low, value_text, preferred_element_type=F32)
    attended = attended.reshape(tokens, local)

    second_mean = jnp.mean(attended, axis=-1, keepdims=True)
    second_center = attended - second_mean
    second_square = jnp.sum(second_center * second_center, axis=-1, keepdims=True)
    second_sums = grp_gather(jnp.concatenate([second_mean, second_square], axis=1))
    branch_part = dot((second_center * gain_two).astype(BF), out_t, 1, 1)
    branch_parts = grp_scatter(branch_part, BF)
    gain_out = grp_gather(dot(jnp.broadcast_to(gain_two.astype(BF)[None], (8, local)), out_t, 1, 1)[:1])
    second_means = second_sums[:, :, :1]
    second_all = jnp.mean(second_means, axis=0)
    second_spread = (
        jnp.sum(second_sums[:, :, 1:] + local * jnp.square(second_means - second_all), axis=0) / width
    )
    second_scale = lax.rsqrt(second_spread + EPSILON)
    second_hat = (attended - second_all) * second_scale
    second_input = (second_hat * gain_two).astype(BF)
    shift_own = lax.dynamic_slice_in_dim(second_means - second_all, group * own_rows, own_rows, 1)
    branch = own_of(second_scale) * total(branch_parts + shift_own * gain_out)
    gain_out_total = total(gain_out)

    middle = own_of(inputs) + branch
    third_hat, third_scale = row_norm(middle)
    third_input = grp_gather((third_hat * gain_three).astype(BF)).reshape(tokens, width)
    up_rows = dot(third_input, up_weight, 1, 0)
    activated, gelu_back = jax.vjp(partial(jax.nn.gelu, approximate=False), up_rows)
    grad_output = cotangent[0]
    grad_fourth = dot(grad_output, down_t, 1, 0)
    grad_hat = grad_fourth * gain_four
    fourth_mean = jnp.mean(activated, axis=-1, keepdims=True)
    fourth_center = activated - fourth_mean
    fourth_sums = grp_gather(
        jnp.concatenate(
            [
                fourth_mean,
                jnp.sum(fourth_center * fourth_center, axis=-1, keepdims=True),
                jnp.sum(grad_hat, axis=-1, keepdims=True),
                jnp.sum(grad_hat * fourth_center, axis=-1, keepdims=True),
            ],
            axis=1,
        )
    )
    fourth_means = fourth_sums[:, :, :1]
    fourth_all = jnp.mean(fourth_means, axis=0)
    fourth_shift = fourth_means - fourth_all
    fourth_scale = lax.rsqrt(
        jnp.sum(fourth_sums[:, :, 1:2] + local_ff * fourth_shift * fourth_shift, axis=0) / hidden + EPSILON
    )
    fourth_hat = (activated - fourth_all) * fourth_scale
    fourth_input = (fourth_hat * gain_four).astype(BF)
    sum_grad = total(fourth_sums[:, :, 2:3]) / hidden
    sum_cross = (
        fourth_scale * total(fourth_sums[:, :, 3:] + fourth_shift * fourth_sums[:, :, 2:3]) / hidden
    )
    grad_active = fourth_scale * (grad_hat - sum_grad - fourth_hat * sum_cross)
    grad_up_rows = gelu_back(grad_active)[0].astype(BF)
    grad_gain_four = jnp.sum(grad_fourth * fourth_hat, axis=0)
    grad_third = total(grp_scatter(dot(grad_up_rows, up_weight, 1, 1), BF))

    result = middle + total(grp_scatter(dot(fourth_input, down_t, 1, 1), BF))
    layer_output = grp_gather(result).reshape(1, tokens, width)

    ff_grads = jnp.concatenate(
        [
            dot(third_input, grad_up_rows, 0, 0).astype(BF),
            dot(grad_output, fourth_input, 0, 0).astype(BF),
        ],
        axis=1,
    )
    ff_grads = lax.psum_scatter(ff_grads, "dp", scatter_dimension=0, tiled=True)

    grad_middle = own_of(grad_output).astype(F32) + row_norm_back(
        grad_third, third_hat, third_scale, gain_three
    )
    grad_gain_three = jnp.sum(grad_third * third_hat, axis=0)
    branch_low = grad_middle.astype(BF)
    branch_wide = branch_low.astype(F32)
    second_back = jnp.concatenate(
        [
            jnp.sum(branch_wide * gain_out_total, axis=-1, keepdims=True),
            jnp.sum(branch_wide * branch, axis=-1, keepdims=True),
        ],
        axis=1,
    )
    grad_branch = grp_gather(branch_low).reshape(tokens, width)
    second_back = grp_gather(second_back).reshape(tokens, 2) / width
    grad_gain_three = total(grp_gather(grad_gain_three))

    grad_second = dot(grad_branch, out_t, 1, 0)
    grad_attended = second_scale * (
        grad_second * gain_two - second_back[:, :1] - second_hat * second_back[:, 1:]
    )
    grad_gain_two = jnp.sum(grad_second * second_hat, axis=0)
    grad_att = grad_attended.astype(BF).reshape(tokens, heads_here, HD)
    grad_value = jnp.einsum("hqk,qhe->khe", weights_low, grad_att, preferred_element_type=F32)
    grad_weights = jnp.einsum("qhe,khe->hqk", grad_att, value_text, preferred_element_type=F32)
    grad_scores = probability * (
        grad_weights - jnp.sum(probability * grad_weights, axis=-1, keepdims=True)
    )
    grad_scores = grad_scores.astype(BF)
    grad_query = (
        jnp.einsum("hqk,khe->qhe", grad_scores, key_text, preferred_element_type=F32) * text_factor
    )
    grad_key = (
        jnp.einsum("hqk,qhe->khe", grad_scores, query_text, preferred_element_type=F32) * text_factor
    )
    grad_projected = jnp.concatenate(
        [part.reshape(tokens, local) for part in (grad_query, grad_key, grad_value)], axis=1
    ).astype(BF)
    grad_first = total(grp_scatter(dot(grad_projected, in_weight, 1, 1), BF))
    first_hat_own = own_of(first_hat)
    input_own = grad_middle + row_norm_back(grad_first, first_hat_own, own_of(first_scale), gain_one)
    grad_gain_one = total(grp_gather(jnp.sum(grad_first * first_hat_own, axis=0)))
    input_low = grp_gather(input_own.astype(BF)).reshape(tokens, width)
    input_grad = grp_gather(input_own).reshape(1, tokens, width)

    text_low = lax.dynamic_slice_in_dim(input_low[NL:], group * local, local, 1)
    text_all = gather_offsets(text_low).reshape(DP * spans, local)
    table_sums = dot(one_hot(by_offset.reshape(-1)), text_all, 0, 0).astype(BF)
    table_sums = lax.all_to_all(table_sums, "grp", 0, 1, tiled=True)
    table_grad = table_sums.astype(F32)

    image_low = input_low[:NL]
    grad_sampled = dot(image_low, mixer_t, 1, 0).astype(BF).reshape(NL, sampler_heads, RHD)
    grad_source_value = jnp.einsum("hln,lhe->nhe", sampler_low, grad_sampled, preferred_element_type=F32)
    grad_sampler = jnp.einsum("lhe,nhe->hln", grad_sampled, value_heads, preferred_element_type=F32)
    grad_sampler = sampler_prob * (
        grad_sampler - jnp.sum(sampler_prob * grad_sampler, axis=-1, keepdims=True)
    )
    grad_sampler = grad_sampler.astype(BF)
    grad_query_heads = (
        jnp.einsum("hln,nhe->lhe", grad_sampler, key_heads, preferred_element_type=F32) * sampler_factor
    )
    grad_source_key = (
        jnp.einsum("hln,lhe->nhe", grad_sampler, query_heads, preferred_element_type=F32) * sampler_factor
    )
    grad_sources = jnp.concatenate(
        [grad_source_key.reshape(patches, local), grad_source_value.reshape(patches, local)], axis=1
    ).astype(BF)
    grad_query_total = dp_total(grad_query_heads.reshape(NL, local))
    grad_query_low = grad_query_total.astype(BF)
    grad_query_wide = grad_query_low.astype(F32)
    sampler_query_grad = dot(query_own, grad_query_low, 0, 0)
    sampler_back = jnp.concatenate(
        [
            dot(grad_query_low, sampler_query, 1, 1),
            jnp.sum(grad_query_wide * gain_rows, axis=-1, keepdims=True),
            jnp.sum(grad_query_wide * query_rows, axis=-1, keepdims=True),
        ],
        axis=1,
    )
    sampler_back = total(grp_gather(sampler_back))
    grad_query_norm = sampler_back[:, :own]
    sampler_means = sampler_back[:, own:] / width
    grad_latent_norm = latent_scale * (
        grad_query_norm * sampler_gain.astype(F32)
        - sampler_means[:, :1]
        - latent_hat_own * sampler_means[:, 1:]
    )
    sampler_gain_grad = jnp.sum(grad_query_norm * latent_hat_own, axis=0)

    mixer_and_latents = dot(
        image_low, jnp.concatenate([sampled, jnp.eye(NL, dtype=BF)], axis=1), 0, 0
    ).astype(BF)
    per_own = norm_gain_two.shape[0]
    gain_two_cols = jnp.pad(grad_gain_two.reshape(DP, per_own), ((0, 0), (0, own - per_own)))
    gain_cols = jnp.stack(
        [grad_gain_one, grad_gain_three, grad_gain_four, gain_two_cols.reshape(-1)], axis=1
    ).astype(BF)
    rest = jnp.concatenate(
        [
            dot(first_input, grad_projected, 0, 0).astype(BF),
            dot(grad_branch, second_input, 0, 0).astype(BF),
            dot(pair_rows, grad_sources, 0, 0).astype(BF).reshape(width, local),
            mixer_and_latents,
            gain_cols,
        ],
        axis=1,
    )
    rest = lax.psum_scatter(rest, "dp", scatter_dimension=0, tiled=True).astype(F32)
    cut = 3 * local
    attention_in_grad = rest[:, :cut].reshape(own, 3, local)
    attention_out_grad = rest[:, cut : cut + local].T
    sampler_source_grad = rest[:, cut + local : cut + 2 * local].reshape(own // 2, 2, local)
    sampler_mixer_grad = rest[:, cut + 2 * local : cut + 3 * local].T
    latents_grad = rest[:, cut + 3 * local : cut + 3 * local + NL].T + grad_latent_norm
    gain_grads = rest[:, cut + 3 * local + NL :]
    ff_grads = ff_grads.astype(F32)
    return (
        layer_output,
        input_grad,
        table_grad,
        latents_grad,
        sampler_gain_grad,
        sampler_query_grad,
        sampler_source_grad,
        sampler_mixer_grad,
        gain_grads[:, 0],
        attention_in_grad,
        gain_grads[:per_own, 3],
        attention_out_grad,
        gain_grads[:, 1],
        ff_grads[:, :local_ff],
        gain_grads[:, 2],
        ff_grads[:, local_ff:].T,
    )


def solution(mesh):
    return jax.shard_map(
        shards,
        mesh=mesh,
        in_specs=(
            P("dp", None),
            P("dp"),
            P("dp"),
            P("dp", None, None),
            P(("grp", "dp"), None),
            P(None, "dp"),
            P("dp"),
            P("dp", "grp"),
            P("dp", None, "grp"),
            P("grp", "dp"),
            P("dp"),
            P("dp", None, "grp"),
            P(("grp", "dp")),
            P("grp", "dp"),
            P("dp"),
            P("dp", "grp"),
            P(("grp", "dp")),
            P("grp", "dp"),
            P("dp", None, None),
        ),
        out_specs=(
            P("dp", None, None),
            P("dp", None, None),
            P(("grp", "dp"), None),
            P(None, "dp"),
            P("dp"),
            P("dp", "grp"),
            P("dp", None, "grp"),
            P("grp", "dp"),
            P("dp"),
            P("dp", None, "grp"),
            P(("grp", "dp")),
            P("grp", "dp"),
            P("dp"),
            P("dp", "grp"),
            P(("grp", "dp")),
            P("grp", "dp"),
        ),
        check_vma=False,
    )
```

```python
from functools import partial

import jax
import jax.numpy as jnp
from jax import lax
from jax.experimental import pallas as pl
from jax.experimental.pallas import tpu as pltpu
from jax.sharding import Mesh, PartitionSpec as P

HD = 64
RHD = 128
NL = 64
EPSILON = 1e-05
NEG_FILL = -1e30
GRP = 4
XS = 4
YS = 4
CS = 2
DP = XS * YS * CS
DP_AXES = ("x", "y", "core")
LANES = 128
STATS = 8
KEPT = (4, 4, 2, 2, 4)
VMEM_LIMIT = 56 * 1024 * 1024
BF = jnp.bfloat16
F32 = jnp.float32


def dot(left, right, left_dims, right_dims):
    return lax.dot_general(
        left, right, (((left_dims,), (right_dims,)), ((), ())), preferred_element_type=F32
    )


def fetch(values, step_x, step_y, step_core):
    pairs = []
    for x in range(XS):
        for y in range(YS):
            for core in range(CS):
                source = (((x + step_x) % XS) * YS + (y + step_y) % YS) * CS + (core ^ step_core)
                pairs.append((source, (x * YS + y) * CS + core))
    return lax.ppermute(values, DP_AXES, pairs)


def coordinates():
    place = lax.axis_index(DP_AXES)
    return place // (YS * CS), place // CS % YS, place % CS


def ring(values, axis):
    steps = [(step, 0) if axis == 0 else (0, step) for step in range(4)]
    return [values] + [fetch(values, *step, 0) for step in steps[1:]]


def gather_offsets(values):
    over_y = jnp.stack(ring(values, 1))
    over_x = jnp.stack(ring(over_y, 0))
    return jnp.stack([over_x, fetch(over_x, 0, 0, 1)])


def dp_total(values):
    values = values + fetch(values, 0, 0, 1)
    for axis in (0, 1):
        parts = ring(values, axis)
        values = (parts[0] + parts[2]) + (parts[1] + parts[3])
    return values


def scatter_offsets(values):
    values = values[0] + fetch(values[1], 0, 0, 1)
    values = values[0] + sum(fetch(values[step], -step, 0, 0) for step in range(1, XS))
    return values[0] + sum(fetch(values[step], 0, -step, 0) for step in range(1, YS))


def call(
    body, outs, operands, specs=None, out_specs=None, grid=(1,), scalars=(), scratch=(), after=(), aliases=None
):
    specs = dict(specs or {})
    out_specs = dict(out_specs or {})

    def whole(shape):
        return pl.BlockSpec(shape, lambda *_: (0,) * len(shape))

    def wrapped(*refs):
        held = len(scalars) + len(operands)
        body(*refs[:held], *refs[held + len(after) :])

    in_specs = [specs.get(i, whole(operand.shape)) for i, operand in enumerate(operands)]
    in_specs += [pl.BlockSpec(memory_space=pl.ANY)] * len(after)
    return pl.pallas_call(
        wrapped,
        grid_spec=pltpu.PrefetchScalarGridSpec(
            num_scalar_prefetch=len(scalars),
            grid=grid,
            in_specs=in_specs,
            out_specs=[out_specs.get(i, whole(shape)) for i, (shape, _) in enumerate(outs)],
            scratch_shapes=list(scratch),
        ),
        out_shape=[jax.ShapeDtypeStruct(shape, dtype) for shape, dtype in outs],
        input_output_aliases={len(scalars) + i: out for i, out in (aliases or {}).items()},
        compiler_params=pltpu.CompilerParams(vmem_limit_bytes=VMEM_LIMIT),
    )(*scalars, *operands, *after)


def pair_kernel(pair, features, spread):
    for device in range(GRP):
        spread[device] = features[0]


def sampler_kernel(
    pair, small, query_weight, key_weight, value_weight, mixer, query_gain,
    mixed, latents, latent_hat, latent_scale, query_input, query_rows, sampled, sources, prob,
):
    width = query_weight.shape[1]
    across = jnp.transpose(small[...].astype(F32))
    values = across[:NL]
    latents[...] = values
    hat, scale = row_norm(values)
    latent_hat[...] = hat
    latent_scale[...] = jnp.broadcast_to(scale, latent_scale.shape)
    gain = query_gain[...]
    normed = (hat * gain).astype(BF)
    query_input[...] = normed
    query_rows[:NL, :] = jnp.dot(normed, query_weight[...], preferred_element_type=F32)
    query_rows[NL:, :] = jnp.dot(
        jnp.broadcast_to(gain, (16, gain.shape[1])).astype(BF), query_weight[...], preferred_element_type=F32
    )
    query = query_rows[:NL, :].astype(BF)
    rows = pair[...]
    keys, values = (
        jnp.dot(rows, weight[...].reshape(rows.shape[1], width), preferred_element_type=F32).astype(BF)
        for weight in (key_weight, value_weight)
    )
    sources[:, :width] = keys
    sources[:, width:] = values
    for head in range(width // RHD):
        columns = slice(head * RHD, (head + 1) * RHD)
        scores = dot(query[:, columns], keys[:, columns], 1, 1) * RHD ** (-0.5)
        exponent = jnp.exp(scores - jnp.max(scores, axis=-1, keepdims=True))
        weights = exponent / jnp.sum(exponent, axis=-1, keepdims=True)
        prob[head] = weights
        sampled[:, columns] = jnp.dot(
            weights.astype(BF), values[:, columns], preferred_element_type=F32
        ).astype(BF)
    mixed[...] = dot(sampled[...], mixer[...], 1, 1).reshape(mixed.shape)


def image_kernel(place, parts, latents, images):
    mixed = (parts[0] + parts[1]) + (parts[2] + parts[3])
    rows = (latents[...] + mixed).astype(BF)
    for device in range(GRP):
        images[device] = rows


def lanes_of(numbers, dtype):
    rows = numbers[0].shape[0]
    lane = lax.broadcasted_iota(jnp.int32, (rows, LANES), 1)
    held = jnp.zeros((rows, LANES), F32)
    for number, column in enumerate(numbers):
        held = jnp.where(lane == number, column, held)
    return held.astype(dtype)


def in_pairs(numbers):
    pairs = []
    for number in numbers:
        high = number.astype(BF).astype(F32)
        pairs += [high, number - high]
    return pairs


def from_pairs(lanes, number):
    wide = lanes.astype(F32)
    return wide[:, 2 * number : 2 * number + 1] + wide[:, 2 * number + 1 : 2 * number + 2]


def put_rows(columns):
    tokens = columns[0].shape[0]
    lane = lax.broadcasted_iota(jnp.int32, (tokens, tokens), 1)
    held = jnp.zeros((tokens, tokens), F32)
    for number, column in enumerate(columns):
        held = jnp.where(lane == number, column, held)
    return jnp.transpose(held)[:STATS]


def take_columns(stats):
    return jnp.transpose(stats[:, :STATS, :].reshape(GRP * STATS, stats.shape[2]))


def put_vector(small, first, vector):
    for i in range(vector.shape[1] // LANES):
        small[first + i : first + i + 1, :] = vector[:, i * LANES : (i + 1) * LANES]


def attention_kernel(
    length, image, text, gain_one, in_weight, gain_two, out_t,
    inputs, first_input, projected, prob, attended, parts, vectors,
):
    images = NL
    inputs[:images, :] = image[...].reshape(images, inputs.shape[1])
    local = gain_two.shape[1]
    for device in range(GRP):
        inputs[images:, device * local : (device + 1) * local] = text[device]
    hat, _ = row_norm(inputs[...].astype(F32))
    first_input[...] = (hat * gain_one[...]).astype(BF)
    projected[...] = dot(first_input[...], in_weight[...], 1, 0).astype(BF)
    tokens = inputs.shape[0]
    query = lax.broadcasted_iota(jnp.int32, (tokens, tokens), 0)
    key = lax.broadcasted_iota(jnp.int32, (tokens, tokens), 1)
    allowed = (key <= query) & (key < NL + length[0])
    for head in range(local // HD):
        query_head, key_head, value_head = (
            projected[:, i * local + head * HD : i * local + (head + 1) * HD] for i in range(3)
        )
        scores = jnp.where(allowed, dot(query_head, key_head, 1, 1) * HD ** (-0.5), NEG_FILL)
        exponent = jnp.exp(scores - jnp.max(scores, axis=-1, keepdims=True))
        weights = exponent / jnp.sum(exponent, axis=-1, keepdims=True)
        prob[head] = weights
        attended[:, head * HD : (head + 1) * HD] = jnp.dot(
            weights.astype(BF), value_head, preferred_element_type=F32
        )
    values = attended[...]
    mean = jnp.mean(values, axis=-1, keepdims=True)
    center = values - mean
    square = jnp.sum(center * center, axis=-1, keepdims=True)
    gains = gain_two[...]
    width = inputs.shape[1]
    blocks = dot((center * gains).astype(BF), out_t[...], 1, 1).astype(BF)
    parts[:, :, :width] = blocks.reshape(GRP, tokens // GRP, width)
    numbers = lanes_of(in_pairs([mean, square]), BF)
    parts[:, :, width : width + LANES] = numbers.reshape(GRP, tokens // GRP, LANES)
    products = dot(jnp.broadcast_to(gains, (16, local)).astype(BF), out_t[...], 1, 1)[:1]
    for number, vector in enumerate(in_pairs([products])):
        put_vector(vectors, number * (width // LANES), vector)
    for device in range(GRP):
        parts[device, :, width + LANES :] = vectors[...].astype(BF)


def joined_stats(means, squares, own, full):
    mean = ((means[0] + means[1]) + (means[2] + means[3])) / GRP
    shifts = [part - mean for part in means]
    square = sum(squares[i] + own * shifts[i] * shifts[i] for i in range(GRP))
    return mean, lax.rsqrt(square / full + EPSILON), shifts


def middle_kernel(place, parts, inputs, gain_three, middle, branch, third_input, numbers, gain_out):
    own_rows, width = inputs.shape
    count = width // LANES
    lanes = [parts[i, :, width : width + LANES] for i in range(GRP)]
    mean, scale, shifts = joined_stats(
        [from_pairs(lane, 0) for lane in lanes], [from_pairs(lane, 1) for lane in lanes], width // GRP, width
    )
    vectors = []
    for device in range(GRP):
        pairs = parts[device, :, width + LANES :].astype(F32)
        rows = pairs[:count] + pairs[count:]
        vectors.append(jnp.concatenate([rows[i : i + 1] for i in range(count)], axis=1))
    gain_out[...] = (vectors[0] + vectors[1]) + (vectors[2] + vectors[3])
    gathered = sum(parts[i, :, :width].astype(F32) + shifts[i] * vectors[i] for i in range(GRP))
    added = scale * gathered
    branch[...] = added
    rows = inputs[...].astype(F32) + added
    middle[...] = rows
    numbers[...] = lanes_of([mean, scale], F32)
    hat, _ = row_norm(rows)
    low = (hat * gain_three[...]).astype(BF)
    for device in range(GRP):
        third_input[device] = low


def hidden_kernel(
    third_input, cotangent, gain_four, up_weight, down_t, activated, slope, grad_fourth, stats, third_rows
):
    step = pl.program_id(0)
    block = up_weight.shape[1]
    rows = third_input[...].reshape(cotangent.shape)
    columns = pl.ds(step * block, block)
    values = dot(rows, up_weight[...], 1, 0)
    normal = 0.5 * (1.0 + lax.erf(values * (0.5**0.5)))
    activated[:, columns] = values * normal
    slope[:, columns] = normal + values * jnp.exp(-0.5 * values * values) * 0.3989422804014327
    grad_fourth[:, columns] = dot(cotangent[...], down_t[...], 1, 0)

    @pl.when(step == pl.num_programs(0) - 1)
    def _():
        third_rows[...] = rows
        active = activated[...]
        grad_hat = grad_fourth[...] * gain_four[...]
        mean = jnp.mean(active, axis=-1, keepdims=True)
        center = active - mean
        numbers = put_rows(
            [
                mean,
                jnp.sum(center * center, axis=-1, keepdims=True),
                jnp.sum(grad_hat, axis=-1, keepdims=True),
                jnp.sum(grad_hat * center, axis=-1, keepdims=True),
            ],
        )
        for device in range(GRP):
            stats[device] = numbers


def hidden_back_kernel(
    stats, activated, slope, grad_fourth, gain_four, up_weight,
    fourth_input, grad_up, grad_gain, parts, held, summed,
):
    step = pl.program_id(0)
    block = up_weight.shape[1]
    own = block * pl.num_programs(0)
    full = own * GRP

    @pl.when(step == 0)
    def _():
        columns = take_columns(stats[...])
        means, squares = ([columns[:, STATS * i + n : STATS * i + n + 1] for i in range(GRP)] for n in (0, 1))
        mean, scale, shifts = joined_stats(means, squares, own, full)
        sums = [columns[:, STATS * i + 2 : STATS * i + 3] for i in range(GRP)]
        crosses = [columns[:, STATS * i + 3 : STATS * i + 4] + shifts[i] * sums[i] for i in range(GRP)]
        lane = lax.broadcasted_iota(jnp.int32, held.shape, 1)
        numbers = [
            mean,
            scale,
            ((sums[0] + sums[1]) + (sums[2] + sums[3])) / full,
            scale * ((crosses[0] + crosses[1]) + (crosses[2] + crosses[3])) / full,
        ]
        kept = jnp.zeros(held.shape, F32)
        for number, column in enumerate(numbers):
            kept = jnp.where(lane == number, column, kept)
        held[...] = kept
        summed[...] = jnp.zeros_like(summed)

    mean, scale, sum_grad, sum_cross = (held[:, i : i + 1] for i in range(4))
    gains = gain_four[...]
    hat = (activated[...] - mean) * scale
    fourth_input[...] = (hat * gains).astype(BF)
    grads = grad_fourth[...]
    grad_gain[...] = jnp.sum(grads * hat, axis=0, keepdims=True)
    low = (scale * (grads * gains - sum_grad - hat * sum_cross) * slope[...]).astype(BF)
    grad_up[...] = low
    summed[...] += dot(low, up_weight[...], 1, 1)

    @pl.when(step == pl.num_programs(0) - 1)
    def _():
        parts[...] = summed[...].astype(BF).reshape(parts.shape)


def down_kernel(fourth_input, down_t, parts, summed):
    step = pl.program_id(0)

    @pl.when(step == 0)
    def _():
        summed[...] = jnp.zeros_like(summed)

    summed[...] += dot(fourth_input[...], down_t[...], 1, 1)

    @pl.when(step == pl.num_programs(0) - 1)
    def _():
        parts[...] = summed[...].astype(BF).reshape(parts.shape)


def output_kernel(parts, middle, grad_rows, rows, spread):
    total_rows = (parts[0].astype(F32) + parts[1].astype(F32)) + (parts[2].astype(F32) + parts[3].astype(F32))
    total_rows = middle[...] + total_rows
    for device in range(GRP):
        rows[device] = total_rows
        spread[device] = grad_rows[...]


def text_kernel(place, rows, text):
    text[...] = rows[...].reshape(text.shape)


def third_back_kernel(
    place, parts, middle, branch, cotangent, gain_three, gain_out, numbers, grad_middle, low, gain_grad
):
    width = middle.shape[1]
    grads = (parts[0].astype(F32) + parts[1].astype(F32)) + (parts[2].astype(F32) + parts[3].astype(F32))
    hat, scale = row_norm(middle[...])
    total_rows = cotangent[...].astype(F32) + row_norm_back(grads, hat, scale, gain_three[...])
    grad_middle[...] = total_rows
    rounded = total_rows.astype(BF)
    wide = rounded.astype(F32)
    sum_grad = jnp.sum(wide * gain_out[...], axis=-1, keepdims=True) / width
    sum_cross = jnp.sum(wide * branch[...], axis=-1, keepdims=True) / width
    lanes = lanes_of(in_pairs([numbers[:, 0:1], numbers[:, 1:2], sum_grad, sum_cross]), BF)
    gain_grad[...] = jnp.sum(grads * hat, axis=0, keepdims=True)
    for device in range(GRP):
        low[device, :, :width] = rounded
        low[device, :, width:] = lanes


def attention_back_kernel(
    grad_rows, attended, projected, prob, gain_two, out_t, in_weight,
    grad_branch, second_input, grad_projected, grad_gain_two, parts,
):
    tokens, local = attended.shape
    width = grad_branch.shape[1]
    grad_branch[...] = grad_rows[:, :, :width].reshape(tokens, width)
    lanes = grad_rows[:, :, width:].reshape(tokens, LANES)
    mean, scale, sum_grad, sum_cross = (from_pairs(lanes, i) for i in range(4))
    hat = (attended[...] - mean) * scale
    gains = gain_two[...]
    second_input[...] = (hat * gains).astype(BF)
    grad_second = dot(grad_branch[...], out_t[...], 1, 0)
    grad_gain_two[...] = jnp.sum(grad_second * hat, axis=0, keepdims=True)
    grad_attended = (scale * (grad_second * gains - sum_grad - hat * sum_cross)).astype(BF)
    for head in range(local // HD):
        columns = [slice(i * local + head * HD, i * local + (head + 1) * HD) for i in range(3)]
        query_head, key_head, value_head = (projected[:, column] for column in columns)
        grad_head = grad_attended[:, head * HD : (head + 1) * HD]
        weights = prob[head]
        grad_weights = dot(grad_head, value_head, 1, 1)
        grad_scores = weights * (
            grad_weights - jnp.sum(weights * grad_weights, axis=-1, keepdims=True)
        )
        grad_scores = grad_scores.astype(BF)
        factor = HD ** (-0.5)
        grad_projected[:, columns[0]] = (dot(grad_scores, key_head, 1, 0) * factor).astype(BF)
        grad_projected[:, columns[1]] = (dot(grad_scores, query_head, 0, 0) * factor).astype(BF)
        grad_projected[:, columns[2]] = dot(weights.astype(BF), grad_head, 0, 0).astype(BF)
    parts[...] = dot(grad_projected[...], in_weight[...], 1, 1).astype(BF).reshape(parts.shape)


def first_back_kernel(
    place, parts, inputs, gain_one, grad_middle, gain_three_grad, grad_inputs, low, gain_grads
):
    grads = (parts[0].astype(F32) + parts[1].astype(F32)) + (parts[2].astype(F32) + parts[3].astype(F32))
    hat, scale = row_norm(inputs[...].astype(F32))
    rows = grad_middle[...] + row_norm_back(grads, hat, scale, gain_one[...])
    rounded = rows.astype(BF)
    gain_grad = jnp.sum(grads * hat, axis=0, keepdims=True)
    width = gain_grad.shape[1]
    grad_inputs[...] = rows
    put_vector(gain_grads, 0, gain_grad)
    put_vector(gain_grads, width // LANES, gain_three_grad[...])
    for device in range(GRP):
        low[device, :, :width] = rounded
        low[device, :, width:] = gain_grads[...].astype(BF)


def sampler_back_kernel(
    grad_rows, mixer, query_rows, sources, prob, query_weight, gain_four_grad, gain_two_grad,
    grad_image, grad_sources, grad_query, extra, across,
):
    width = query_rows.shape[1]
    full = grad_image.shape[1]
    query = query_rows[:NL, :].astype(BF)
    grad_image[...] = grad_rows[:2, :, :full].reshape(grad_image.shape)
    grad_sampled = dot(grad_image[...], mixer[...], 1, 0).astype(BF)
    for head in range(width // RHD):
        columns = slice(head * RHD, (head + 1) * RHD)
        value_columns = slice(width + head * RHD, width + (head + 1) * RHD)
        keys, values = sources[:, columns], sources[:, value_columns]
        grad_head = grad_sampled[:, columns]
        weights = prob[head]
        grad_weights = dot(grad_head, values, 1, 1)
        grad_scores = weights * (
            grad_weights - jnp.sum(weights * grad_weights, axis=-1, keepdims=True)
        )
        grad_scores = grad_scores.astype(BF)
        factor = RHD ** (-0.5)
        grad_query[:, columns] = (dot(grad_scores, keys, 1, 0) * factor).astype(BF)
        grad_sources[:, columns] = (dot(grad_scores, query[:, columns], 0, 0) * factor).astype(BF)
        grad_sources[:, value_columns] = dot(weights.astype(BF), grad_head, 0, 0).astype(BF)
    low = grad_query[...]
    wide = low.astype(F32)
    sums = [
        jnp.sum(wide * query_rows[NL : NL + 1, :], axis=-1, keepdims=True),
        jnp.sum(wide * query_rows[:NL, :], axis=-1, keepdims=True),
    ]
    across[...] = jnp.zeros_like(across)
    across[:NL, :] = grad_image[...].astype(F32)
    across[NL : 2 * NL, :] = dot(low, query_weight[...], 1, 1)
    lanes = [grad_rows[i, :, full:].astype(F32) for i in range(GRP)]
    lanes = (lanes[0] + lanes[1]) + (lanes[2] + lanes[3])
    count = full // LANES
    for number in range(2):
        vector = [lanes[number * count + i : number * count + i + 1, :] for i in range(count)]
        across[LANES + number : LANES + number + 1, :] = jnp.concatenate(vector, axis=1)
    across[LANES + 2 : LANES + 3, :] = gain_four_grad[...]
    across[LANES + 3 : LANES + 4, :] = gain_two_grad[...]
    held = jnp.transpose(across[...])
    lane = lax.broadcasted_iota(jnp.int32, held.shape, 1)
    for number, column in enumerate(sums):
        held = jnp.where(lane == LANES + 4 + number, jnp.concatenate([column] * DP, axis=0), held)
    extra[...] = held


def turn(left, turned):
    tokens, columns = left.shape
    for at in range(0, columns, LANES):
        block = left[:, at : at + LANES].astype(F32)
        turned[at : at + LANES, :tokens] = jnp.transpose(block).astype(BF)


def wide_outer_kernel(halves, left, right, other_left, other_right, out, turned):
    step = pl.program_id(0)
    for first, second, start in ((left, right, 0), (other_left, other_right, halves)):

        @pl.when(step == start)
        def _():
            turn(first, turned)

        @pl.when((step >= start) & (step < start + halves))
        def _():
            out[...] = jnp.dot(turned[...], second[...], preferred_element_type=F32).astype(BF)


def outer_kernel(order, keep, kinds, places, *refs):
    step = pl.program_id(0)
    core, x, y = places[0], places[1], places[2]
    turned, chosen = refs[-2:]
    refs = list(refs[:-2])
    outs = [refs.pop() for _ in range(len(KEPT) if keep else 1)][::-1]
    arrived = refs.pop() if keep else None
    side = core if keep else 1 - core

    def row_of(spot, rows):
        first, second = spot // 4, spot % 4
        off_x, off_y = (first, second) if order == 0 else (second, first)
        chip = (x + off_x) % XS * YS + (y + off_y) % YS
        return pl.multiple_of((2 * chip + side) * rows, rows)

    def put(first, rows, blocks):
        if keep:
            blocks = blocks + arrived[:, first : first + rows].astype(F32)
            at = 0
            for out in outs:
                count = out.shape[0]
                out[:, first : first + rows] = blocks[at : at + count].astype(BF)
                at += count
        else:
            outs[0][:, first : first + rows] = blocks.astype(BF)

    for start, count, kind in kinds:
        used = [refs.pop(0) for _ in range({"plain": 1, "product": 2, "stacked": 3}[kind])]
        if kind == "plain":

            @pl.when((step >= start) & (step < start + count))
            def _():
                rows = used[0].shape[0] // DP
                put(0, rows, jnp.stack([used[0][pl.ds(row_of(i, rows), rows), :] for i in range(XS * YS)]))

            continue
        tokens, rows = used[0].shape[0], used[0].shape[1] // DP
        half = XS * YS * rows

        @pl.when(step == start)
        def _():
            turn(used[0], turned)
            for spot in range(XS * YS):
                chosen[spot * rows : (spot + 1) * rows, :tokens] = turned[
                    pl.ds(row_of(spot, rows), rows), :tokens
                ]

        @pl.when((step >= start) & (step < start + count))
        def _():
            for number, right in enumerate(used[1:]):
                product = jnp.dot(chosen[:half, :tokens], right[...], preferred_element_type=F32)
                put(number * rows, rows, product.reshape(XS * YS, rows, product.shape[1]))


def outer_blocks(order, pieces, block, arrived=None, after=()):
    x, y, core = coordinates()
    places = jnp.stack([core, x, y]).astype(jnp.int32)
    kinds, operands, specs, at = [], [], {}, 0
    for piece in pieces:
        kind = ("plain", "product", "stacked")[len(piece) - 1]
        count = piece[-1].shape[1] // block
        kinds.append((at, count, kind))
        for number, operand in enumerate(piece):
            if kind == "plain" or number > 0:
                specs[len(operands)] = pl.BlockSpec(
                    (operand.shape[0], block), lambda i, s, at=at, n=count: (0, jnp.clip(i - at, 0, n - 1))
                )
            operands.append(operand)
        at += count
    width = pieces[0][0].shape[1]
    rows = width // DP
    keep = arrived is not None
    if keep:
        specs[len(operands)] = pl.BlockSpec((XS * YS, rows, block), lambda i, s: (0, 0, i))
        operands.append(arrived)
    counts = KEPT if keep else (XS * YS,)
    outs = call(
        partial(outer_kernel, order, keep, kinds),
        [((count, rows, at * block), BF) for count in counts],
        operands,
        specs=specs,
        out_specs={
            i: pl.BlockSpec((count, rows, block), lambda i, s: (0, 0, i)) for i, count in enumerate(counts)
        },
        grid=(at,),
        scalars=(places,),
        scratch=[pltpu.VMEM((width, 2 * LANES), BF), pltpu.VMEM((width // 2, 2 * LANES), BF)],
        after=after,
    )
    return outs if keep else outs[0]


def step_along(values, along_x, step):
    return fetch(values, step if along_x else 0, 0 if along_x else step, 0)


def half_kernel(right_half, left_half, right, left, right_out, left_out):
    right_out[...] = (right[...].astype(F32) + right_half[...].astype(F32)).astype(BF)
    left_out[...] = (left[...].astype(F32) + left_half[...].astype(F32)).astype(BF)


def both_ways(held, along_x, after=()):
    own, right, far_right, far_left, left = held
    from_left = step_along(far_right, along_x, -1)
    from_right = step_along(far_left, along_x, 1)
    half = pl.BlockSpec((2,) + right.shape[1:], lambda *_: (0, 0, 0))
    other = pl.BlockSpec((2,) + right.shape[1:], lambda *_: (1, 0, 0))
    right, left = call(
        half_kernel,
        [(right.shape, BF), (left.shape, BF)],
        [from_left, from_right, right, left],
        specs={2: half, 3: other},
        out_specs={0: half, 1: other},
        after=after,
        aliases={2: 0, 3: 1},
    )
    return [own, step_along(right, along_x, -1), step_along(left, along_x, 1)]


def ring_moves(held, along_x):
    return [held[0]] + [step_along(held[step], along_x, -step) for step in range(1, 4)]


def sum_kernel(*refs):
    for parts, outs in ((refs[:3], refs[6:10]), (refs[3:6], refs[10:])):
        for number in range(4):
            first, second, third = (part[number].astype(F32) for part in parts)
            outs[number][...] = (first + (second + third)).astype(BF)


def last_sum_kernel(*refs):
    for parts, out in ((refs[:4], refs[8]), (refs[4:8], refs[9])):
        first, second, third, fourth = (part[...].astype(F32) for part in parts)
        out[...] = (first + second) + (third + fourth)


def sum_over_rings(first_held, last_held, after):
    moved = both_ways(first_held, True, after) + both_ways(last_held, False)
    shapes = [held[0].shape[1:] for held in (first_held, last_held)]
    blocks = call(sum_kernel, [(shape, BF) for shape in shapes for _ in range(4)], moved)
    moved = ring_moves(blocks[:4], False) + ring_moves(blocks[4:], True)
    return call(last_sum_kernel, [(shape, F32) for shape in shapes], moved)


def grp_gather(values):
    spread = jnp.broadcast_to(values[None], (GRP,) + values.shape)
    return lax.all_to_all(spread, "grp", 0, 0)


def swap(blocks):
    return lax.all_to_all(blocks, "grp", 0, 0)


def total(parts):
    return (parts[0] + parts[1]) + (parts[2] + parts[3])


def row_norm(values):
    center = values - jnp.mean(values, axis=-1, keepdims=True)
    spread = jnp.mean(center * center, axis=-1, keepdims=True)
    scale_rows = lax.rsqrt(spread + EPSILON)
    return center * scale_rows, scale_rows


def row_norm_back(grad_normed, normed, scale_rows, scale_gain):
    grad_hat = grad_normed * scale_gain
    return scale_rows * (
        grad_hat
        - jnp.mean(grad_hat, axis=-1, keepdims=True)
        - normed * jnp.mean(grad_hat * normed, axis=-1, keepdims=True)
    )


def shards(
    caption_token_index,
    lengths,
    slot_image_pair,
    features,
    text_table,
    latents,
    sampler_gain,
    sampler_query,
    sampler_source,
    sampler_mixer,
    norm_gain_one,
    attention_in,
    norm_gain_two,
    attention_out,
    norm_gain_three,
    feed_up,
    norm_gain_four,
    feed_down,
    cotangent,
):
    group = lax.axis_index("grp")
    place = lax.axis_index(DP_AXES)
    width = feed_down.shape[1] * DP
    hidden = feed_down.shape[0] * GRP
    own = width // DP
    local = attention_out.shape[0]
    local_ff = feed_up.shape[1]
    patches, feature_width = features.shape[1:]
    tokens = cotangent.shape[1]
    spans = caption_token_index.shape[1]
    own_rows = tokens // GRP

    quarter = patches // GRP
    source_part = jnp.concatenate([sampler_source[:, 0], sampler_source[:, 1]], axis=0)
    small_part = jnp.pad(latents.T, ((0, 0), (0, LANES - NL)))
    first_part = jnp.concatenate(
        [
            attention_in.reshape(own, 3 * local),
            attention_out.T,
            sampler_mixer.T,
            source_part,
            lax.dynamic_slice_in_dim(features[0], group * quarter, quarter, 0),
            sampler_query,
            small_part,
        ],
        axis=1,
    )
    second_part = jnp.concatenate([feed_up, feed_down.T], axis=1)
    first_all = lax.all_gather(first_part, DP_AXES, axis=0, tiled=True)
    second_all = lax.all_gather(second_part, DP_AXES, axis=0, tiled=True)

    def first_spec(number, columns):
        return pl.BlockSpec((width, columns), lambda *_: (0, number))

    table_rows = text_table.shape[0]
    table_block = lax.all_to_all(text_table, "grp", 1, 0, tiled=True)
    x, y, core = coordinates()
    flat_ids = caption_token_index[0]
    numbers = jnp.stack(
        [
            (flat_ids // 256).astype(BF),
            (flat_ids % 256).astype(BF),
            sampler_gain,
            norm_gain_one,
            norm_gain_three,
            norm_gain_four,
            jnp.pad(norm_gain_two, (0, own - norm_gain_two.shape[0])),
        ]
    )
    numbers = gather_offsets(jnp.pad(numbers, ((0, 16 - numbers.shape[0]), (0, 0))))
    wide_numbers = numbers.astype(F32)
    by_offset = (wide_numbers[:, :, :, 0] * 256 + wide_numbers[:, :, :, 1]).astype(jnp.int32)
    placed = jnp.moveaxis(jnp.roll(wide_numbers[:, :, :, :7], (core, x, y), axis=(0, 1, 2)), 0, 2)
    all_ids = (placed[:, :, :, 0] * 256 + placed[:, :, :, 1]).astype(jnp.int32).reshape(-1)
    gains = placed[:, :, :, 2:]
    query_gain, gain_one, gain_three, gain_four, gain_two = (
        gains[:, :, :, i].reshape(1, width) for i in range(5)
    )
    gain_two = gain_two.reshape(DP, own)[:, : norm_gain_two.shape[0]].reshape(1, local)

    def block_rows(ids):
        span = table_rows * DP
        held = ids % span // table_rows == place
        return jnp.where(held, ids // span * table_rows + ids % table_rows, -1)

    def one_hot(ids):
        return (block_rows(ids)[:, None] == jnp.arange(GRP * table_rows, dtype=jnp.int32)[None]).astype(BF)

    picked = dot(one_hot(by_offset.reshape(-1)), table_block, 1, 0).astype(BF)
    text_cols = scatter_offsets(picked.reshape(CS, XS, YS, spans, local))
    text_parts = grp_gather(text_cols)

    split_first = first_all.reshape(DP, own, first_all.shape[1])
    (pair_parts,) = call(
        pair_kernel,
        [((GRP, quarter, feature_width), BF)],
        [split_first],
        specs={0: pl.BlockSpec((1, quarter, feature_width), lambda i, s: (s[0], 0, 3))},
        scalars=(slot_image_pair,),
        after=(text_parts,),
    )
    pair_rows = swap(pair_parts).reshape(patches, feature_width)
    small_spec = first_spec(36, LANES)
    mixer_spec = first_spec(4, local)
    vector_rows = width // LANES
    (
        mixed, latent_values, latent_hat, latent_scale, query_input, query_rows, sampled, sources, sampler_prob,
    ) = call(
        sampler_kernel,
        [
            ((GRP, NL // GRP, width), F32),
            ((NL, width), F32),
            ((NL, width), F32),
            ((NL, LANES), F32),
            ((NL, width), BF),
            ((NL + 16, local), F32),
            ((NL, local), BF),
            ((patches, 2 * local), BF),
            ((local // RHD, NL, patches), F32),
        ],
        [pair_rows, first_all, first_all, split_first, split_first, first_all, query_gain],
        specs={
            1: small_spec,
            2: first_spec(8, local),
            3: pl.BlockSpec((DP, own // 2, local), lambda *_: (0, 0, 5)),
            4: pl.BlockSpec((DP, own // 2, local), lambda *_: (0, 1, 5)),
            5: mixer_spec,
        },
    )
    place_row = jnp.reshape(group, (1,)).astype(jnp.int32)
    latent_spec = pl.BlockSpec((NL // GRP, width), lambda i, s: (s[0], 0))
    (images,) = call(
        image_kernel,
        [((GRP, NL // GRP, width), BF)],
        [swap(mixed), latent_values],
        specs={1: latent_spec},
        scalars=(place_row,),
    )
    image_parts = swap(images)

    out_spec = first_spec(3, local)
    in_spec = first_spec(0, 3 * local)
    own_spec = pl.BlockSpec((own_rows, width), lambda i, s: (s[0], 0))
    blocks = ((GRP, own_rows, width), BF)
    wide_blocks = ((GRP, own_rows, width + LANES), BF)
    inputs, first_input, projected, prob, attended, branch_parts = call(
        attention_kernel,
        [
            ((tokens, width), BF),
            ((tokens, width), BF),
            ((tokens, 3 * local), BF),
            ((local // HD, tokens, tokens), F32),
            ((tokens, local), F32),
            ((GRP, own_rows, width + 2 * LANES), BF),
        ],
        [image_parts, text_parts, gain_one, first_all, gain_two, first_all],
        specs={3: in_spec, 5: out_spec},
        scalars=(lengths,),
        scratch=[pltpu.VMEM((2 * vector_rows, LANES), F32)],
    )
    middle, branch, third_input, second_numbers, gain_out = call(
        middle_kernel,
        [
            ((own_rows, width), F32),
            ((own_rows, width), F32),
            blocks,
            ((own_rows, LANES), F32),
            ((1, width), F32),
        ],
        [swap(branch_parts), inputs, gain_three],
        specs={1: own_spec},
        scalars=(place_row,),
    )

    grad_output = cotangent[0]
    hidden_block = 512
    steps = local_ff // hidden_block
    up_spec = pl.BlockSpec((width, hidden_block), lambda i: (0, i))
    down_spec = pl.BlockSpec((width, hidden_block), lambda i: (0, steps + i))
    columns_spec = pl.BlockSpec((tokens, hidden_block), lambda i: (0, i))
    row_spec = pl.BlockSpec((1, hidden_block), lambda i: (0, i))
    wide = ((tokens, local_ff), F32)
    activated, slope, grad_fourth, fourth_stats, third_rows = call(
        hidden_kernel,
        [wide, wide, wide, ((GRP, STATS, tokens), F32), ((tokens, width), BF)],
        [swap(third_input), grad_output, gain_four, second_all, second_all],
        specs={3: up_spec, 4: down_spec},
        grid=(steps,),
    )
    fourth_input, grad_up_rows, grad_gain_four, third_parts = call(
        hidden_back_kernel,
        [((tokens, local_ff), BF), ((tokens, local_ff), BF), ((1, local_ff), F32), blocks],
        [swap(fourth_stats), activated, slope, grad_fourth, gain_four, second_all],
        specs={1: columns_spec, 2: columns_spec, 3: columns_spec, 4: row_spec, 5: up_spec},
        out_specs={0: columns_spec, 1: columns_spec, 2: row_spec},
        grid=(steps,),
        scratch=[pltpu.VMEM((tokens, LANES), F32), pltpu.VMEM((tokens, width), F32)],
    )
    third_parts = swap(third_parts)
    outer_block = 512
    outer_steps = local_ff // outer_block
    (ff_grads,) = call(
        partial(wide_outer_kernel, outer_steps),
        [((width, 2 * local_ff), BF)],
        [third_rows, grad_up_rows, grad_output, fourth_input],
        specs={
            1: pl.BlockSpec((tokens, outer_block), lambda i: (0, jnp.minimum(i, outer_steps - 1))),
            3: pl.BlockSpec((tokens, outer_block), lambda i: (0, jnp.maximum(i - outer_steps, 0))),
        },
        out_specs={0: pl.BlockSpec((width, outer_block), lambda i: (0, i))},
        grid=(2 * outer_steps,),
        scratch=[pltpu.VMEM((width, tokens), BF)],
    )
    ff_low = lax.psum_scatter(ff_grads, DP_AXES, scatter_dimension=0, tiled=True)
    ff_sums = ff_low.astype(F32)
    grad_middle, branch_low, gain_three_grad = call(
        third_back_kernel,
        [((own_rows, width), F32), wide_blocks, ((1, width), F32)],
        [third_parts, middle, branch, grad_output, gain_three, gain_out, second_numbers],
        specs={3: own_spec},
        scalars=(place_row,),
    )

    grad_branch, second_input, grad_projected, grad_gain_two, first_parts = call(
        attention_back_kernel,
        [
            ((tokens, width), BF),
            ((tokens, local), BF),
            ((tokens, 3 * local), BF),
            ((1, local), F32),
            blocks,
        ],
        [swap(branch_low), attended, projected, prob, gain_two, first_all, first_all],
        specs={5: out_spec, 6: in_spec},
        after=(ff_grads,),
    )
    first_pieces = [(first_input, grad_projected), (grad_branch, second_input)]
    first_arrived = fetch(outer_blocks(0, first_pieces, 512), 0, 0, 1)
    input_own, input_low = call(
        first_back_kernel,
        [((own_rows, width), F32), wide_blocks],
        [swap(first_parts), inputs, gain_one, grad_middle, gain_three_grad],
        specs={1: own_spec},
        scalars=(place_row,),
        scratch=[pltpu.VMEM((2 * vector_rows, LANES), F32)],
    )
    input_low = swap(input_low)
    first_held = outer_blocks(0, first_pieces, 512, first_arrived)

    per_own = norm_gain_two.shape[0]
    gain_two_row = jnp.pad(grad_gain_two.reshape(DP, per_own), ((0, 0), (0, own - per_own))).reshape(1, width)
    image_low, grad_sources, grad_query, extra = call(
        sampler_back_kernel,
        [((NL, width), BF), ((patches, 2 * local), BF), ((NL, local), BF), ((width, 2 * LANES), F32)],
        [input_low, first_all, query_rows, sources, sampler_prob, first_all, grad_gain_four, gain_two_row],
        specs={1: mixer_spec, 5: first_spec(8, local)},
        scratch=[pltpu.VMEM((2 * LANES, width), F32)],
        after=first_held[:1],
    )

    last_pieces = [
        (image_low, sampled),
        (query_input, grad_query),
        (pair_rows, grad_sources[:, :local], grad_sources[:, local:]),
        (extra,),
    ]
    last_sent = outer_blocks(1, last_pieces, 256)
    last_held = outer_blocks(1, last_pieces, 256, fetch(last_sent, 0, 0, 1))

    (text_low,) = call(
        text_kernel,
        [((spans, local), BF)],
        [input_low],
        specs={0: pl.BlockSpec((2, own_rows, local), lambda i, s: (1, 0, s[0]))},
        scalars=(place_row,),
        after=(ff_low, last_held[0]),
    )
    text_all = lax.all_gather(text_low, DP_AXES, axis=0, tiled=True)
    table_sums = dot(one_hot(all_ids), text_all, 0, 0).astype(BF)
    table_sums = lax.all_to_all(table_sums, "grp", 0, 1, tiled=True)
    table_grad = table_sums.astype(F32)

    (down_parts,) = call(
        down_kernel,
        [blocks],
        [fourth_input, second_all],
        specs={0: columns_spec, 1: down_spec},
        grid=(steps,),
        scratch=[pltpu.VMEM((tokens, width), F32)],
        after=last_held[:1],
    )

    output_rows, input_rows = call(
        output_kernel,
        [((GRP, own_rows, width), F32)] * 2,
        [swap(down_parts), middle, input_own],
    )
    layer_output = swap(output_rows).reshape(1, tokens, width)
    input_grad = swap(input_rows).reshape(1, tokens, width)
    first_sums, last_sums = sum_over_rings(first_held, last_held, (last_sent,))
    cut = 3 * local
    numbers = last_sums[:, 3 * local :]
    source_sums = last_sums[:, 2 * local : 3 * local]

    latent_hat_own = lax.dynamic_slice_in_dim(latent_hat, place * own, own, 1)
    sampler_back = total(grp_gather(jnp.concatenate([numbers[:, NL:LANES].T, numbers[:, LANES + 4 : LANES + 6]], axis=1)))
    grad_query_norm = sampler_back[:, :own]
    sampler_means = sampler_back[:, own:] / width
    grad_latent_norm = latent_scale[:, :1] * (
        grad_query_norm * sampler_gain.astype(F32)
        - sampler_means[:, :1]
        - latent_hat_own * sampler_means[:, 1:]
    )
    sampler_gain_grad = jnp.sum(grad_query_norm * latent_hat_own, axis=0)
    latents_grad = numbers[:, :NL].T + grad_latent_norm
    return (
        layer_output,
        input_grad,
        table_grad,
        latents_grad,
        sampler_gain_grad,
        last_sums[:, local : 2 * local],
        jnp.stack([source_sums[: own // 2], source_sums[own // 2 :]], axis=1),
        last_sums[:, :local].T,
        numbers[:, LANES],
        first_sums[:, :cut].reshape(own, 3, local),
        numbers[:per_own, LANES + 3],
        first_sums[:, cut:].T,
        numbers[:, LANES + 1],
        ff_sums[:, :local_ff],
        numbers[:, LANES + 2],
        ff_sums[:, local_ff:].T,
    )


def solution(mesh):
    mesh = Mesh(mesh.devices.reshape(GRP, XS, YS, CS), ("grp",) + DP_AXES)
    return jax.shard_map(
        shards,
        mesh=mesh,
        in_specs=(
            P(DP_AXES, None),
            P(DP_AXES),
            P(DP_AXES),
            P(DP_AXES, None, None),
            P(("grp",) + DP_AXES, None),
            P(None, DP_AXES),
            P(DP_AXES),
            P(DP_AXES, "grp"),
            P(DP_AXES, None, "grp"),
            P("grp", DP_AXES),
            P(DP_AXES),
            P(DP_AXES, None, "grp"),
            P(("grp",) + DP_AXES),
            P("grp", DP_AXES),
            P(DP_AXES),
            P(DP_AXES, "grp"),
            P(("grp",) + DP_AXES),
            P("grp", DP_AXES),
            P(DP_AXES, None, None),
        ),
        out_specs=(
            P(DP_AXES, None, None),
            P(DP_AXES, None, None),
            P(("grp",) + DP_AXES, None),
            P(None, DP_AXES),
            P(DP_AXES),
            P(DP_AXES, "grp"),
            P(DP_AXES, None, "grp"),
            P("grp", DP_AXES),
            P(DP_AXES),
            P(DP_AXES, None, "grp"),
            P(("grp",) + DP_AXES),
            P("grp", DP_AXES),
            P(DP_AXES),
            P(DP_AXES, "grp"),
            P(("grp",) + DP_AXES),
            P("grp", DP_AXES),
        ),
        check_vma=False,
    )
```

```python
from functools import partial

import jax
import jax.numpy as jnp
from jax import lax
from jax.experimental import pallas as pl
from jax.experimental.pallas import tpu as pltpu
from jax.sharding import Mesh, PartitionSpec as P

HD = 64
RHD = 128
NL = 64
EPSILON = 1e-05
NEG_FILL = -1e30
GRP = 4
XS = 4
YS = 4
CS = 2
DP = XS * YS * CS
DP_AXES = ("x", "y", "core")
LANES = 128
STATS = 8
KEPT = (4, 4, 2, 2, 4)
VMEM_LIMIT = 56 * 1024 * 1024
BF = jnp.bfloat16
F32 = jnp.float32


def dot(left, right, left_dims, right_dims):
    return lax.dot_general(
        left, right, (((left_dims,), (right_dims,)), ((), ())), preferred_element_type=F32
    )


def fetch(values, step_x, step_y, step_core):
    pairs = []
    for x in range(XS):
        for y in range(YS):
            for core in range(CS):
                source = (((x + step_x) % XS) * YS + (y + step_y) % YS) * CS + (core ^ step_core)
                pairs.append((source, (x * YS + y) * CS + core))
    return lax.ppermute(values, DP_AXES, pairs)


def coordinates():
    place = lax.axis_index(DP_AXES)
    return place // (YS * CS), place // CS % YS, place % CS


def ring(values, axis):
    steps = [(step, 0) if axis == 0 else (0, step) for step in range(4)]
    return [values] + [fetch(values, *step, 0) for step in steps[1:]]


def gather_offsets(values):
    over_y = jnp.stack(ring(values, 1))
    over_x = jnp.stack(ring(over_y, 0))
    return jnp.stack([over_x, fetch(over_x, 0, 0, 1)])


def dp_total(values):
    values = values + fetch(values, 0, 0, 1)
    for axis in (0, 1):
        parts = ring(values, axis)
        values = (parts[0] + parts[2]) + (parts[1] + parts[3])
    return values


def scatter_offsets(values):
    values = values[0] + fetch(values[1], 0, 0, 1)
    values = values[0] + sum(fetch(values[step], -step, 0, 0) for step in range(1, XS))
    return values[0] + sum(fetch(values[step], 0, -step, 0) for step in range(1, YS))


def call(
    body, outs, operands, specs=None, out_specs=None, grid=(1,), scalars=(), scratch=(), after=(), aliases=None
):
    specs = dict(specs or {})
    out_specs = dict(out_specs or {})

    def whole(shape):
        return pl.BlockSpec(shape, lambda *_: (0,) * len(shape))

    def wrapped(*refs):
        held = len(scalars) + len(operands)
        body(*refs[:held], *refs[held + len(after) :])

    in_specs = [specs.get(i, whole(operand.shape)) for i, operand in enumerate(operands)]
    in_specs += [pl.BlockSpec(memory_space=pl.ANY)] * len(after)
    return pl.pallas_call(
        wrapped,
        grid_spec=pltpu.PrefetchScalarGridSpec(
            num_scalar_prefetch=len(scalars),
            grid=grid,
            in_specs=in_specs,
            out_specs=[out_specs.get(i, whole(shape)) for i, (shape, _) in enumerate(outs)],
            scratch_shapes=list(scratch),
        ),
        out_shape=[jax.ShapeDtypeStruct(shape, dtype) for shape, dtype in outs],
        input_output_aliases={len(scalars) + i: out for i, out in (aliases or {}).items()},
        compiler_params=pltpu.CompilerParams(vmem_limit_bytes=VMEM_LIMIT),
    )(*scalars, *operands, *after)


def pair_kernel(pair, features, spread):
    for device in range(GRP):
        spread[device] = features[0]


def sampler_kernel(
    pair, small, query_weight, key_weight, value_weight, mixer, query_gain,
    mixed, latents, latent_hat, latent_scale, query_input, query_rows, sampled, sources, prob,
):
    width = query_weight.shape[1]
    across = jnp.transpose(small[...].astype(F32))
    values = across[:NL]
    latents[...] = values
    hat, scale = row_norm(values)
    latent_hat[...] = hat
    latent_scale[...] = jnp.broadcast_to(scale, latent_scale.shape)
    gain = query_gain[...]
    normed = (hat * gain).astype(BF)
    query_input[...] = normed
    query_rows[:NL, :] = jnp.dot(normed, query_weight[...], preferred_element_type=F32)
    query_rows[NL:, :] = jnp.dot(
        jnp.broadcast_to(gain, (16, gain.shape[1])).astype(BF), query_weight[...], preferred_element_type=F32
    )
    query = query_rows[:NL, :].astype(BF)
    rows = pair[...]
    keys, values = (
        jnp.dot(rows, weight[...].reshape(rows.shape[1], width), preferred_element_type=F32).astype(BF)
        for weight in (key_weight, value_weight)
    )
    sources[:, :width] = keys
    sources[:, width:] = values
    for head in range(width // RHD):
        columns = slice(head * RHD, (head + 1) * RHD)
        scores = dot(query[:, columns], keys[:, columns], 1, 1) * RHD ** (-0.5)
        exponent = jnp.exp(scores - jnp.max(scores, axis=-1, keepdims=True))
        weights = exponent / jnp.sum(exponent, axis=-1, keepdims=True)
        prob[head] = weights
        sampled[:, columns] = jnp.dot(
            weights.astype(BF), values[:, columns], preferred_element_type=F32
        ).astype(BF)
    mixed[...] = dot(sampled[...], mixer[...], 1, 1).reshape(mixed.shape)


def image_kernel(place, parts, latents, images):
    mixed = (parts[0] + parts[1]) + (parts[2] + parts[3])
    rows = (latents[...] + mixed).astype(BF)
    for device in range(GRP):
        images[device] = rows


def lanes_of(numbers, dtype):
    rows = numbers[0].shape[0]
    lane = lax.broadcasted_iota(jnp.int32, (rows, LANES), 1)
    held = jnp.zeros((rows, LANES), F32)
    for number, column in enumerate(numbers):
        held = jnp.where(lane == number, column, held)
    return held.astype(dtype)


def in_pairs(numbers):
    pairs = []
    for number in numbers:
        high = number.astype(BF).astype(F32)
        pairs += [high, number - high]
    return pairs


def from_pairs(lanes, number):
    wide = lanes.astype(F32)
    return wide[:, 2 * number : 2 * number + 1] + wide[:, 2 * number + 1 : 2 * number + 2]


def put_rows(columns):
    tokens = columns[0].shape[0]
    lane = lax.broadcasted_iota(jnp.int32, (tokens, tokens), 1)
    held = jnp.zeros((tokens, tokens), F32)
    for number, column in enumerate(columns):
        held = jnp.where(lane == number, column, held)
    return jnp.transpose(held)[:STATS]


def take_columns(stats):
    return jnp.transpose(stats[:, :STATS, :].reshape(GRP * STATS, stats.shape[2]))


def put_vector(small, first, vector):
    for i in range(vector.shape[1] // LANES):
        small[first + i : first + i + 1, :] = vector[:, i * LANES : (i + 1) * LANES]


def attention_kernel(
    length, image, text, gain_one, in_weight, gain_two, out_t,
    inputs, first_input, projected, prob, attended, parts, vectors,
):
    images = NL
    inputs[:images, :] = image[...].reshape(images, inputs.shape[1])
    local = gain_two.shape[1]
    for device in range(GRP):
        inputs[images:, device * local : (device + 1) * local] = text[device]
    hat, _ = row_norm(inputs[...].astype(F32))
    first_input[...] = (hat * gain_one[...]).astype(BF)
    projected[...] = dot(first_input[...], in_weight[...], 1, 0).astype(BF)
    tokens = inputs.shape[0]
    query = lax.broadcasted_iota(jnp.int32, (tokens, tokens), 0)
    key = lax.broadcasted_iota(jnp.int32, (tokens, tokens), 1)
    allowed = (key <= query) & (key < NL + length[0])
    for head in range(local // HD):
        query_head, key_head, value_head = (
            projected[:, i * local + head * HD : i * local + (head + 1) * HD] for i in range(3)
        )
        scores = jnp.where(allowed, dot(query_head, key_head, 1, 1) * HD ** (-0.5), NEG_FILL)
        exponent = jnp.exp(scores - jnp.max(scores, axis=-1, keepdims=True))
        weights = exponent / jnp.sum(exponent, axis=-1, keepdims=True)
        prob[head] = weights
        attended[:, head * HD : (head + 1) * HD] = jnp.dot(
            weights.astype(BF), value_head, preferred_element_type=F32
        )
    values = attended[...]
    mean = jnp.mean(values, axis=-1, keepdims=True)
    center = values - mean
    square = jnp.sum(center * center, axis=-1, keepdims=True)
    gains = gain_two[...]
    width = inputs.shape[1]
    blocks = dot((center * gains).astype(BF), out_t[...], 1, 1).astype(BF)
    parts[:, :, :width] = blocks.reshape(GRP, tokens // GRP, width)
    numbers = lanes_of(in_pairs([mean, square]), BF)
    parts[:, :, width : width + LANES] = numbers.reshape(GRP, tokens // GRP, LANES)
    products = dot(jnp.broadcast_to(gains, (16, local)).astype(BF), out_t[...], 1, 1)[:1]
    for number, vector in enumerate(in_pairs([products])):
        put_vector(vectors, number * (width // LANES), vector)
    for device in range(GRP):
        parts[device, :, width + LANES :] = vectors[...].astype(BF)


def joined_stats(means, squares, own, full):
    mean = ((means[0] + means[1]) + (means[2] + means[3])) / GRP
    shifts = [part - mean for part in means]
    square = sum(squares[i] + own * shifts[i] * shifts[i] for i in range(GRP))
    return mean, lax.rsqrt(square / full + EPSILON), shifts


def middle_kernel(place, parts, inputs, gain_three, middle, branch, third_input, numbers, gain_out):
    own_rows, width = inputs.shape
    count = width // LANES
    lanes = [parts[i, :, width : width + LANES] for i in range(GRP)]
    mean, scale, shifts = joined_stats(
        [from_pairs(lane, 0) for lane in lanes], [from_pairs(lane, 1) for lane in lanes], width // GRP, width
    )
    vectors = []
    for device in range(GRP):
        pairs = parts[device, :, width + LANES :].astype(F32)
        rows = pairs[:count] + pairs[count:]
        vectors.append(jnp.concatenate([rows[i : i + 1] for i in range(count)], axis=1))
    gain_out[...] = (vectors[0] + vectors[1]) + (vectors[2] + vectors[3])
    gathered = sum(parts[i, :, :width].astype(F32) + shifts[i] * vectors[i] for i in range(GRP))
    added = scale * gathered
    branch[...] = added
    rows = inputs[...].astype(F32) + added
    middle[...] = rows
    numbers[...] = lanes_of([mean, scale], F32)
    hat, _ = row_norm(rows)
    low = (hat * gain_three[...]).astype(BF)
    for device in range(GRP):
        third_input[device] = low


def hidden_kernel(
    third_input, cotangent, gain_four, up_weight, down_t, activated, slope, grad_fourth, stats, third_rows
):
    step = pl.program_id(0)
    block = up_weight.shape[1]
    rows = third_input[...].reshape(cotangent.shape)
    columns = pl.ds(step * block, block)
    values = dot(rows, up_weight[...], 1, 0)
    normal = 0.5 * (1.0 + lax.erf(values * (0.5**0.5)))
    activated[:, columns] = values * normal
    slope[:, columns] = normal + values * jnp.exp(-0.5 * values * values) * 0.3989422804014327
    grad_fourth[:, columns] = dot(cotangent[...], down_t[...], 1, 0)

    @pl.when(step == pl.num_programs(0) - 1)
    def _():
        third_rows[...] = rows
        active = activated[...]
        grad_hat = grad_fourth[...] * gain_four[...]
        mean = jnp.mean(active, axis=-1, keepdims=True)
        center = active - mean
        numbers = put_rows(
            [
                mean,
                jnp.sum(center * center, axis=-1, keepdims=True),
                jnp.sum(grad_hat, axis=-1, keepdims=True),
                jnp.sum(grad_hat * center, axis=-1, keepdims=True),
            ],
        )
        for device in range(GRP):
            stats[device] = numbers


def hidden_back_kernel(
    stats, activated, slope, grad_fourth, gain_four, up_weight,
    fourth_input, grad_up, grad_gain, parts, held, summed,
):
    step = pl.program_id(0)
    block = up_weight.shape[1]
    own = block * pl.num_programs(0)
    full = own * GRP

    @pl.when(step == 0)
    def _():
        columns = take_columns(stats[...])
        means, squares = ([columns[:, STATS * i + n : STATS * i + n + 1] for i in range(GRP)] for n in (0, 1))
        mean, scale, shifts = joined_stats(means, squares, own, full)
        sums = [columns[:, STATS * i + 2 : STATS * i + 3] for i in range(GRP)]
        crosses = [columns[:, STATS * i + 3 : STATS * i + 4] + shifts[i] * sums[i] for i in range(GRP)]
        lane = lax.broadcasted_iota(jnp.int32, held.shape, 1)
        numbers = [
            mean,
            scale,
            ((sums[0] + sums[1]) + (sums[2] + sums[3])) / full,
            scale * ((crosses[0] + crosses[1]) + (crosses[2] + crosses[3])) / full,
        ]
        kept = jnp.zeros(held.shape, F32)
        for number, column in enumerate(numbers):
            kept = jnp.where(lane == number, column, kept)
        held[...] = kept
        summed[...] = jnp.zeros_like(summed)

    mean, scale, sum_grad, sum_cross = (held[:, i : i + 1] for i in range(4))
    gains = gain_four[...]
    hat = (activated[...] - mean) * scale
    fourth_input[...] = (hat * gains).astype(BF)
    grads = grad_fourth[...]
    grad_gain[...] = jnp.sum(grads * hat, axis=0, keepdims=True)
    low = (scale * (grads * gains - sum_grad - hat * sum_cross) * slope[...]).astype(BF)
    grad_up[...] = low
    summed[...] += dot(low, up_weight[...], 1, 1)

    @pl.when(step == pl.num_programs(0) - 1)
    def _():
        parts[...] = summed[...].astype(BF).reshape(parts.shape)


def down_kernel(fourth_input, down_t, parts, summed):
    step = pl.program_id(0)

    @pl.when(step == 0)
    def _():
        summed[...] = jnp.zeros_like(summed)

    summed[...] += dot(fourth_input[...], down_t[...], 1, 1)

    @pl.when(step == pl.num_programs(0) - 1)
    def _():
        parts[...] = summed[...].astype(BF).reshape(parts.shape)


def output_kernel(parts, middle, rows):
    total_rows = (parts[0].astype(F32) + parts[1].astype(F32)) + (parts[2].astype(F32) + parts[3].astype(F32))
    low = (middle[...] + total_rows).astype(BF)
    for device in range(GRP):
        rows[device] = low


def widen_kernel(output_rows, grad_rows, layer_output, input_grad):
    width = layer_output.shape[1]
    layer_output[...] = output_rows[...].astype(F32).reshape(layer_output.shape)
    input_grad[...] = grad_rows[:, :, :width].astype(F32).reshape(input_grad.shape)


def text_kernel(place, rows, text):
    text[...] = rows[...].reshape(text.shape)


def third_back_kernel(
    place, parts, middle, branch, cotangent, gain_three, gain_out, numbers, grad_middle, low, gain_grad
):
    width = middle.shape[1]
    grads = (parts[0].astype(F32) + parts[1].astype(F32)) + (parts[2].astype(F32) + parts[3].astype(F32))
    hat, scale = row_norm(middle[...])
    total_rows = cotangent[...].astype(F32) + row_norm_back(grads, hat, scale, gain_three[...])
    grad_middle[...] = total_rows
    rounded = total_rows.astype(BF)
    wide = rounded.astype(F32)
    sum_grad = jnp.sum(wide * gain_out[...], axis=-1, keepdims=True) / width
    sum_cross = jnp.sum(wide * branch[...], axis=-1, keepdims=True) / width
    lanes = lanes_of(in_pairs([numbers[:, 0:1], numbers[:, 1:2], sum_grad, sum_cross]), BF)
    gain_grad[...] = jnp.sum(grads * hat, axis=0, keepdims=True)
    for device in range(GRP):
        low[device, :, :width] = rounded
        low[device, :, width:] = lanes


def attention_back_kernel(
    grad_rows, attended, projected, prob, gain_two, out_t, in_weight,
    grad_branch, second_input, grad_projected, grad_gain_two, parts,
):
    tokens, local = attended.shape
    width = grad_branch.shape[1]
    grad_branch[...] = grad_rows[:, :, :width].reshape(tokens, width)
    lanes = grad_rows[:, :, width:].reshape(tokens, LANES)
    mean, scale, sum_grad, sum_cross = (from_pairs(lanes, i) for i in range(4))
    hat = (attended[...] - mean) * scale
    gains = gain_two[...]
    second_input[...] = (hat * gains).astype(BF)
    grad_second = dot(grad_branch[...], out_t[...], 1, 0)
    grad_gain_two[...] = jnp.sum(grad_second * hat, axis=0, keepdims=True)
    grad_attended = (scale * (grad_second * gains - sum_grad - hat * sum_cross)).astype(BF)
    for head in range(local // HD):
        columns = [slice(i * local + head * HD, i * local + (head + 1) * HD) for i in range(3)]
        query_head, key_head, value_head = (projected[:, column] for column in columns)
        grad_head = grad_attended[:, head * HD : (head + 1) * HD]
        weights = prob[head]
        grad_weights = dot(grad_head, value_head, 1, 1)
        grad_scores = weights * (
            grad_weights - jnp.sum(weights * grad_weights, axis=-1, keepdims=True)
        )
        grad_scores = grad_scores.astype(BF)
        factor = HD ** (-0.5)
        grad_projected[:, columns[0]] = (dot(grad_scores, key_head, 1, 0) * factor).astype(BF)
        grad_projected[:, columns[1]] = (dot(grad_scores, query_head, 0, 0) * factor).astype(BF)
        grad_projected[:, columns[2]] = dot(weights.astype(BF), grad_head, 0, 0).astype(BF)
    parts[...] = dot(grad_projected[...], in_weight[...], 1, 1).astype(BF).reshape(parts.shape)


def first_back_kernel(
    place, parts, inputs, gain_one, grad_middle, gain_three_grad, low, gain_grads
):
    grads = (parts[0].astype(F32) + parts[1].astype(F32)) + (parts[2].astype(F32) + parts[3].astype(F32))
    hat, scale = row_norm(inputs[...].astype(F32))
    rows = grad_middle[...] + row_norm_back(grads, hat, scale, gain_one[...])
    rounded = rows.astype(BF)
    gain_grad = jnp.sum(grads * hat, axis=0, keepdims=True)
    width = gain_grad.shape[1]
    put_vector(gain_grads, 0, gain_grad)
    put_vector(gain_grads, width // LANES, gain_three_grad[...])
    for device in range(GRP):
        low[device, :, :width] = rounded
        low[device, :, width:] = gain_grads[...].astype(BF)


def sampler_back_kernel(
    grad_rows, mixer, query_rows, sources, prob, query_weight, gain_four_grad, gain_two_grad,
    grad_image, grad_keys, grad_values, grad_query, extra, across,
):
    width = query_rows.shape[1]
    full = grad_image.shape[1]
    query = query_rows[:NL, :].astype(BF)
    grad_image[...] = grad_rows[:2, :, :full].reshape(grad_image.shape)
    grad_sampled = dot(grad_image[...], mixer[...], 1, 0).astype(BF)
    for head in range(width // RHD):
        columns = slice(head * RHD, (head + 1) * RHD)
        value_columns = slice(width + head * RHD, width + (head + 1) * RHD)
        keys, values = sources[:, columns], sources[:, value_columns]
        grad_head = grad_sampled[:, columns]
        weights = prob[head]
        grad_weights = dot(grad_head, values, 1, 1)
        grad_scores = weights * (
            grad_weights - jnp.sum(weights * grad_weights, axis=-1, keepdims=True)
        )
        grad_scores = grad_scores.astype(BF)
        factor = RHD ** (-0.5)
        grad_query[:, columns] = (dot(grad_scores, keys, 1, 0) * factor).astype(BF)
        grad_keys[:, columns] = (dot(grad_scores, query[:, columns], 0, 0) * factor).astype(BF)
        grad_values[:, columns] = dot(weights.astype(BF), grad_head, 0, 0).astype(BF)
    low = grad_query[...]
    wide = low.astype(F32)
    sums = [
        jnp.sum(wide * query_rows[NL : NL + 1, :], axis=-1, keepdims=True),
        jnp.sum(wide * query_rows[:NL, :], axis=-1, keepdims=True),
    ]
    across[...] = jnp.zeros_like(across)
    across[:NL, :] = grad_image[...].astype(F32)
    across[NL : 2 * NL, :] = dot(low, query_weight[...], 1, 1)
    lanes = [grad_rows[i, :, full:].astype(F32) for i in range(GRP)]
    lanes = (lanes[0] + lanes[1]) + (lanes[2] + lanes[3])
    count = full // LANES
    for number in range(2):
        vector = [lanes[number * count + i : number * count + i + 1, :] for i in range(count)]
        across[LANES + number : LANES + number + 1, :] = jnp.concatenate(vector, axis=1)
    across[LANES + 2 : LANES + 3, :] = gain_four_grad[...]
    across[LANES + 3 : LANES + 4, :] = gain_two_grad[...]
    held = jnp.transpose(across[...])
    lane = lax.broadcasted_iota(jnp.int32, held.shape, 1)
    for number, column in enumerate(sums):
        held = jnp.where(lane == LANES + 4 + number, jnp.concatenate([column] * DP, axis=0), held)
    extra[...] = held


def turn(left, turned):
    tokens, columns = left.shape
    for at in range(0, columns, LANES):
        block = left[:, at : at + LANES].astype(F32)
        turned[at : at + LANES, :tokens] = jnp.transpose(block).astype(BF)


def wide_outer_kernel(count, *refs):
    step = pl.program_id(0)
    out, turned = refs[-2:]
    start = 0
    for piece in range(len(count)):
        left, right = refs[2 * piece], refs[2 * piece + 1]

        @pl.when(step == start)
        def _():
            turn(left, turned)

        @pl.when((step >= start) & (step < start + count[piece]))
        def _():
            out[...] = jnp.dot(turned[...], right[...], preferred_element_type=F32).astype(BF)

        start += count[piece]


def wide_outer(pieces, block, full, first, held=None):
    count, operands, specs, at = [], [], {}, 0
    for left, right in pieces:
        count.append(right.shape[1] // block)
        specs[len(operands) + 1] = pl.BlockSpec(
            (right.shape[0], block), lambda i, at=at, n=count[-1]: (0, jnp.clip(i - at, 0, n - 1))
        )
        operands += [left, right]
        at += count[-1]
    tokens, width = pieces[0][0].shape
    aliases = None
    if held is not None:
        specs[len(operands)] = pl.BlockSpec(memory_space=pl.ANY)
        aliases = {len(operands): 0}
        operands.append(held)

    def body(*refs):
        wide_outer_kernel(count, *refs[: 2 * len(pieces)], *refs[-2:])

    (out,) = call(
        body,
        [((width, full), BF)],
        operands,
        specs=specs,
        out_specs={0: pl.BlockSpec((width, block), lambda i: (0, first + i))},
        grid=(at,),
        scratch=[pltpu.VMEM((width, tokens), BF)],
        aliases=aliases,
    )
    return out


def outer_kernel(keep, kinds, places, *refs):
    step = pl.program_id(0)
    core, x, y = places[0], places[1], places[2]
    turned, chosen = refs[-2:]
    refs = list(refs[:-2])
    outs = [refs.pop() for _ in range(2 * len(KEPT) if keep else 1)][::-1]
    arrived = refs.pop() if keep else None
    side = core if keep else 1 - core

    def row_of(spot, rows, path):
        first, second = spot // 4, spot % 4
        off_x, off_y = (first, second) if path == 0 or not keep else (second, first)
        chip = (x + off_x) % XS * YS + (y + off_y) % YS
        return pl.multiple_of((2 * chip + side) * rows, rows)

    def put(path, first, rows, blocks):
        if not keep:
            outs[0][:, first : first + rows] = blocks.astype(BF)
            return
        at = 0
        for out in outs[path * len(KEPT) : (path + 1) * len(KEPT)]:
            for number in range(out.shape[0]):
                spot = at + number
                sent = spot if path == 0 else spot % 4 * 4 + spot // 4
                total_block = blocks[spot] + arrived[sent, first : first + rows].astype(F32)
                out[number, first : first + rows] = total_block.astype(BF)
            at += out.shape[0]

    for start, count, kind, path in kinds:
        used = [refs.pop(0) for _ in range({"plain": 1, "product": 2, "stacked": 3}[kind])]
        if kind == "plain":

            @pl.when((step >= start) & (step < start + count))
            def _():
                rows = used[0].shape[0] // DP
                blocks = [used[0][pl.ds(row_of(i, rows, path), rows), :] for i in range(XS * YS)]
                put(path, 0, rows, jnp.stack(blocks))

            continue
        tokens, rows = used[0].shape[0], used[0].shape[1] // DP
        half = XS * YS * rows

        @pl.when(step == start)
        def _():
            turn(used[0], turned)
            for spot in range(XS * YS):
                chosen[spot * rows : (spot + 1) * rows, :tokens] = turned[
                    pl.ds(row_of(spot, rows, path), rows), :tokens
                ]

        @pl.when((step >= start) & (step < start + count))
        def _():
            for number, right in enumerate(used[1:]):
                product = jnp.dot(chosen[:half, :tokens], right[...], preferred_element_type=F32)
                put(path, number * rows, rows, product.reshape(XS * YS, rows, product.shape[1]))


def outer_blocks(paths, block, arrived=None, after=()):
    x, y, core = coordinates()
    places = jnp.stack([core, x, y]).astype(jnp.int32)
    kinds, operands, specs, ends, at = [], [], {}, [], 0
    for path, pieces in enumerate(paths):
        for piece in pieces:
            kind = ("plain", "product", "stacked")[len(piece) - 1]
            count = piece[-1].shape[1] // block
            kinds.append((at, count, kind, path))
            for number, operand in enumerate(piece):
                if kind == "plain" or number > 0:
                    specs[len(operands)] = pl.BlockSpec(
                        (operand.shape[0], block), lambda i, s, at=at, n=count: (0, jnp.clip(i - at, 0, n - 1))
                    )
                operands.append(operand)
            at += count
        ends.append(at)
    width = paths[0][0][0].shape[1]
    rows = width // DP
    keep = arrived is not None
    if keep:
        specs[len(operands)] = pl.BlockSpec((XS * YS, rows, block), lambda i, s: (0, 0, i))
        operands.append(arrived)
        outs, out_specs = [], {}
        for first, end in ((0, ends[0]), (ends[0], ends[1])):
            for count in KEPT:
                out_specs[len(outs)] = pl.BlockSpec(
                    (count, rows, block), lambda i, s, first=first, end=end: (0, 0, jnp.clip(i, first, end - 1) - first)
                )
                outs.append(((count, rows, (end - first) * block), BF))
    else:
        outs = [((XS * YS, rows, at * block), BF)]
        out_specs = {0: pl.BlockSpec((XS * YS, rows, block), lambda i, s: (0, 0, i))}
    outs = call(
        partial(outer_kernel, keep, kinds),
        outs,
        operands,
        specs=specs,
        out_specs=out_specs,
        grid=(at,),
        scalars=(places,),
        scratch=[pltpu.VMEM((width, 2 * LANES), BF), pltpu.VMEM((width // 2, 2 * LANES), BF)],
        after=after,
    )
    return (outs[: len(KEPT)], outs[len(KEPT) :]) if keep else outs[0]


def step_along(values, along_x, step):
    return fetch(values, step if along_x else 0, 0 if along_x else step, 0)


def half_kernel(*refs):
    for number in range(4):
        arrived, held, out = refs[number], refs[4 + number], refs[8 + number]
        out[...] = (held[...].astype(F32) + arrived[...].astype(F32)).astype(BF)


def both_ways(first_held, last_held, after):
    arrived, sides, shapes = [], [], []
    for along_x, (_, right, far_right, far_left, left) in ((True, first_held), (False, last_held)):
        arrived += [step_along(far_right, along_x, -1), step_along(far_left, along_x, 1)]
        sides += [right, left]
        shapes += [right.shape] * 2
    specs = [
        pl.BlockSpec((2,) + shape[1:], lambda *_, first=number % 2: (first, 0, 0))
        for number, shape in enumerate(shapes)
    ]
    sides = call(
        half_kernel,
        [(shape, BF) for shape in shapes],
        arrived + sides,
        specs={4 + number: spec for number, spec in enumerate(specs)},
        out_specs=dict(enumerate(specs)),
        aliases={4 + number: number for number in range(4)},
        after=after,
    )
    moved = []
    for along_x, held, (right, left) in ((True, first_held, sides[:2]), (False, last_held, sides[2:])):
        moved.append([held[0], step_along(right, along_x, -1), step_along(left, along_x, 1)])
    return moved


def ring_moves(held, along_x):
    return [held[0]] + [step_along(held[step], along_x, -step) for step in range(1, 4)]


def sum_kernel(*refs):
    for parts, outs in ((refs[:3], refs[6:10]), (refs[3:6], refs[10:])):
        for number in range(4):
            first, second, third = (part[number].astype(F32) for part in parts)
            outs[number][...] = (first + (second + third)).astype(BF)


def last_sum_kernel(*refs):
    for parts, out in ((refs[:4], refs[8]), (refs[4:8], refs[9])):
        first, second, third, fourth = (part[...].astype(F32) for part in parts)
        out[...] = (first + second) + (third + fourth)


def sum_over_rings(first_moved, last_moved, after, after_last):
    moved = first_moved + last_moved
    shapes = [parts[0].shape[1:] for parts in (first_moved, last_moved)]
    blocks = call(sum_kernel, [(shape, BF) for shape in shapes for _ in range(4)], moved, after=after)
    moved = ring_moves(blocks[:4], False) + ring_moves(blocks[4:], True)
    return call(last_sum_kernel, [(shape, F32) for shape in shapes], moved, after=after_last)


def grp_gather(values):
    spread = jnp.broadcast_to(values[None], (GRP,) + values.shape)
    return lax.all_to_all(spread, "grp", 0, 0)


def swap(blocks):
    return lax.all_to_all(blocks, "grp", 0, 0)


def total(parts):
    return (parts[0] + parts[1]) + (parts[2] + parts[3])


def row_norm(values):
    center = values - jnp.mean(values, axis=-1, keepdims=True)
    spread = jnp.mean(center * center, axis=-1, keepdims=True)
    scale_rows = lax.rsqrt(spread + EPSILON)
    return center * scale_rows, scale_rows


def row_norm_back(grad_normed, normed, scale_rows, scale_gain):
    grad_hat = grad_normed * scale_gain
    return scale_rows * (
        grad_hat
        - jnp.mean(grad_hat, axis=-1, keepdims=True)
        - normed * jnp.mean(grad_hat * normed, axis=-1, keepdims=True)
    )


def shards(
    caption_token_index,
    lengths,
    slot_image_pair,
    features,
    text_table,
    latents,
    sampler_gain,
    sampler_query,
    sampler_source,
    sampler_mixer,
    norm_gain_one,
    attention_in,
    norm_gain_two,
    attention_out,
    norm_gain_three,
    feed_up,
    norm_gain_four,
    feed_down,
    cotangent,
):
    group = lax.axis_index("grp")
    place = lax.axis_index(DP_AXES)
    width = feed_down.shape[1] * DP
    hidden = feed_down.shape[0] * GRP
    own = width // DP
    local = attention_out.shape[0]
    local_ff = feed_up.shape[1]
    patches, feature_width = features.shape[1:]
    tokens = cotangent.shape[1]
    spans = caption_token_index.shape[1]
    own_rows = tokens // GRP

    quarter = patches // GRP
    source_part = jnp.concatenate([sampler_source[:, 0], sampler_source[:, 1]], axis=0)
    small_part = jnp.pad(latents.T, ((0, 0), (0, LANES - NL)))
    first_part = jnp.concatenate(
        [
            attention_in.reshape(own, 3 * local),
            attention_out.T,
            sampler_mixer.T,
            source_part,
            lax.dynamic_slice_in_dim(features[0], group * quarter, quarter, 0),
            sampler_query,
            small_part,
        ],
        axis=1,
    )
    second_part = jnp.concatenate([feed_up, feed_down.T], axis=1)
    first_all = lax.all_gather(first_part, DP_AXES, axis=0, tiled=True)
    second_all = lax.all_gather(second_part, DP_AXES, axis=0, tiled=True)

    def first_spec(number, columns):
        return pl.BlockSpec((width, columns), lambda *_: (0, number))

    table_rows = text_table.shape[0]
    table_block = lax.all_to_all(text_table, "grp", 1, 0, tiled=True)
    x, y, core = coordinates()
    flat_ids = caption_token_index[0]
    numbers = jnp.stack(
        [
            (flat_ids // 256).astype(BF),
            (flat_ids % 256).astype(BF),
            sampler_gain,
            norm_gain_one,
            norm_gain_three,
            norm_gain_four,
            jnp.pad(norm_gain_two, (0, own - norm_gain_two.shape[0])),
        ]
    )
    numbers = gather_offsets(jnp.pad(numbers, ((0, 16 - numbers.shape[0]), (0, 0))))
    wide_numbers = numbers.astype(F32)
    by_offset = (wide_numbers[:, :, :, 0] * 256 + wide_numbers[:, :, :, 1]).astype(jnp.int32)
    placed = jnp.moveaxis(jnp.roll(wide_numbers[:, :, :, 2:7], (core, x, y), axis=(0, 1, 2)), 0, 2)
    gains = placed
    query_gain, gain_one, gain_three, gain_four, gain_two = (
        gains[:, :, :, i].reshape(1, width) for i in range(5)
    )
    gain_two = gain_two.reshape(DP, own)[:, : norm_gain_two.shape[0]].reshape(1, local)

    def block_rows(ids):
        span = table_rows * DP
        held = ids % span // table_rows == place
        return jnp.where(held, ids // span * table_rows + ids % table_rows, -1)

    def one_hot(ids):
        return (block_rows(ids)[:, None] == jnp.arange(GRP * table_rows, dtype=jnp.int32)[None]).astype(BF)

    picked = dot(one_hot(by_offset.reshape(-1)), table_block, 1, 0).astype(BF)
    text_cols = scatter_offsets(picked.reshape(CS, XS, YS, spans, local))
    text_parts = grp_gather(text_cols)

    split_first = first_all.reshape(DP, own, first_all.shape[1])
    (pair_parts,) = call(
        pair_kernel,
        [((GRP, quarter, feature_width), BF)],
        [split_first],
        specs={0: pl.BlockSpec((1, quarter, feature_width), lambda i, s: (s[0], 0, 3))},
        scalars=(slot_image_pair,),
        after=(text_parts,),
    )
    pair_rows = swap(pair_parts).reshape(patches, feature_width)
    small_spec = first_spec(36, LANES)
    mixer_spec = first_spec(4, local)
    vector_rows = width // LANES
    (
        mixed, latent_values, latent_hat, latent_scale, query_input, query_rows, sampled, sources, sampler_prob,
    ) = call(
        sampler_kernel,
        [
            ((GRP, NL // GRP, width), F32),
            ((NL, width), F32),
            ((NL, width), F32),
            ((NL, LANES), F32),
            ((NL, width), BF),
            ((NL + 16, local), F32),
            ((NL, local), BF),
            ((patches, 2 * local), BF),
            ((local // RHD, NL, patches), F32),
        ],
        [pair_rows, first_all, first_all, split_first, split_first, first_all, query_gain],
        specs={
            1: small_spec,
            2: first_spec(8, local),
            3: pl.BlockSpec((DP, own // 2, local), lambda *_: (0, 0, 5)),
            4: pl.BlockSpec((DP, own // 2, local), lambda *_: (0, 1, 5)),
            5: mixer_spec,
        },
    )
    place_row = jnp.reshape(group, (1,)).astype(jnp.int32)
    latent_spec = pl.BlockSpec((NL // GRP, width), lambda i, s: (s[0], 0))
    (images,) = call(
        image_kernel,
        [((GRP, NL // GRP, width), BF)],
        [swap(mixed), latent_values],
        specs={1: latent_spec},
        scalars=(place_row,),
    )
    image_parts = swap(images)

    out_spec = first_spec(3, local)
    in_spec = first_spec(0, 3 * local)
    own_spec = pl.BlockSpec((own_rows, width), lambda i, s: (s[0], 0))
    blocks = ((GRP, own_rows, width), BF)
    wide_blocks = ((GRP, own_rows, width + LANES), BF)
    inputs, first_input, projected, prob, attended, branch_parts = call(
        attention_kernel,
        [
            ((tokens, width), BF),
            ((tokens, width), BF),
            ((tokens, 3 * local), BF),
            ((local // HD, tokens, tokens), F32),
            ((tokens, local), F32),
            ((GRP, own_rows, width + 2 * LANES), BF),
        ],
        [image_parts, text_parts, gain_one, first_all, gain_two, first_all],
        specs={3: in_spec, 5: out_spec},
        scalars=(lengths,),
        scratch=[pltpu.VMEM((2 * vector_rows, LANES), F32)],
    )
    middle, branch, third_input, second_numbers, gain_out = call(
        middle_kernel,
        [
            ((own_rows, width), F32),
            ((own_rows, width), F32),
            blocks,
            ((own_rows, LANES), F32),
            ((1, width), F32),
        ],
        [swap(branch_parts), inputs, gain_three],
        specs={1: own_spec},
        scalars=(place_row,),
    )

    grad_output = cotangent[0]
    hidden_block = 512
    steps = local_ff // hidden_block
    up_spec = pl.BlockSpec((width, hidden_block), lambda i: (0, i))
    down_spec = pl.BlockSpec((width, hidden_block), lambda i: (0, steps + i))
    columns_spec = pl.BlockSpec((tokens, hidden_block), lambda i: (0, i))
    row_spec = pl.BlockSpec((1, hidden_block), lambda i: (0, i))
    wide = ((tokens, local_ff), F32)
    activated, slope, grad_fourth, fourth_stats, third_rows = call(
        hidden_kernel,
        [wide, wide, wide, ((GRP, STATS, tokens), F32), ((tokens, width), BF)],
        [swap(third_input), grad_output, gain_four, second_all, second_all],
        specs={3: up_spec, 4: down_spec},
        grid=(steps,),
    )
    fourth_input, grad_up_rows, grad_gain_four, third_parts = call(
        hidden_back_kernel,
        [((tokens, local_ff), BF), ((tokens, local_ff), BF), ((1, local_ff), F32), blocks],
        [swap(fourth_stats), activated, slope, grad_fourth, gain_four, second_all],
        specs={1: columns_spec, 2: columns_spec, 3: columns_spec, 4: row_spec, 5: up_spec},
        out_specs={0: columns_spec, 1: columns_spec, 2: row_spec},
        grid=(steps,),
        scratch=[pltpu.VMEM((tokens, LANES), F32), pltpu.VMEM((tokens, width), F32)],
    )
    third_parts = swap(third_parts)
    outer_block = 512
    wide_columns = 2 * local_ff + 4 * local
    ff_grads = wide_outer(
        [(third_rows, grad_up_rows), (grad_output, fourth_input)], outer_block, wide_columns, 0
    )
    (down_parts,) = call(
        down_kernel,
        [blocks],
        [fourth_input, second_all],
        specs={0: columns_spec, 1: down_spec},
        grid=(steps,),
        scratch=[pltpu.VMEM((tokens, width), F32)],
    )
    grad_middle, branch_low, gain_three_grad = call(
        third_back_kernel,
        [((own_rows, width), F32), wide_blocks, ((1, width), F32)],
        [third_parts, middle, branch, grad_output, gain_three, gain_out, second_numbers],
        specs={3: own_spec},
        scalars=(place_row,),
        after=(down_parts,),
    )

    grad_branch, second_input, grad_projected, grad_gain_two, first_parts = call(
        attention_back_kernel,
        [
            ((tokens, width), BF),
            ((tokens, local), BF),
            ((tokens, 3 * local), BF),
            ((1, local), F32),
            blocks,
        ],
        [swap(branch_low), attended, projected, prob, gain_two, first_all, first_all],
        specs={5: out_spec, 6: in_spec},
    )
    layer_grads = wide_outer(
        [(first_input, grad_projected), (grad_branch, second_input)],
        outer_block,
        wide_columns,
        2 * local_ff // outer_block,
        ff_grads,
    )
    layer_sums = lax.psum_scatter(layer_grads, DP_AXES, scatter_dimension=0, tiled=True).astype(F32)
    (input_low,) = call(
        first_back_kernel,
        [wide_blocks],
        [swap(first_parts), inputs, gain_one, grad_middle, gain_three_grad],
        specs={1: own_spec},
        scalars=(place_row,),
        scratch=[pltpu.VMEM((2 * vector_rows, LANES), F32)],
    )
    input_low = swap(input_low)

    per_own = norm_gain_two.shape[0]
    gain_two_row = jnp.pad(grad_gain_two.reshape(DP, per_own), ((0, 0), (0, own - per_own))).reshape(1, width)
    image_low, grad_keys, grad_values, grad_query, extra = call(
        sampler_back_kernel,
        [((NL, width), BF), ((patches, local), BF), ((patches, local), BF), ((NL, local), BF), ((width, 2 * LANES), F32)],
        [input_low, first_all, query_rows, sources, sampler_prob, first_all, grad_gain_four, gain_two_row],
        specs={1: mixer_spec, 5: first_spec(8, local)},
        scratch=[pltpu.VMEM((2 * LANES, width), F32)],
    )

    paths = (
        [(image_low, sampled), (extra,)],
        [(query_input, grad_query), (pair_rows, grad_keys, grad_values)],
    )
    arrived = fetch(outer_blocks(paths, 256), 0, 0, 1)

    (text_low,) = call(
        text_kernel,
        [((spans, local), BF)],
        [input_low],
        specs={0: pl.BlockSpec((2, own_rows, local), lambda i, s: (1, 0, s[0]))},
        scalars=(place_row,),
    )
    text_column = jnp.stack(ring(text_low, 1))
    (output_rows,) = call(output_kernel, [blocks], [swap(down_parts), middle])
    first_held, last_held = outer_blocks(paths, 256, arrived, (text_column, output_rows))
    text_same = jnp.stack(ring(text_column, 0))
    first_moved, last_moved = both_ways(first_held, last_held, (text_same,))
    text_other = fetch(text_same, 0, 0, 1)
    text_all = jnp.concatenate([text_same, text_other]).reshape(DP * spans, local)
    table_sums = dot(one_hot(by_offset.reshape(-1)), text_all, 0, 0).astype(BF)
    table_rows = lax.all_to_all(table_sums, "grp", 0, 1, tiled=True)
    table_grad = table_rows.astype(F32)

    layer_output, input_grad = call(
        widen_kernel, [((tokens, width), F32)] * 2, [swap(output_rows), input_low]
    )
    first_sums, last_sums = sum_over_rings(first_moved, last_moved, (table_sums,), (table_rows,))
    cut = 2 * local_ff
    numbers = first_sums[:, local:]
    source_sums = last_sums[:, local:]

    latent_hat_own = lax.dynamic_slice_in_dim(latent_hat, place * own, own, 1)
    sampler_back = total(grp_gather(jnp.concatenate([numbers[:, NL:LANES].T, numbers[:, LANES + 4 : LANES + 6]], axis=1)))
    grad_query_norm = sampler_back[:, :own]
    sampler_means = sampler_back[:, own:] / width
    grad_latent_norm = latent_scale[:, :1] * (
        grad_query_norm * sampler_gain.astype(F32)
        - sampler_means[:, :1]
        - latent_hat_own * sampler_means[:, 1:]
    )
    sampler_gain_grad = jnp.sum(grad_query_norm * latent_hat_own, axis=0)
    latents_grad = numbers[:, :NL].T + grad_latent_norm
    return (
        layer_output[None],
        input_grad[None],
        table_grad,
        latents_grad,
        sampler_gain_grad,
        last_sums[:, :local],
        jnp.stack([source_sums[: own // 2], source_sums[own // 2 :]], axis=1),
        first_sums[:, :local].T,
        numbers[:, LANES],
        layer_sums[:, cut : cut + 3 * local].reshape(own, 3, local),
        numbers[:per_own, LANES + 3],
        layer_sums[:, cut + 3 * local :].T,
        numbers[:, LANES + 1],
        layer_sums[:, :local_ff],
        numbers[:, LANES + 2],
        layer_sums[:, local_ff:cut].T,
    )


def solution(mesh):
    mesh = Mesh(mesh.devices.reshape(GRP, XS, YS, CS), ("grp",) + DP_AXES)
    return jax.shard_map(
        shards,
        mesh=mesh,
        in_specs=(
            P(DP_AXES, None),
            P(DP_AXES),
            P(DP_AXES),
            P(DP_AXES, None, None),
            P(("grp",) + DP_AXES, None),
            P(None, DP_AXES),
            P(DP_AXES),
            P(DP_AXES, "grp"),
            P(DP_AXES, None, "grp"),
            P("grp", DP_AXES),
            P(DP_AXES),
            P(DP_AXES, None, "grp"),
            P(("grp",) + DP_AXES),
            P("grp", DP_AXES),
            P(DP_AXES),
            P(DP_AXES, "grp"),
            P(("grp",) + DP_AXES),
            P("grp", DP_AXES),
            P(DP_AXES, None, None),
        ),
        out_specs=(
            P(DP_AXES, None, None),
            P(DP_AXES, None, None),
            P(("grp",) + DP_AXES, None),
            P(None, DP_AXES),
            P(DP_AXES),
            P(DP_AXES, "grp"),
            P(DP_AXES, None, "grp"),
            P("grp", DP_AXES),
            P(DP_AXES),
            P(DP_AXES, None, "grp"),
            P(("grp",) + DP_AXES),
            P("grp", DP_AXES),
            P(DP_AXES),
            P(DP_AXES, "grp"),
            P(("grp",) + DP_AXES),
            P("grp", DP_AXES),
        ),
        check_vma=False,
    )
```

```python
from functools import partial

import jax
import jax.numpy as jnp
from jax import lax
from jax.experimental import pallas as pl
from jax.experimental.pallas import tpu as pltpu
from jax.sharding import Mesh, PartitionSpec as P

HD = 64
RHD = 128
NL = 64
EPSILON = 1e-05
NEG_FILL = -1e30
GRP = 4
XS = 4
YS = 4
CS = 2
DP = XS * YS * CS
DP_AXES = ("x", "y", "core")
LANES = 128
STATS = 8
KEPT = (4, 4, 2, 2, 4)
VMEM_LIMIT = 56 * 1024 * 1024
BF = jnp.bfloat16
F32 = jnp.float32


def dot(left, right, left_dims, right_dims):
    return lax.dot_general(
        left, right, (((left_dims,), (right_dims,)), ((), ())), preferred_element_type=F32
    )


def fetch(values, step_x, step_y, step_core):
    pairs = []
    for x in range(XS):
        for y in range(YS):
            for core in range(CS):
                source = (((x + step_x) % XS) * YS + (y + step_y) % YS) * CS + (core ^ step_core)
                pairs.append((source, (x * YS + y) * CS + core))
    return lax.ppermute(values, DP_AXES, pairs)


def coordinates():
    place = lax.axis_index(DP_AXES)
    return place // (YS * CS), place // CS % YS, place % CS


def ring(values, axis):
    steps = [(step, 0) if axis == 0 else (0, step) for step in range(4)]
    return [values] + [fetch(values, *step, 0) for step in steps[1:]]


def gather_offsets(values):
    over_y = jnp.stack(ring(values, 1))
    over_x = jnp.stack(ring(over_y, 0))
    return jnp.stack([over_x, fetch(over_x, 0, 0, 1)])


def dp_total(values):
    values = values + fetch(values, 0, 0, 1)
    for axis in (0, 1):
        parts = ring(values, axis)
        values = (parts[0] + parts[2]) + (parts[1] + parts[3])
    return values


def scatter_offsets(values):
    values = values[0] + fetch(values[1], 0, 0, 1)
    values = values[0] + sum(fetch(values[step], -step, 0, 0) for step in range(1, XS))
    return values[0] + sum(fetch(values[step], 0, -step, 0) for step in range(1, YS))


def call(
    body, outs, operands, specs=None, out_specs=None, grid=(1,), scalars=(), scratch=(), after=(), aliases=None
):
    specs = dict(specs or {})
    out_specs = dict(out_specs or {})

    def whole(shape):
        return pl.BlockSpec(shape, lambda *_: (0,) * len(shape))

    def wrapped(*refs):
        held = len(scalars) + len(operands)
        body(*refs[:held], *refs[held + len(after) :])

    in_specs = [specs.get(i, whole(operand.shape)) for i, operand in enumerate(operands)]
    in_specs += [pl.BlockSpec(memory_space=pl.ANY)] * len(after)
    return pl.pallas_call(
        wrapped,
        grid_spec=pltpu.PrefetchScalarGridSpec(
            num_scalar_prefetch=len(scalars),
            grid=grid,
            in_specs=in_specs,
            out_specs=[out_specs.get(i, whole(shape)) for i, (shape, _) in enumerate(outs)],
            scratch_shapes=list(scratch),
        ),
        out_shape=[jax.ShapeDtypeStruct(shape, dtype) for shape, dtype in outs],
        input_output_aliases={len(scalars) + i: out for i, out in (aliases or {}).items()},
        compiler_params=pltpu.CompilerParams(vmem_limit_bytes=VMEM_LIMIT),
    )(*scalars, *operands, *after)


def pack_kernel(place, projections, out_t, mixer_t, sources, features, query, latents, packed):
    local = query.shape[1]
    half = sources.shape[1]
    for i in range(3):
        packed[:, i * local : (i + 1) * local] = projections[i]
    packed[:, 3 * local : 4 * local] = out_t[...]
    packed[:, 4 * local : 5 * local] = mixer_t[...]
    for i in range(2):
        packed[i * half : (i + 1) * half, 5 * local : 6 * local] = sources[i]
    packed[:, 6 * local : 8 * local] = features[...]
    packed[:, 8 * local : 9 * local] = query[...]
    rows = jnp.concatenate([latents[...].astype(F32), jnp.zeros((NL, LANES - NL), F32)], axis=1)
    across = jnp.transpose(jnp.concatenate([rows, jnp.zeros((LANES - NL, LANES), F32)], axis=0))
    packed[:, 9 * local :] = across[:NL].astype(BF)


def pair_kernel(pair, features, spread):
    for device in range(GRP):
        spread[device] = features[0]


def query_kernel(
    small, query_weight, query_gain, gain_two, out_t,
    latents, latent_hat, latent_scale, query_input, query_rows, vectors,
):
    values = jnp.transpose(small[...].astype(F32))[:NL]
    latents[...] = values
    hat, scale = row_norm(values)
    latent_hat[...] = jnp.transpose(jnp.concatenate([hat, jnp.zeros_like(hat)], axis=0))
    latent_scale[...] = jnp.broadcast_to(scale, latent_scale.shape)
    gain = query_gain[...]
    normed = (hat * gain).astype(BF)
    query_input[...] = normed
    query_rows[:NL, :] = jnp.dot(normed, query_weight[...], preferred_element_type=F32)
    query_rows[NL:, :] = jnp.dot(
        jnp.broadcast_to(gain, (16, gain.shape[1])).astype(BF), query_weight[...], preferred_element_type=F32
    )
    gains = jnp.broadcast_to(gain_two[...], (16, gain_two.shape[1])).astype(BF)
    products = dot(gains, out_t[...], 1, 1)[:1]
    for number, vector in enumerate(in_pairs([products])):
        put_vector(vectors, number * (vector.shape[1] // LANES), vector)


def sampler_kernel(pair, query_rows, key_weight, value_weight, mixer, mixed, sampled, sources, prob):
    width = query_rows.shape[1]
    query = query_rows[:NL, :].astype(BF)
    rows = pair[...]
    keys, values = (
        jnp.dot(rows, weight[...].reshape(rows.shape[1], width), preferred_element_type=F32).astype(BF)
        for weight in (key_weight, value_weight)
    )
    sources[:, :width] = keys
    sources[:, width:] = values
    for head in range(width // RHD):
        columns = slice(head * RHD, (head + 1) * RHD)
        scores = dot(query[:, columns], keys[:, columns], 1, 1) * RHD ** (-0.5)
        exponent = jnp.exp(scores - jnp.max(scores, axis=-1, keepdims=True))
        weights = exponent / jnp.sum(exponent, axis=-1, keepdims=True)
        prob[head] = weights
        sampled[:, columns] = jnp.dot(
            weights.astype(BF), values[:, columns], preferred_element_type=F32
        ).astype(BF)
    mixed[...] = dot(sampled[...], mixer[...], 1, 1).reshape(mixed.shape)


def image_kernel(place, parts, latents, images):
    mixed = (parts[0] + parts[1]) + (parts[2] + parts[3])
    rows = (latents[...] + mixed).astype(BF)
    for device in range(GRP):
        images[device] = rows


def lanes_of(numbers, dtype):
    rows = numbers[0].shape[0]
    lane = lax.broadcasted_iota(jnp.int32, (rows, LANES), 1)
    held = jnp.zeros((rows, LANES), F32)
    for number, column in enumerate(numbers):
        held = jnp.where(lane == number, column, held)
    return held.astype(dtype)


def in_pairs(numbers):
    pairs = []
    for number in numbers:
        high = number.astype(BF).astype(F32)
        pairs += [high, number - high]
    return pairs


def from_pairs(lanes, number):
    wide = lanes.astype(F32)
    return wide[:, 2 * number : 2 * number + 1] + wide[:, 2 * number + 1 : 2 * number + 2]


def put_rows(columns):
    tokens = columns[0].shape[0]
    lane = lax.broadcasted_iota(jnp.int32, (tokens, tokens), 1)
    held = jnp.zeros((tokens, tokens), F32)
    for number, column in enumerate(columns):
        held = jnp.where(lane == number, column, held)
    return jnp.transpose(held)[:STATS]


def take_columns(stats):
    return jnp.transpose(jnp.concatenate([rows[...] for rows in stats], axis=0))


def put_vector(small, first, vector):
    for i in range(vector.shape[1] // LANES):
        small[first + i : first + i + 1, :] = vector[:, i * LANES : (i + 1) * LANES]


def attention_kernel(
    length, image, text, gain_one, in_weight, gain_two, out_t, vectors,
    inputs, first_input, projected, prob, attended, parts,
):
    images = NL
    inputs[:images, :] = image[...].reshape(images, inputs.shape[1])
    local = gain_two.shape[1]
    for device in range(GRP):
        inputs[images:, device * local : (device + 1) * local] = text[device]
    hat, _ = row_norm(inputs[...].astype(F32))
    first_input[...] = (hat * gain_one[...]).astype(BF)
    projected[...] = dot(first_input[...], in_weight[...], 1, 0).astype(BF)
    tokens = inputs.shape[0]
    query = lax.broadcasted_iota(jnp.int32, (tokens, tokens), 0)
    key = lax.broadcasted_iota(jnp.int32, (tokens, tokens), 1)
    allowed = (key <= query) & (key < NL + length[0])
    for head in range(local // HD):
        query_head, key_head, value_head = (
            projected[:, i * local + head * HD : i * local + (head + 1) * HD] for i in range(3)
        )
        scores = jnp.where(allowed, dot(query_head, key_head, 1, 1) * HD ** (-0.5), NEG_FILL)
        exponent = jnp.exp(scores - jnp.max(scores, axis=-1, keepdims=True))
        weights = exponent / jnp.sum(exponent, axis=-1, keepdims=True)
        prob[head] = weights
        attended[:, head * HD : (head + 1) * HD] = jnp.dot(
            weights.astype(BF), value_head, preferred_element_type=F32
        )
    values = attended[...]
    mean = jnp.mean(values, axis=-1, keepdims=True)
    center = values - mean
    square = jnp.sum(center * center, axis=-1, keepdims=True)
    gains = gain_two[...]
    width = inputs.shape[1]
    blocks = dot((center * gains).astype(BF), out_t[...], 1, 1).astype(BF)
    parts[:, :, :width] = blocks.reshape(GRP, tokens // GRP, width)
    numbers = lanes_of(in_pairs([mean, square]), BF)
    parts[:, :, width : width + LANES] = numbers.reshape(GRP, tokens // GRP, LANES)
    for device in range(GRP):
        parts[device, :, width + LANES :] = vectors[...].astype(BF)


def joined_stats(means, squares, own, full):
    mean = ((means[0] + means[1]) + (means[2] + means[3])) / GRP
    shifts = [part - mean for part in means]
    square = sum(squares[i] + own * shifts[i] * shifts[i] for i in range(GRP))
    return mean, lax.rsqrt(square / full + EPSILON), shifts


def middle_kernel(place, parts, inputs, gain_three, middle, branch, third_input, numbers, gain_out):
    own_rows, width = inputs.shape
    count = width // LANES
    lanes = [parts[i, :, width : width + LANES] for i in range(GRP)]
    mean, scale, shifts = joined_stats(
        [from_pairs(lane, 0) for lane in lanes], [from_pairs(lane, 1) for lane in lanes], width // GRP, width
    )
    vectors = []
    for device in range(GRP):
        pairs = parts[device, :, width + LANES :].astype(F32)
        rows = pairs[:count] + pairs[count:]
        vectors.append(jnp.concatenate([rows[i : i + 1] for i in range(count)], axis=1))
    gain_out[...] = (vectors[0] + vectors[1]) + (vectors[2] + vectors[3])
    gathered = sum(parts[i, :, :width].astype(F32) + shifts[i] * vectors[i] for i in range(GRP))
    added = scale * gathered
    branch[...] = added
    rows = inputs[...].astype(F32) + added
    middle[...] = rows
    numbers[...] = lanes_of([mean, scale], F32)
    hat, _ = row_norm(rows)
    low = (hat * gain_three[...]).astype(BF)
    for device in range(GRP):
        third_input[device] = low


def grad_fourth_kernel(cotangent, down_t, grad_fourth):
    grad_fourth[...] = dot(cotangent[...], down_t[...], 1, 0)


def hidden_kernel(third_input, grad_fourth, gain_four, up_weight, activated, slope, stats, third_rows):
    step = pl.program_id(0)
    block = up_weight.shape[1]
    rows = third_input[...].reshape(third_rows.shape)
    columns = pl.ds(step * block, block)
    values = dot(rows, up_weight[...], 1, 0)
    normal = 0.5 * (1.0 + lax.erf(values * (0.5**0.5)))
    activated[:, columns] = values * normal
    slope[:, columns] = normal + values * jnp.exp(-0.5 * values * values) * 0.3989422804014327

    @pl.when(step == pl.num_programs(0) - 1)
    def _():
        third_rows[...] = rows
        active = activated[...]
        grad_hat = grad_fourth[...] * gain_four[...]
        mean = jnp.mean(active, axis=-1, keepdims=True)
        center = active - mean
        stats[...] = put_rows(
            [
                mean,
                jnp.sum(center * center, axis=-1, keepdims=True),
                jnp.sum(grad_hat, axis=-1, keepdims=True),
                jnp.sum(grad_hat * center, axis=-1, keepdims=True),
            ]
        )


def hidden_back_kernel(
    first_stats, second_stats, third_stats, fourth_stats, activated, slope, grad_fourth, gain_four, up_weight,
    fourth_input, grad_up, grad_gain, parts, held, summed,
):
    step = pl.program_id(0)
    block = up_weight.shape[1]
    own = block * pl.num_programs(0)
    full = own * GRP

    @pl.when(step == 0)
    def _():
        columns = take_columns([first_stats, second_stats, third_stats, fourth_stats])
        means, squares = ([columns[:, STATS * i + n : STATS * i + n + 1] for i in range(GRP)] for n in (0, 1))
        mean, scale, shifts = joined_stats(means, squares, own, full)
        sums = [columns[:, STATS * i + 2 : STATS * i + 3] for i in range(GRP)]
        crosses = [columns[:, STATS * i + 3 : STATS * i + 4] + shifts[i] * sums[i] for i in range(GRP)]
        lane = lax.broadcasted_iota(jnp.int32, held.shape, 1)
        numbers = [
            mean,
            scale,
            ((sums[0] + sums[1]) + (sums[2] + sums[3])) / full,
            scale * ((crosses[0] + crosses[1]) + (crosses[2] + crosses[3])) / full,
        ]
        kept = jnp.zeros(held.shape, F32)
        for number, column in enumerate(numbers):
            kept = jnp.where(lane == number, column, kept)
        held[...] = kept
        summed[...] = jnp.zeros_like(summed)

    mean, scale, sum_grad, sum_cross = (held[:, i : i + 1] for i in range(4))
    gains = gain_four[...]
    hat = (activated[...] - mean) * scale
    fourth_input[...] = (hat * gains).astype(BF)
    grads = grad_fourth[...]
    grad_gain[...] = jnp.sum(grads * hat, axis=0, keepdims=True)
    low = (scale * (grads * gains - sum_grad - hat * sum_cross) * slope[...]).astype(BF)
    grad_up[...] = low
    summed[...] += dot(low, up_weight[...], 1, 1)

    @pl.when(step == pl.num_programs(0) - 1)
    def _():
        parts[...] = summed[...].astype(BF).reshape(parts.shape)


def down_kernel(fourth_input, down_t, parts, summed):
    step = pl.program_id(0)

    @pl.when(step == 0)
    def _():
        summed[...] = jnp.zeros_like(summed)

    summed[...] += dot(fourth_input[...], down_t[...], 1, 1)

    @pl.when(step == pl.num_programs(0) - 1)
    def _():
        parts[...] = summed[...].astype(BF).reshape(parts.shape)


def output_kernel(parts, middle, rows):
    total_rows = (parts[0].astype(F32) + parts[1].astype(F32)) + (parts[2].astype(F32) + parts[3].astype(F32))
    low = (middle[...] + total_rows).astype(BF)
    for device in range(GRP):
        rows[device] = low


def widen_kernel(output_rows, grad_rows, layer_output, input_grad):
    width = layer_output.shape[1]
    layer_output[...] = output_rows[...].astype(F32).reshape(layer_output.shape)
    input_grad[...] = grad_rows[:, :, :width].astype(F32).reshape(input_grad.shape)


def stack_kernel(*refs):
    for number, part in enumerate(refs[:-1]):
        refs[-1][number] = part[...]


def text_kernel(place, rows, text):
    text[...] = rows[...].reshape(text.shape)


def third_back_kernel(
    place, parts, middle, branch, cotangent, gain_three, gain_out, numbers, grad_middle, low, gain_grad
):
    width = middle.shape[1]
    grads = (parts[0].astype(F32) + parts[1].astype(F32)) + (parts[2].astype(F32) + parts[3].astype(F32))
    hat, scale = row_norm(middle[...])
    total_rows = cotangent[...].astype(F32) + row_norm_back(grads, hat, scale, gain_three[...])
    grad_middle[...] = total_rows
    rounded = total_rows.astype(BF)
    wide = rounded.astype(F32)
    sum_grad = jnp.sum(wide * gain_out[...], axis=-1, keepdims=True) / width
    sum_cross = jnp.sum(wide * branch[...], axis=-1, keepdims=True) / width
    lanes = lanes_of(in_pairs([numbers[:, 0:1], numbers[:, 1:2], sum_grad, sum_cross]), BF)
    gain_grad[...] = jnp.sum(grads * hat, axis=0, keepdims=True)
    for device in range(GRP):
        low[device, :, :width] = rounded
        low[device, :, width:] = lanes


def attention_back_kernel(
    grad_rows, attended, projected, prob, gain_two, out_t, in_weight,
    grad_branch, second_input, grad_projected, grad_gain_two, parts,
):
    tokens, local = attended.shape
    width = grad_branch.shape[1]
    grad_branch[...] = grad_rows[:, :, :width].reshape(tokens, width)
    lanes = grad_rows[:, :, width:].reshape(tokens, LANES)
    mean, scale, sum_grad, sum_cross = (from_pairs(lanes, i) for i in range(4))
    hat = (attended[...] - mean) * scale
    gains = gain_two[...]
    second_input[...] = (hat * gains).astype(BF)
    grad_second = dot(grad_branch[...], out_t[...], 1, 0)
    grad_gain_two[...] = jnp.sum(grad_second * hat, axis=0, keepdims=True)
    grad_attended = (scale * (grad_second * gains - sum_grad - hat * sum_cross)).astype(BF)
    for head in range(local // HD):
        columns = [slice(i * local + head * HD, i * local + (head + 1) * HD) for i in range(3)]
        query_head, key_head, value_head = (projected[:, column] for column in columns)
        grad_head = grad_attended[:, head * HD : (head + 1) * HD]
        weights = prob[head]
        grad_weights = dot(grad_head, value_head, 1, 1)
        grad_scores = weights * (
            grad_weights - jnp.sum(weights * grad_weights, axis=-1, keepdims=True)
        )
        grad_scores = grad_scores.astype(BF)
        factor = HD ** (-0.5)
        grad_projected[:, columns[0]] = (dot(grad_scores, key_head, 1, 0) * factor).astype(BF)
        grad_projected[:, columns[1]] = (dot(grad_scores, query_head, 0, 0) * factor).astype(BF)
        grad_projected[:, columns[2]] = dot(weights.astype(BF), grad_head, 0, 0).astype(BF)
    parts[...] = dot(grad_projected[...], in_weight[...], 1, 1).astype(BF).reshape(parts.shape)


def first_back_kernel(
    place, parts, inputs, gain_one, grad_middle, gain_three_grad, low, gain_grads
):
    grads = (parts[0].astype(F32) + parts[1].astype(F32)) + (parts[2].astype(F32) + parts[3].astype(F32))
    hat, scale = row_norm(inputs[...].astype(F32))
    rows = grad_middle[...] + row_norm_back(grads, hat, scale, gain_one[...])
    rounded = rows.astype(BF)
    gain_grad = jnp.sum(grads * hat, axis=0, keepdims=True)
    width = gain_grad.shape[1]
    put_vector(gain_grads, 0, gain_grad)
    put_vector(gain_grads, width // LANES, gain_three_grad[...])
    for device in range(GRP):
        low[device, :, :width] = rounded
        low[device, :, width:] = gain_grads[...].astype(BF)


def sampler_back_kernel(
    grad_rows, mixer, query_rows, sources, prob, query_weight, gain_four_grad, gain_two_grad,
    grad_image, grad_keys, grad_values, grad_query, extra, across,
):
    width = query_rows.shape[1]
    full = grad_image.shape[1]
    query = query_rows[:NL, :].astype(BF)
    grad_image[...] = grad_rows[:2, :, :full].reshape(grad_image.shape)
    grad_sampled = dot(grad_image[...], mixer[...], 1, 0).astype(BF)
    for head in range(width // RHD):
        columns = slice(head * RHD, (head + 1) * RHD)
        value_columns = slice(width + head * RHD, width + (head + 1) * RHD)
        keys, values = sources[:, columns], sources[:, value_columns]
        grad_head = grad_sampled[:, columns]
        weights = prob[head]
        grad_weights = dot(grad_head, values, 1, 1)
        grad_scores = weights * (
            grad_weights - jnp.sum(weights * grad_weights, axis=-1, keepdims=True)
        )
        grad_scores = grad_scores.astype(BF)
        factor = RHD ** (-0.5)
        grad_query[:, columns] = (dot(grad_scores, keys, 1, 0) * factor).astype(BF)
        grad_keys[:, columns] = (dot(grad_scores, query[:, columns], 0, 0) * factor).astype(BF)
        grad_values[:, columns] = dot(weights.astype(BF), grad_head, 0, 0).astype(BF)
    low = grad_query[...]
    wide = low.astype(F32)
    sums = [
        jnp.sum(wide * query_rows[NL : NL + 1, :], axis=-1, keepdims=True),
        jnp.sum(wide * query_rows[:NL, :], axis=-1, keepdims=True),
    ]
    across[...] = jnp.zeros_like(across)
    across[:NL, :] = grad_image[...].astype(F32)
    across[NL : 2 * NL, :] = dot(low, query_weight[...], 1, 1)
    lanes = [grad_rows[i, :, full:].astype(F32) for i in range(GRP)]
    lanes = (lanes[0] + lanes[1]) + (lanes[2] + lanes[3])
    count = full // LANES
    for number in range(2):
        vector = [lanes[number * count + i : number * count + i + 1, :] for i in range(count)]
        across[LANES + number : LANES + number + 1, :] = jnp.concatenate(vector, axis=1)
    across[LANES + 2 : LANES + 3, :] = gain_four_grad[...]
    across[LANES + 3 : LANES + 4, :] = gain_two_grad[...]
    held = jnp.transpose(across[...])
    lane = lax.broadcasted_iota(jnp.int32, held.shape, 1)
    for number, column in enumerate(sums):
        held = jnp.where(lane == LANES + 4 + number, jnp.concatenate([column] * DP, axis=0), held)
    extra[...] = held


def turn(left, turned):
    tokens, columns = left.shape
    for at in range(0, columns, LANES):
        block = left[:, at : at + LANES].astype(F32)
        turned[at : at + LANES, :tokens] = jnp.transpose(block).astype(BF)


def wide_outer_kernel(count, *refs):
    step = pl.program_id(0)
    out, turned = refs[-2:]
    start = 0
    for piece in range(len(count)):
        left, right = refs[2 * piece], refs[2 * piece + 1]

        @pl.when(step == start)
        def _():
            turn(left, turned)

        @pl.when((step >= start) & (step < start + count[piece]))
        def _():
            out[...] = jnp.dot(turned[...], right[...], preferred_element_type=F32).astype(BF)

        start += count[piece]


def wide_outer(pieces, block, full, first, held=None):
    count, operands, specs, at = [], [], {}, 0
    for left, right in pieces:
        count.append(right.shape[1] // block)
        specs[len(operands) + 1] = pl.BlockSpec(
            (right.shape[0], block), lambda i, at=at, n=count[-1]: (0, jnp.clip(i - at, 0, n - 1))
        )
        operands += [left, right]
        at += count[-1]
    tokens, width = pieces[0][0].shape
    aliases = None
    if held is not None:
        specs[len(operands)] = pl.BlockSpec(memory_space=pl.ANY)
        aliases = {len(operands): 0}
        operands.append(held)

    def body(*refs):
        wide_outer_kernel(count, *refs[: 2 * len(pieces)], *refs[-2:])

    (out,) = call(
        body,
        [((width, full), BF)],
        operands,
        specs=specs,
        out_specs={0: pl.BlockSpec((width, block), lambda i: (0, first + i))},
        grid=(at,),
        scratch=[pltpu.VMEM((width, tokens), BF)],
        aliases=aliases,
    )
    return out


def outer_kernel(keep, kinds, places, *refs):
    step = pl.program_id(0)
    core, x, y = places[0], places[1], places[2]
    turned, chosen = refs[-2:]
    refs = list(refs[:-2])
    outs = [refs.pop() for _ in range(2 * len(KEPT) if keep else 1)][::-1]
    arrived = refs.pop() if keep else None
    side = core if keep else 1 - core

    def row_of(spot, rows, path):
        first, second = spot // 4, spot % 4
        off_x, off_y = (first, second) if path == 0 or not keep else (second, first)
        chip = (x + off_x) % XS * YS + (y + off_y) % YS
        return pl.multiple_of((2 * chip + side) * rows, rows)

    def put(path, first, rows, blocks):
        if not keep:
            outs[0][:, first : first + rows] = blocks.astype(BF)
            return
        at = 0
        for out in outs[path * len(KEPT) : (path + 1) * len(KEPT)]:
            for number in range(out.shape[0]):
                spot = at + number
                sent = spot if path == 0 else spot % 4 * 4 + spot // 4
                total_block = blocks[spot] + arrived[sent, first : first + rows].astype(F32)
                out[number, first : first + rows] = total_block.astype(BF)
            at += out.shape[0]

    for start, count, kind, path in kinds:
        used = [refs.pop(0) for _ in range({"plain": 1, "product": 2, "stacked": 3}[kind])]
        if kind == "plain":

            @pl.when((step >= start) & (step < start + count))
            def _():
                rows = used[0].shape[0] // DP
                blocks = [used[0][pl.ds(row_of(i, rows, path), rows), :] for i in range(XS * YS)]
                put(path, 0, rows, jnp.stack(blocks))

            continue
        tokens, rows = used[0].shape[0], used[0].shape[1] // DP
        half = XS * YS * rows

        @pl.when(step == start)
        def _():
            turn(used[0], turned)
            for spot in range(XS * YS):
                chosen[spot * rows : (spot + 1) * rows, :tokens] = turned[
                    pl.ds(row_of(spot, rows, path), rows), :tokens
                ]

        @pl.when((step >= start) & (step < start + count))
        def _():
            for number, right in enumerate(used[1:]):
                product = jnp.dot(chosen[:half, :tokens], right[...], preferred_element_type=F32)
                put(path, number * rows, rows, product.reshape(XS * YS, rows, product.shape[1]))


def outer_blocks(paths, block, arrived=None, after=()):
    x, y, core = coordinates()
    places = jnp.stack([core, x, y]).astype(jnp.int32)
    kinds, operands, specs, ends, at = [], [], {}, [], 0
    for path, pieces in enumerate(paths):
        for piece in pieces:
            kind = ("plain", "product", "stacked")[len(piece) - 1]
            count = piece[-1].shape[1] // block
            kinds.append((at, count, kind, path))
            for number, operand in enumerate(piece):
                if kind == "plain" or number > 0:
                    specs[len(operands)] = pl.BlockSpec(
                        (operand.shape[0], block), lambda i, s, at=at, n=count: (0, jnp.clip(i - at, 0, n - 1))
                    )
                operands.append(operand)
            at += count
        ends.append(at)
    width = paths[0][0][0].shape[1]
    rows = width // DP
    keep = arrived is not None
    if keep:
        specs[len(operands)] = pl.BlockSpec((XS * YS, rows, block), lambda i, s: (0, 0, i))
        operands.append(arrived)
        outs, out_specs = [], {}
        for first, end in ((0, ends[0]), (ends[0], ends[1])):
            for count in KEPT:
                out_specs[len(outs)] = pl.BlockSpec(
                    (count, rows, block), lambda i, s, first=first, end=end: (0, 0, jnp.clip(i, first, end - 1) - first)
                )
                outs.append(((count, rows, (end - first) * block), BF))
    else:
        outs = [((XS * YS, rows, at * block), BF)]
        out_specs = {0: pl.BlockSpec((XS * YS, rows, block), lambda i, s: (0, 0, i))}
    outs = call(
        partial(outer_kernel, keep, kinds),
        outs,
        operands,
        specs=specs,
        out_specs=out_specs,
        grid=(at,),
        scalars=(places,),
        scratch=[pltpu.VMEM((width, 2 * LANES), BF), pltpu.VMEM((width // 2, 2 * LANES), BF)],
        after=after,
    )
    return (outs[: len(KEPT)], outs[len(KEPT) :]) if keep else outs[0]


def step_along(values, along_x, step):
    return fetch(values, step if along_x else 0, 0 if along_x else step, 0)


def half_kernel(*refs):
    for number in range(4):
        arrived, held, out = refs[number], refs[4 + number], refs[8 + number]
        out[...] = (held[...].astype(F32) + arrived[...].astype(F32)).astype(BF)


def both_ways(first_held, last_held):
    arrived, sides, shapes = [], [], []
    for along_x, (_, right, far_right, far_left, left) in ((True, first_held), (False, last_held)):
        arrived += [step_along(far_right, along_x, -1), step_along(far_left, along_x, 1)]
        sides += [right, left]
        shapes += [right.shape] * 2
    specs = [
        pl.BlockSpec((2,) + shape[1:], lambda *_, first=number % 2: (first, 0, 0))
        for number, shape in enumerate(shapes)
    ]
    sides = call(
        half_kernel,
        [(shape, BF) for shape in shapes],
        arrived + sides,
        specs={4 + number: spec for number, spec in enumerate(specs)},
        out_specs=dict(enumerate(specs)),
        aliases={4 + number: number for number in range(4)},
    )
    moved = []
    for along_x, held, (right, left) in ((True, first_held, sides[:2]), (False, last_held, sides[2:])):
        moved.append([held[0], step_along(right, along_x, -1), step_along(left, along_x, 1)])
    return moved


def ring_moves(held, along_x):
    return [held[0]] + [step_along(held[step], along_x, -step) for step in range(1, 4)]


def sum_kernel(*refs):
    for parts, outs in ((refs[:3], refs[6:10]), (refs[3:6], refs[10:])):
        for number in range(4):
            first, second, third = (part[number].astype(F32) for part in parts)
            outs[number][...] = (first + (second + third)).astype(BF)


def last_sum_kernel(*refs):
    mixer_grad, query_grad, source_grad, numbers, spread = refs[8:]
    sums = []
    for parts in (refs[:4], refs[4:8]):
        first, second, third, fourth = (part[...].astype(F32) for part in parts)
        sums.append((first + second) + (third + fourth))
    local = mixer_grad.shape[1]
    mixer_grad[...] = sums[0][:, :local]
    held = sums[0][:, local:]
    numbers[...] = held
    lane = lax.broadcasted_iota(jnp.int32, (held.shape[0], LANES), 1)
    means = [held[:, LANES + 4 + i : LANES + 5 + i] for i in range(2)]
    shared = jnp.concatenate([held[:, NL:LANES], jnp.zeros((held.shape[0], LANES - NL), F32)], axis=1)
    for i in range(2):
        shared = jnp.where(lane == NL + i, means[i], shared)
    for device in range(GRP):
        spread[device] = shared
    query_grad[...] = sums[1][:, :local]
    half = sums[1].shape[0] // 2
    for i in range(2):
        source_grad[i] = sums[1][i * half : (i + 1) * half, local:]


def latent_kernel(place, parts, numbers, hat, scale, gain, latents_grad, gain_grads):
    rows = (parts[0] + parts[1]) + (parts[2] + parts[3])
    width = gain.shape[1] * DP
    across = jnp.transpose(jnp.concatenate([rows, jnp.zeros_like(rows)], axis=0))
    direct = jnp.transpose(jnp.concatenate([numbers[...], jnp.zeros_like(numbers)], axis=0))
    hats = jnp.transpose(jnp.concatenate([hat[...], jnp.zeros_like(hat)], axis=0))[:NL, :NL]
    grad = across[:NL, :NL]
    normed = grad * gain[...] - rows[:, NL : NL + 1] / width - hats * (rows[:, NL + 1 : NL + 2] / width)
    latents_grad[...] = direct[:NL, :NL] + scale[:, :1] * normed
    gain_grads[...] = jnp.zeros_like(gain_grads)
    gain_grads[0:1, :] = jnp.sum(grad * hats, axis=0, keepdims=True)
    gain_grads[1:5, :] = direct[LANES : LANES + 4, :NL]


def layer_sum_kernel(sums, up_grad, down_grad, in_grad, out_grad):
    wide = up_grad.shape[1]
    local = out_grad.shape[1]
    up_grad[...] = sums[:, :wide].astype(F32)
    down_grad[...] = sums[:, wide : 2 * wide].astype(F32)
    for i in range(3):
        in_grad[i] = sums[:, 2 * wide + i * local : 2 * wide + (i + 1) * local].astype(F32)
    out_grad[...] = sums[:, 2 * wide + 3 * local :].astype(F32)


def sum_over_rings(first_moved, last_moved, after):
    moved = first_moved + last_moved
    shapes = [parts[0].shape[1:] for parts in (first_moved, last_moved)]
    blocks = call(sum_kernel, [(shape, BF) for shape in shapes for _ in range(4)], moved, after=after)
    return ring_moves(blocks[:4], False) + ring_moves(blocks[4:], True), blocks[0]


def last_sums(moved, after):
    rows, local = moved[0].shape[0], moved[4].shape[1] // 2
    outs = [(rows, local), (rows, local), (2, rows // 2, local), (rows, 2 * LANES), (GRP, rows, LANES)]
    return call(last_sum_kernel, [(shape, F32) for shape in outs], moved, after=after)


def grp_gather(values):
    spread = jnp.broadcast_to(values[None], (GRP,) + values.shape)
    return lax.all_to_all(spread, "grp", 0, 0)


def swap(blocks):
    return lax.all_to_all(blocks, "grp", 0, 0)


def total(parts):
    return (parts[0] + parts[1]) + (parts[2] + parts[3])


def row_norm(values):
    center = values - jnp.mean(values, axis=-1, keepdims=True)
    spread = jnp.mean(center * center, axis=-1, keepdims=True)
    scale_rows = lax.rsqrt(spread + EPSILON)
    return center * scale_rows, scale_rows


def row_norm_back(grad_normed, normed, scale_rows, scale_gain):
    grad_hat = grad_normed * scale_gain
    return scale_rows * (
        grad_hat
        - jnp.mean(grad_hat, axis=-1, keepdims=True)
        - normed * jnp.mean(grad_hat * normed, axis=-1, keepdims=True)
    )


def shards(
    caption_token_index,
    lengths,
    slot_image_pair,
    features,
    text_table,
    latents,
    sampler_gain,
    sampler_query,
    sampler_source,
    sampler_mixer,
    norm_gain_one,
    attention_in,
    norm_gain_two,
    attention_out,
    norm_gain_three,
    feed_up,
    norm_gain_four,
    feed_down,
    cotangent,
):
    group = lax.axis_index("grp")
    place = lax.axis_index(DP_AXES)
    width = feed_down.shape[1] * DP
    hidden = feed_down.shape[0] * GRP
    own = width // DP
    local = attention_out.shape[0]
    local_ff = feed_up.shape[1]
    patches, feature_width = features.shape[1:]
    tokens = cotangent.shape[1]
    spans = caption_token_index.shape[1]
    own_rows = tokens // GRP

    quarter = patches // GRP
    place_row = jnp.reshape(group, (1,)).astype(jnp.int32)
    (first_part,) = call(
        pack_kernel,
        [((own, 7 * local + feature_width + LANES), BF)],
        [
            jnp.transpose(attention_in, (1, 0, 2)),
            attention_out.T,
            sampler_mixer.T,
            jnp.transpose(sampler_source, (1, 0, 2)),
            features[0],
            sampler_query,
            latents,
        ],
        specs={4: pl.BlockSpec((quarter, feature_width), lambda i, s: (s[0], 0))},
        scalars=(place_row,),
    )
    second_part = jnp.concatenate([feed_up, feed_down.T], axis=1)
    first_all = lax.all_gather(first_part, DP_AXES, axis=0, tiled=True)
    second_all = lax.all_gather(second_part, DP_AXES, axis=0, tiled=True)

    def first_spec(number, columns):
        return pl.BlockSpec((width, columns), lambda *_: (0, number))

    table_rows = text_table.shape[0]
    table_block = lax.all_to_all(text_table, "grp", 1, 0, tiled=True)
    x, y, core = coordinates()
    flat_ids = caption_token_index[0]
    numbers = jnp.stack(
        [
            (flat_ids // 256).astype(BF),
            (flat_ids % 256).astype(BF),
            sampler_gain,
            norm_gain_one,
            norm_gain_three,
            norm_gain_four,
            jnp.pad(norm_gain_two, (0, own - norm_gain_two.shape[0])),
        ]
    )
    numbers = gather_offsets(jnp.pad(numbers, ((0, 16 - numbers.shape[0]), (0, 0))))
    wide_numbers = numbers.astype(F32)
    by_offset = (wide_numbers[:, :, :, 0] * 256 + wide_numbers[:, :, :, 1]).astype(jnp.int32)
    placed = jnp.moveaxis(jnp.roll(wide_numbers[:, :, :, 2:7], (core, x, y), axis=(0, 1, 2)), 0, 2)
    gains = placed
    query_gain, gain_one, gain_three, gain_four, gain_two = (
        gains[:, :, :, i].reshape(1, width) for i in range(5)
    )
    gain_two = gain_two.reshape(DP, own)[:, : norm_gain_two.shape[0]].reshape(1, local)

    def block_rows(ids):
        span = table_rows * DP
        held = ids % span // table_rows == place
        return jnp.where(held, ids // span * table_rows + ids % table_rows, -1)

    def one_hot(ids):
        return (block_rows(ids)[:, None] == jnp.arange(GRP * table_rows, dtype=jnp.int32)[None]).astype(BF)

    picked = dot(one_hot(by_offset.reshape(-1)), table_block, 1, 0).astype(BF)
    text_cols = scatter_offsets(picked.reshape(CS, XS, YS, spans, local))
    text_parts = grp_gather(text_cols)

    split_first = first_all.reshape(DP, own, first_all.shape[1])
    (pair_parts,) = call(
        pair_kernel,
        [((GRP, quarter, feature_width), BF)],
        [split_first],
        specs={0: pl.BlockSpec((1, quarter, feature_width), lambda i, s: (s[0], 0, 3))},
        scalars=(slot_image_pair,),
        after=(text_parts,),
    )
    pair_rows = swap(pair_parts).reshape(patches, feature_width)
    small_spec = first_spec(36, LANES)
    mixer_spec = first_spec(4, local)
    vector_rows = width // LANES
    latent_values, latent_hat_t, latent_scale, query_input, query_rows, vectors = call(
        query_kernel,
        [
            ((NL, width), F32),
            ((width, LANES), F32),
            ((NL, LANES), F32),
            ((NL, width), BF),
            ((NL + 16, local), F32),
            ((2 * vector_rows, LANES), F32),
        ],
        [first_all, first_all, query_gain, gain_two, first_all],
        specs={0: small_spec, 1: first_spec(8, local), 4: first_spec(3, local)},
    )
    mixed, sampled, sources, sampler_prob = call(
        sampler_kernel,
        [
            ((GRP, NL // GRP, width), F32),
            ((NL, local), BF),
            ((patches, 2 * local), BF),
            ((local // RHD, NL, patches), F32),
        ],
        [pair_rows, query_rows, split_first, split_first, first_all],
        specs={
            2: pl.BlockSpec((DP, own // 2, local), lambda *_: (0, 0, 5)),
            3: pl.BlockSpec((DP, own // 2, local), lambda *_: (0, 1, 5)),
            4: mixer_spec,
        },
    )
    latent_spec = pl.BlockSpec((NL // GRP, width), lambda i, s: (s[0], 0))
    (images,) = call(
        image_kernel,
        [((GRP, NL // GRP, width), BF)],
        [swap(mixed), latent_values],
        specs={1: latent_spec},
        scalars=(place_row,),
    )
    image_parts = swap(images)

    out_spec = first_spec(3, local)
    in_spec = first_spec(0, 3 * local)
    own_spec = pl.BlockSpec((own_rows, width), lambda i, s: (s[0], 0))
    blocks = ((GRP, own_rows, width), BF)
    wide_blocks = ((GRP, own_rows, width + LANES), BF)
    inputs, first_input, projected, prob, attended, branch_parts = call(
        attention_kernel,
        [
            ((tokens, width), BF),
            ((tokens, width), BF),
            ((tokens, 3 * local), BF),
            ((local // HD, tokens, tokens), F32),
            ((tokens, local), F32),
            ((GRP, own_rows, width + 2 * LANES), BF),
        ],
        [image_parts, text_parts, gain_one, first_all, gain_two, first_all, vectors],
        specs={3: in_spec, 5: out_spec},
        scalars=(lengths,),
    )
    middle, branch, third_input, second_numbers, gain_out = call(
        middle_kernel,
        [
            ((own_rows, width), F32),
            ((own_rows, width), F32),
            blocks,
            ((own_rows, LANES), F32),
            ((1, width), F32),
        ],
        [swap(branch_parts), inputs, gain_three],
        specs={1: own_spec},
        scalars=(place_row,),
    )

    grad_output = cotangent[0]
    hidden_block = 512
    steps = local_ff // hidden_block
    up_spec = pl.BlockSpec((width, hidden_block), lambda i: (0, i))
    down_spec = pl.BlockSpec((width, hidden_block), lambda i: (0, steps + i))
    columns_spec = pl.BlockSpec((tokens, hidden_block), lambda i: (0, i))
    row_spec = pl.BlockSpec((1, hidden_block), lambda i: (0, i))
    wide = ((tokens, local_ff), F32)
    (grad_fourth,) = call(
        grad_fourth_kernel,
        [wide],
        [grad_output, second_all],
        specs={1: down_spec},
        out_specs={0: columns_spec},
        grid=(steps,),
    )
    activated, slope, fourth_stats, third_rows = call(
        hidden_kernel,
        [wide, wide, ((STATS, tokens), F32), ((tokens, width), BF)],
        [swap(third_input), grad_fourth, gain_four, second_all],
        specs={3: up_spec},
        grid=(steps,),
    )
    fourth_stats = [fourth_stats] + [
        lax.ppermute(fourth_stats, "grp", [((i + step) % GRP, i) for i in range(GRP)]) for step in range(1, GRP)
    ]
    fourth_input, grad_up_rows, grad_gain_four, third_parts = call(
        hidden_back_kernel,
        [((tokens, local_ff), BF), ((tokens, local_ff), BF), ((1, local_ff), F32), blocks],
        [*fourth_stats, activated, slope, grad_fourth, gain_four, second_all],
        specs={4: columns_spec, 5: columns_spec, 6: columns_spec, 7: row_spec, 8: up_spec},
        out_specs={0: columns_spec, 1: columns_spec, 2: row_spec},
        grid=(steps,),
        scratch=[pltpu.VMEM((tokens, LANES), F32), pltpu.VMEM((tokens, width), F32)],
    )
    third_parts = swap(third_parts)
    outer_block = 512
    wide_columns = 2 * local_ff + 4 * local
    down_first = local_ff // outer_block
    down_grads = wide_outer([(grad_output, fourth_input)], outer_block, wide_columns, down_first)
    (down_parts,) = call(
        down_kernel,
        [blocks],
        [fourth_input, second_all],
        specs={0: columns_spec, 1: down_spec},
        grid=(steps,),
        scratch=[pltpu.VMEM((tokens, width), F32)],
    )
    grad_middle, branch_low, gain_three_grad = call(
        third_back_kernel,
        [((own_rows, width), F32), wide_blocks, ((1, width), F32)],
        [third_parts, middle, branch, grad_output, gain_three, gain_out, second_numbers],
        specs={3: own_spec},
        scalars=(place_row,),
        after=(down_grads,),
    )

    ff_grads = wide_outer([(third_rows, grad_up_rows)], outer_block, wide_columns, 0, down_grads)

    grad_branch, second_input, grad_projected, grad_gain_two, first_parts = call(
        attention_back_kernel,
        [
            ((tokens, width), BF),
            ((tokens, local), BF),
            ((tokens, 3 * local), BF),
            ((1, local), F32),
            blocks,
        ],
        [swap(branch_low), attended, projected, prob, gain_two, first_all, first_all],
        specs={5: out_spec, 6: in_spec},
        after=(ff_grads,),
    )
    layer_grads = wide_outer(
        [(first_input, grad_projected), (grad_branch, second_input)],
        outer_block,
        wide_columns,
        2 * local_ff // outer_block,
        ff_grads,
    )
    layer_sums = lax.psum_scatter(layer_grads, DP_AXES, scatter_dimension=0, tiled=True)
    (input_low,) = call(
        first_back_kernel,
        [wide_blocks],
        [swap(first_parts), inputs, gain_one, grad_middle, gain_three_grad],
        specs={1: own_spec},
        after=(down_parts,),
        scalars=(place_row,),
        scratch=[pltpu.VMEM((2 * vector_rows, LANES), F32)],
    )
    input_low = swap(input_low)

    per_own = norm_gain_two.shape[0]
    gain_two_row = jnp.pad(grad_gain_two.reshape(DP, per_own), ((0, 0), (0, own - per_own))).reshape(1, width)
    image_low, grad_keys, grad_values, grad_query, extra = call(
        sampler_back_kernel,
        [((NL, width), BF), ((patches, local), BF), ((patches, local), BF), ((NL, local), BF), ((width, 2 * LANES), F32)],
        [input_low, first_all, query_rows, sources, sampler_prob, first_all, grad_gain_four, gain_two_row],
        specs={1: mixer_spec, 5: first_spec(8, local)},
        scratch=[pltpu.VMEM((2 * LANES, width), F32)],
    )

    paths = (
        [(image_low, sampled), (extra,)],
        [(query_input, grad_query), (pair_rows, grad_keys, grad_values)],
    )
    arrived = fetch(outer_blocks(paths, 256), 0, 0, 1)

    (text_low,) = call(
        text_kernel,
        [((spans, local), BF)],
        [input_low],
        specs={0: pl.BlockSpec((2, own_rows, local), lambda i, s: (1, 0, s[0]))},
        scalars=(place_row,),
    )
    text_parts = ring(text_low, 1)
    first_held, last_held = outer_blocks(paths, 256, arrived, text_parts[1:])
    (text_column,) = call(stack_kernel, [((YS, spans, local), BF)], text_parts, after=first_held[:1])
    text_parts = ring(text_column, 0)
    (output_rows,) = call(
        output_kernel, [blocks], [swap(down_parts), middle], after=first_held[:1]
    )
    first_moved, last_moved = both_ways(first_held, last_held)
    (text_same,) = call(
        stack_kernel, [((XS, YS, spans, local), BF)], text_parts, after=(*first_moved[1:], *last_moved[1:], output_rows)
    )
    moved, first_block = sum_over_rings(first_moved, last_moved, ())
    (text_all,) = call(
        stack_kernel,
        [((CS, XS, YS, spans, local), BF)],
        [text_same, fetch(text_same, 0, 0, 1)],
        after=(first_block,),
    )
    table_sums = dot(one_hot(by_offset.reshape(-1)), text_all.reshape(DP * spans, local), 0, 0).astype(BF)
    table_rows = lax.all_to_all(table_sums, "grp", 0, 1, tiled=True)
    table_grad = table_rows.astype(F32)

    layer_output, input_grad = call(
        widen_kernel, [((tokens, width), F32)] * 2, [swap(output_rows), input_low]
    )
    mixer_grad, query_grad, source_grad, numbers, shared = last_sums(moved, (table_sums,))

    latents_grad, gain_grads = call(
        latent_kernel,
        [((NL, own), F32), ((8, own), F32)],
        [swap(shared), numbers, latent_hat_t, latent_scale, sampler_gain.astype(F32)[None]],
        specs={2: pl.BlockSpec((own, LANES), lambda i, s: (s[0], 0))},
        after=(table_rows,),
        scalars=(jnp.reshape(place, (1,)).astype(jnp.int32),),
    )
    up_grad, down_grad, in_grad, out_grad = call(
        layer_sum_kernel,
        [((own, local_ff), F32), ((own, local_ff), F32), ((3, own, local), F32), ((own, local), F32)],
        [layer_sums],
    )
    return (
        layer_output[None],
        input_grad[None],
        table_grad,
        latents_grad,
        gain_grads[0],
        query_grad,
        jnp.transpose(source_grad, (1, 0, 2)),
        mixer_grad.T,
        gain_grads[1],
        jnp.transpose(in_grad, (1, 0, 2)),
        gain_grads[4, :per_own],
        out_grad.T,
        gain_grads[2],
        up_grad,
        gain_grads[3],
        down_grad.T,
    )


def solution(mesh):
    mesh = Mesh(mesh.devices.reshape(GRP, XS, YS, CS), ("grp",) + DP_AXES)
    return jax.shard_map(
        shards,
        mesh=mesh,
        in_specs=(
            P(DP_AXES, None),
            P(DP_AXES),
            P(DP_AXES),
            P(DP_AXES, None, None),
            P(("grp",) + DP_AXES, None),
            P(None, DP_AXES),
            P(DP_AXES),
            P(DP_AXES, "grp"),
            P(DP_AXES, None, "grp"),
            P("grp", DP_AXES),
            P(DP_AXES),
            P(DP_AXES, None, "grp"),
            P(("grp",) + DP_AXES),
            P("grp", DP_AXES),
            P(DP_AXES),
            P(DP_AXES, "grp"),
            P(("grp",) + DP_AXES),
            P("grp", DP_AXES),
            P(DP_AXES, None, None),
        ),
        out_specs=(
            P(DP_AXES, None, None),
            P(DP_AXES, None, None),
            P(("grp",) + DP_AXES, None),
            P(None, DP_AXES),
            P(DP_AXES),
            P(DP_AXES, "grp"),
            P(DP_AXES, None, "grp"),
            P("grp", DP_AXES),
            P(DP_AXES),
            P(DP_AXES, None, "grp"),
            P(("grp",) + DP_AXES),
            P("grp", DP_AXES),
            P(DP_AXES),
            P(DP_AXES, "grp"),
            P(("grp",) + DP_AXES),
            P("grp", DP_AXES),
        ),
        check_vma=False,
    )
```

```python
from functools import partial

import jax
import jax.numpy as jnp
from jax import lax
from jax.experimental import pallas as pl
from jax.experimental.pallas import tpu as pltpu
from jax.sharding import Mesh, PartitionSpec as P

HD = 64
RHD = 128
NL = 64
EPSILON = 1e-05
NEG_FILL = -1e30
GRP = 4
XS = 4
YS = 4
CS = 2
DP = XS * YS * CS
DP_AXES = ("x", "y", "core")
LANES = 128
STATS = 8
KEPT = (4, 4, 2, 2, 4)
VMEM_LIMIT = 56 * 1024 * 1024
BF = jnp.bfloat16
F32 = jnp.float32


def dot(left, right, left_dims, right_dims):
    return lax.dot_general(
        left, right, (((left_dims,), (right_dims,)), ((), ())), preferred_element_type=F32
    )


def fetch(values, step_x, step_y, step_core):
    pairs = []
    for x in range(XS):
        for y in range(YS):
            for core in range(CS):
                source = (((x + step_x) % XS) * YS + (y + step_y) % YS) * CS + (core ^ step_core)
                pairs.append((source, (x * YS + y) * CS + core))
    return lax.ppermute(values, DP_AXES, pairs)


def coordinates():
    place = lax.axis_index(DP_AXES)
    return place // (YS * CS), place // CS % YS, place % CS


def ring(values, axis):
    steps = [(step, 0) if axis == 0 else (0, step) for step in range(4)]
    return [values] + [fetch(values, *step, 0) for step in steps[1:]]


def gather_offsets(values):
    over_y = jnp.stack(ring(values, 1))
    over_x = jnp.stack(ring(over_y, 0))
    return jnp.stack([over_x, fetch(over_x, 0, 0, 1)])


def dp_total(values):
    values = values + fetch(values, 0, 0, 1)
    for axis in (0, 1):
        parts = ring(values, axis)
        values = (parts[0] + parts[2]) + (parts[1] + parts[3])
    return values


def scatter_offsets(values):
    values = values[0] + fetch(values[1], 0, 0, 1)
    values = values[0] + sum(fetch(values[step], -step, 0, 0) for step in range(1, XS))
    return values[0] + sum(fetch(values[step], 0, -step, 0) for step in range(1, YS))


def call(
    body, outs, operands, specs=None, out_specs=None, grid=(1,), scalars=(), scratch=(), after=(), aliases=None
):
    specs = dict(specs or {})
    out_specs = dict(out_specs or {})

    def whole(shape):
        return pl.BlockSpec(shape, lambda *_: (0,) * len(shape))

    def wrapped(*refs):
        held = len(scalars) + len(operands)
        body(*refs[:held], *refs[held + len(after) :])

    in_specs = [specs.get(i, whole(operand.shape)) for i, operand in enumerate(operands)]
    in_specs += [pl.BlockSpec(memory_space=pl.ANY)] * len(after)
    return pl.pallas_call(
        wrapped,
        grid_spec=pltpu.PrefetchScalarGridSpec(
            num_scalar_prefetch=len(scalars),
            grid=grid,
            in_specs=in_specs,
            out_specs=[out_specs.get(i, whole(shape)) for i, (shape, _) in enumerate(outs)],
            scratch_shapes=list(scratch),
        ),
        out_shape=[jax.ShapeDtypeStruct(shape, dtype) for shape, dtype in outs],
        input_output_aliases={len(scalars) + i: out for i, out in (aliases or {}).items()},
        compiler_params=pltpu.CompilerParams(vmem_limit_bytes=VMEM_LIMIT),
    )(*scalars, *operands, *after)


def pack_kernel(place, projections, out_t, mixer_t, sources, features, query, latents, packed):
    local = query.shape[1]
    half = sources.shape[1]
    for i in range(3):
        packed[:, i * local : (i + 1) * local] = projections[i]
    packed[:, 3 * local : 4 * local] = out_t[...]
    packed[:, 4 * local : 5 * local] = mixer_t[...]
    for i in range(2):
        packed[i * half : (i + 1) * half, 5 * local : 6 * local] = sources[i]
    packed[:, 6 * local : 8 * local] = features[...]
    packed[:, 8 * local : 9 * local] = query[...]
    rows = jnp.concatenate([latents[...].astype(F32), jnp.zeros((NL, LANES - NL), F32)], axis=1)
    across = jnp.transpose(jnp.concatenate([rows, jnp.zeros((LANES - NL, LANES), F32)], axis=0))
    packed[:, 9 * local :] = across[:NL].astype(BF)


def pair_kernel(pair, features, spread):
    for device in range(GRP):
        spread[device] = features[0]


def query_kernel(
    small, query_weight, query_gain, gain_two, out_t,
    latents, latent_hat, latent_scale, query_input, query_rows, vectors,
):
    values = jnp.transpose(small[...].astype(F32))[:NL]
    latents[...] = values
    hat, scale = row_norm(values)
    latent_hat[...] = jnp.transpose(jnp.concatenate([hat, jnp.zeros_like(hat)], axis=0))
    latent_scale[...] = jnp.broadcast_to(scale, latent_scale.shape)
    gain = query_gain[...]
    normed = (hat * gain).astype(BF)
    query_input[...] = normed
    query_rows[:NL, :] = jnp.dot(normed, query_weight[...], preferred_element_type=F32)
    query_rows[NL:, :] = jnp.dot(
        jnp.broadcast_to(gain, (16, gain.shape[1])).astype(BF), query_weight[...], preferred_element_type=F32
    )
    gains = jnp.broadcast_to(gain_two[...], (16, gain_two.shape[1])).astype(BF)
    products = dot(gains, out_t[...], 1, 1)[:1]
    for number, vector in enumerate(in_pairs([products])):
        put_vector(vectors, number * (vector.shape[1] // LANES), vector)


def sampler_kernel(pair, query_rows, key_weight, value_weight, mixer, mixed, sampled, sources, prob):
    width = query_rows.shape[1]
    query = query_rows[:NL, :].astype(BF)
    rows = pair[...]
    keys, values = (
        jnp.dot(rows, weight[...].reshape(rows.shape[1], width), preferred_element_type=F32).astype(BF)
        for weight in (key_weight, value_weight)
    )
    sources[:, :width] = keys
    sources[:, width:] = values
    for head in range(width // RHD):
        columns = slice(head * RHD, (head + 1) * RHD)
        scores = dot(query[:, columns], keys[:, columns], 1, 1) * RHD ** (-0.5)
        exponent = jnp.exp(scores - jnp.max(scores, axis=-1, keepdims=True))
        weights = exponent / jnp.sum(exponent, axis=-1, keepdims=True)
        prob[head] = weights
        sampled[:, columns] = jnp.dot(
            weights.astype(BF), values[:, columns], preferred_element_type=F32
        ).astype(BF)
    mixed[...] = dot(sampled[...], mixer[...], 1, 1).reshape(mixed.shape)


def image_kernel(place, parts, latents, images):
    mixed = (parts[0] + parts[1]) + (parts[2] + parts[3])
    rows = (latents[...] + mixed).astype(BF)
    for device in range(GRP):
        images[device] = rows


def lanes_of(numbers, dtype):
    rows = numbers[0].shape[0]
    lane = lax.broadcasted_iota(jnp.int32, (rows, LANES), 1)
    held = jnp.zeros((rows, LANES), F32)
    for number, column in enumerate(numbers):
        held = jnp.where(lane == number, column, held)
    return held.astype(dtype)


def in_pairs(numbers):
    pairs = []
    for number in numbers:
        high = number.astype(BF).astype(F32)
        pairs += [high, number - high]
    return pairs


def from_pairs(lanes, number):
    wide = lanes.astype(F32)
    return wide[:, 2 * number : 2 * number + 1] + wide[:, 2 * number + 1 : 2 * number + 2]


def put_rows(columns):
    tokens = columns[0].shape[0]
    lane = lax.broadcasted_iota(jnp.int32, (tokens, tokens), 1)
    held = jnp.zeros((tokens, tokens), F32)
    for number, column in enumerate(columns):
        held = jnp.where(lane == number, column, held)
    return jnp.transpose(held)[:STATS]


def take_columns(stats):
    return jnp.transpose(jnp.concatenate([rows[...] for rows in stats], axis=0))


def put_vector(small, first, vector):
    for i in range(vector.shape[1] // LANES):
        small[first + i : first + i + 1, :] = vector[:, i * LANES : (i + 1) * LANES]


def attention_kernel(
    length, image, text, gain_one, in_weight, gain_two, out_t, vectors,
    inputs, first_input, projected, prob, attended, parts,
):
    images = NL
    inputs[:images, :] = image[...].reshape(images, inputs.shape[1])
    local = gain_two.shape[1]
    for device in range(GRP):
        inputs[images:, device * local : (device + 1) * local] = text[device]
    hat, _ = row_norm(inputs[...].astype(F32))
    first_input[...] = (hat * gain_one[...]).astype(BF)
    projected[...] = dot(first_input[...], in_weight[...], 1, 0).astype(BF)
    tokens = inputs.shape[0]
    query = lax.broadcasted_iota(jnp.int32, (tokens, tokens), 0)
    key = lax.broadcasted_iota(jnp.int32, (tokens, tokens), 1)
    allowed = (key <= query) & (key < NL + length[0])
    for head in range(local // HD):
        query_head, key_head, value_head = (
            projected[:, i * local + head * HD : i * local + (head + 1) * HD] for i in range(3)
        )
        scores = jnp.where(allowed, dot(query_head, key_head, 1, 1) * HD ** (-0.5), NEG_FILL)
        exponent = jnp.exp(scores - jnp.max(scores, axis=-1, keepdims=True))
        weights = exponent / jnp.sum(exponent, axis=-1, keepdims=True)
        prob[head] = weights
        attended[:, head * HD : (head + 1) * HD] = jnp.dot(
            weights.astype(BF), value_head, preferred_element_type=F32
        )
    values = attended[...]
    mean = jnp.mean(values, axis=-1, keepdims=True)
    center = values - mean
    square = jnp.sum(center * center, axis=-1, keepdims=True)
    gains = gain_two[...]
    width = inputs.shape[1]
    blocks = dot((center * gains).astype(BF), out_t[...], 1, 1).astype(BF)
    parts[:, :, :width] = blocks.reshape(GRP, tokens // GRP, width)
    numbers = lanes_of(in_pairs([mean, square]), BF)
    parts[:, :, width : width + LANES] = numbers.reshape(GRP, tokens // GRP, LANES)
    for device in range(GRP):
        parts[device, :, width + LANES :] = vectors[...].astype(BF)


def joined_stats(means, squares, own, full):
    mean = ((means[0] + means[1]) + (means[2] + means[3])) / GRP
    shifts = [part - mean for part in means]
    square = sum(squares[i] + own * shifts[i] * shifts[i] for i in range(GRP))
    return mean, lax.rsqrt(square / full + EPSILON), shifts


def middle_kernel(place, parts, inputs, gain_three, middle, branch, third_input, numbers, gain_out):
    own_rows, width = inputs.shape
    count = width // LANES
    lanes = [parts[i, :, width : width + LANES] for i in range(GRP)]
    mean, scale, shifts = joined_stats(
        [from_pairs(lane, 0) for lane in lanes], [from_pairs(lane, 1) for lane in lanes], width // GRP, width
    )
    vectors = []
    for device in range(GRP):
        pairs = parts[device, :, width + LANES :].astype(F32)
        rows = pairs[:count] + pairs[count:]
        vectors.append(jnp.concatenate([rows[i : i + 1] for i in range(count)], axis=1))
    gain_out[...] = (vectors[0] + vectors[1]) + (vectors[2] + vectors[3])
    gathered = sum(parts[i, :, :width].astype(F32) + shifts[i] * vectors[i] for i in range(GRP))
    added = scale * gathered
    branch[...] = added
    rows = inputs[...].astype(F32) + added
    middle[...] = rows
    numbers[...] = lanes_of([mean, scale], F32)
    hat, _ = row_norm(rows)
    low = (hat * gain_three[...]).astype(BF)
    for device in range(GRP):
        third_input[device] = low


def grad_fourth_kernel(cotangent, down_t, grad_fourth):
    grad_fourth[...] = dot(cotangent[...], down_t[...], 1, 0)


def hidden_kernel(third_input, grad_fourth, gain_four, up_weight, activated, slope, stats, third_rows):
    step = pl.program_id(0)
    block = up_weight.shape[1]
    rows = third_input[...].reshape(third_rows.shape)
    columns = pl.ds(step * block, block)
    values = dot(rows, up_weight[...], 1, 0)
    normal = 0.5 * (1.0 + lax.erf(values * (0.5**0.5)))
    activated[:, columns] = values * normal
    slope[:, columns] = normal + values * jnp.exp(-0.5 * values * values) * 0.3989422804014327

    @pl.when(step == pl.num_programs(0) - 1)
    def _():
        third_rows[...] = rows
        active = activated[...]
        grad_hat = grad_fourth[...] * gain_four[...]
        mean = jnp.mean(active, axis=-1, keepdims=True)
        center = active - mean
        stats[...] = put_rows(
            [
                mean,
                jnp.sum(center * center, axis=-1, keepdims=True),
                jnp.sum(grad_hat, axis=-1, keepdims=True),
                jnp.sum(grad_hat * center, axis=-1, keepdims=True),
            ]
        )


def hidden_back_kernel(
    first_stats, second_stats, third_stats, fourth_stats, activated, slope, grad_fourth, gain_four, up_weight,
    fourth_input, grad_up, grad_gain, parts, held, summed,
):
    step = pl.program_id(0)
    block = up_weight.shape[1]
    own = block * pl.num_programs(0)
    full = own * GRP

    @pl.when(step == 0)
    def _():
        columns = take_columns([first_stats, second_stats, third_stats, fourth_stats])
        means, squares = ([columns[:, STATS * i + n : STATS * i + n + 1] for i in range(GRP)] for n in (0, 1))
        mean, scale, shifts = joined_stats(means, squares, own, full)
        sums = [columns[:, STATS * i + 2 : STATS * i + 3] for i in range(GRP)]
        crosses = [columns[:, STATS * i + 3 : STATS * i + 4] + shifts[i] * sums[i] for i in range(GRP)]
        lane = lax.broadcasted_iota(jnp.int32, held.shape, 1)
        numbers = [
            mean,
            scale,
            ((sums[0] + sums[1]) + (sums[2] + sums[3])) / full,
            scale * ((crosses[0] + crosses[1]) + (crosses[2] + crosses[3])) / full,
        ]
        kept = jnp.zeros(held.shape, F32)
        for number, column in enumerate(numbers):
            kept = jnp.where(lane == number, column, kept)
        held[...] = kept
        summed[...] = jnp.zeros_like(summed)

    mean, scale, sum_grad, sum_cross = (held[:, i : i + 1] for i in range(4))
    gains = gain_four[...]
    hat = (activated[...] - mean) * scale
    fourth_input[...] = (hat * gains).astype(BF)
    grads = grad_fourth[...]
    grad_gain[...] = jnp.sum(grads * hat, axis=0, keepdims=True)
    low = (scale * (grads * gains - sum_grad - hat * sum_cross) * slope[...]).astype(BF)
    grad_up[...] = low
    summed[...] += dot(low, up_weight[...], 1, 1)

    @pl.when(step == pl.num_programs(0) - 1)
    def _():
        parts[...] = summed[...].astype(BF).reshape(parts.shape)


def down_kernel(fourth_input, down_t, parts, summed):
    step = pl.program_id(0)

    @pl.when(step == 0)
    def _():
        summed[...] = jnp.zeros_like(summed)

    summed[...] += dot(fourth_input[...], down_t[...], 1, 1)

    @pl.when(step == pl.num_programs(0) - 1)
    def _():
        parts[...] = summed[...].astype(BF).reshape(parts.shape)


def output_kernel(parts, middle, rows):
    total_rows = (parts[0].astype(F32) + parts[1].astype(F32)) + (parts[2].astype(F32) + parts[3].astype(F32))
    low = (middle[...] + total_rows).astype(BF)
    for device in range(GRP):
        rows[device] = low


def widen_kernel(output_rows, grad_rows, layer_output, input_grad):
    width = layer_output.shape[1]
    layer_output[...] = output_rows[...].astype(F32).reshape(layer_output.shape)
    input_grad[...] = grad_rows[:, :, :width].astype(F32).reshape(input_grad.shape)


def stack_kernel(*refs):
    for number, part in enumerate(refs[:-1]):
        refs[-1][number] = part[...]


def table_kernel(places, same, other, out):
    count, width = out.shape
    total_rows = jnp.zeros((count, width), F32)
    at = 0
    for rows in (same, other):
        held = rows[...].reshape(-1, width)
        ids = places[:, at : at + held.shape[0]]
        row = lax.broadcasted_iota(jnp.int32, (count, held.shape[0]), 0)
        chosen = jnp.where(row == ids, 1.0, 0.0).astype(BF)
        total_rows = total_rows + jnp.dot(chosen, held, preferred_element_type=F32)
        at += held.shape[0]
    out[...] = total_rows.astype(BF)


def text_kernel(place, rows, text):
    text[...] = rows[...].reshape(text.shape)


def third_back_kernel(
    place, parts, middle, branch, cotangent, gain_three, gain_out, numbers, grad_middle, low, gain_grad
):
    width = middle.shape[1]
    grads = (parts[0].astype(F32) + parts[1].astype(F32)) + (parts[2].astype(F32) + parts[3].astype(F32))
    hat, scale = row_norm(middle[...])
    total_rows = cotangent[...].astype(F32) + row_norm_back(grads, hat, scale, gain_three[...])
    grad_middle[...] = total_rows
    rounded = total_rows.astype(BF)
    wide = rounded.astype(F32)
    sum_grad = jnp.sum(wide * gain_out[...], axis=-1, keepdims=True) / width
    sum_cross = jnp.sum(wide * branch[...], axis=-1, keepdims=True) / width
    lanes = lanes_of(in_pairs([numbers[:, 0:1], numbers[:, 1:2], sum_grad, sum_cross]), BF)
    gain_grad[...] = jnp.sum(grads * hat, axis=0, keepdims=True)
    for device in range(GRP):
        low[device, :, :width] = rounded
        low[device, :, width:] = lanes


def attention_back_kernel(
    grad_rows, attended, projected, prob, gain_two, out_t, in_weight,
    grad_branch, second_input, grad_projected, grad_gain_two, parts,
):
    tokens, local = attended.shape
    width = grad_branch.shape[1]
    grad_branch[...] = grad_rows[:, :, :width].reshape(tokens, width)
    lanes = grad_rows[:, :, width:].reshape(tokens, LANES)
    mean, scale, sum_grad, sum_cross = (from_pairs(lanes, i) for i in range(4))
    hat = (attended[...] - mean) * scale
    gains = gain_two[...]
    second_input[...] = (hat * gains).astype(BF)
    grad_second = dot(grad_branch[...], out_t[...], 1, 0)
    grad_gain_two[...] = jnp.sum(grad_second * hat, axis=0, keepdims=True)
    grad_attended = (scale * (grad_second * gains - sum_grad - hat * sum_cross)).astype(BF)
    for head in range(local // HD):
        columns = [slice(i * local + head * HD, i * local + (head + 1) * HD) for i in range(3)]
        query_head, key_head, value_head = (projected[:, column] for column in columns)
        grad_head = grad_attended[:, head * HD : (head + 1) * HD]
        weights = prob[head]
        grad_weights = dot(grad_head, value_head, 1, 1)
        grad_scores = weights * (
            grad_weights - jnp.sum(weights * grad_weights, axis=-1, keepdims=True)
        )
        grad_scores = grad_scores.astype(BF)
        factor = HD ** (-0.5)
        grad_projected[:, columns[0]] = (dot(grad_scores, key_head, 1, 0) * factor).astype(BF)
        grad_projected[:, columns[1]] = (dot(grad_scores, query_head, 0, 0) * factor).astype(BF)
        grad_projected[:, columns[2]] = dot(weights.astype(BF), grad_head, 0, 0).astype(BF)
    parts[...] = dot(grad_projected[...], in_weight[...], 1, 1).astype(BF).reshape(parts.shape)


def first_back_kernel(
    place, parts, inputs, gain_one, grad_middle, gain_three_grad, low, gain_grads
):
    grads = (parts[0].astype(F32) + parts[1].astype(F32)) + (parts[2].astype(F32) + parts[3].astype(F32))
    hat, scale = row_norm(inputs[...].astype(F32))
    rows = grad_middle[...] + row_norm_back(grads, hat, scale, gain_one[...])
    rounded = rows.astype(BF)
    gain_grad = jnp.sum(grads * hat, axis=0, keepdims=True)
    width = gain_grad.shape[1]
    put_vector(gain_grads, 0, gain_grad)
    put_vector(gain_grads, width // LANES, gain_three_grad[...])
    for device in range(GRP):
        low[device, :, :width] = rounded
        low[device, :, width:] = gain_grads[...].astype(BF)


def sampler_back_kernel(
    grad_rows, mixer, query_rows, sources, prob, query_weight, gain_four_grad, gain_two_grad,
    grad_image, grad_keys, grad_values, grad_query, extra, across,
):
    width = query_rows.shape[1]
    full = grad_image.shape[1]
    query = query_rows[:NL, :].astype(BF)
    grad_image[...] = grad_rows[:2, :, :full].reshape(grad_image.shape)
    grad_sampled = dot(grad_image[...], mixer[...], 1, 0).astype(BF)
    for head in range(width // RHD):
        columns = slice(head * RHD, (head + 1) * RHD)
        value_columns = slice(width + head * RHD, width + (head + 1) * RHD)
        keys, values = sources[:, columns], sources[:, value_columns]
        grad_head = grad_sampled[:, columns]
        weights = prob[head]
        grad_weights = dot(grad_head, values, 1, 1)
        grad_scores = weights * (
            grad_weights - jnp.sum(weights * grad_weights, axis=-1, keepdims=True)
        )
        grad_scores = grad_scores.astype(BF)
        factor = RHD ** (-0.5)
        grad_query[:, columns] = (dot(grad_scores, keys, 1, 0) * factor).astype(BF)
        grad_keys[:, columns] = (dot(grad_scores, query[:, columns], 0, 0) * factor).astype(BF)
        grad_values[:, columns] = dot(weights.astype(BF), grad_head, 0, 0).astype(BF)
    low = grad_query[...]
    wide = low.astype(F32)
    sums = [
        jnp.sum(wide * query_rows[NL : NL + 1, :], axis=-1, keepdims=True),
        jnp.sum(wide * query_rows[:NL, :], axis=-1, keepdims=True),
    ]
    across[...] = jnp.zeros_like(across)
    across[:NL, :] = grad_image[...].astype(F32)
    across[NL : 2 * NL, :] = dot(low, query_weight[...], 1, 1)
    lanes = [grad_rows[i, :, full:].astype(F32) for i in range(GRP)]
    lanes = (lanes[0] + lanes[1]) + (lanes[2] + lanes[3])
    count = full // LANES
    for number in range(2):
        vector = [lanes[number * count + i : number * count + i + 1, :] for i in range(count)]
        across[LANES + number : LANES + number + 1, :] = jnp.concatenate(vector, axis=1)
    across[LANES + 2 : LANES + 3, :] = gain_four_grad[...]
    across[LANES + 3 : LANES + 4, :] = gain_two_grad[...]
    held = jnp.transpose(across[...])
    lane = lax.broadcasted_iota(jnp.int32, held.shape, 1)
    for number, column in enumerate(sums):
        held = jnp.where(lane == LANES + 4 + number, jnp.concatenate([column] * DP, axis=0), held)
    extra[...] = held


def turn(left, turned):
    tokens, columns = left.shape
    for at in range(0, columns, LANES):
        block = left[:, at : at + LANES].astype(F32)
        turned[at : at + LANES, :tokens] = jnp.transpose(block).astype(BF)


def wide_outer_kernel(count, *refs):
    step = pl.program_id(0)
    out, turned = refs[-2:]
    start = 0
    for piece in range(len(count)):
        left, right = refs[2 * piece], refs[2 * piece + 1]

        @pl.when(step == start)
        def _():
            turn(left, turned)

        @pl.when((step >= start) & (step < start + count[piece]))
        def _():
            out[...] = jnp.dot(turned[...], right[...], preferred_element_type=F32).astype(BF)

        start += count[piece]


def wide_outer(pieces, block, full, first, held=None):
    count, operands, specs, at = [], [], {}, 0
    for left, right in pieces:
        count.append(right.shape[1] // block)
        specs[len(operands) + 1] = pl.BlockSpec(
            (right.shape[0], block), lambda i, at=at, n=count[-1]: (0, jnp.clip(i - at, 0, n - 1))
        )
        operands += [left, right]
        at += count[-1]
    tokens, width = pieces[0][0].shape
    aliases = None
    if held is not None:
        specs[len(operands)] = pl.BlockSpec(memory_space=pl.ANY)
        aliases = {len(operands): 0}
        operands.append(held)

    def body(*refs):
        wide_outer_kernel(count, *refs[: 2 * len(pieces)], *refs[-2:])

    (out,) = call(
        body,
        [((width, full), BF)],
        operands,
        specs=specs,
        out_specs={0: pl.BlockSpec((width, block), lambda i: (0, first + i))},
        grid=(at,),
        scratch=[pltpu.VMEM((width, tokens), BF)],
        aliases=aliases,
    )
    return out


def outer_kernel(keep, kinds, places, *refs):
    step = pl.program_id(0)
    core, x, y = places[0], places[1], places[2]
    turned, chosen = refs[-2:]
    refs = list(refs[:-2])
    outs = [refs.pop() for _ in range(2 * len(KEPT) if keep else 1)][::-1]
    arrived = refs.pop() if keep else None
    side = core if keep else 1 - core

    def row_of(spot, rows, path):
        first, second = spot // 4, spot % 4
        off_x, off_y = (first, second) if path == 0 or not keep else (second, first)
        chip = (x + off_x) % XS * YS + (y + off_y) % YS
        return pl.multiple_of((2 * chip + side) * rows, rows)

    def put(path, first, rows, blocks):
        if not keep:
            outs[0][:, first : first + rows] = blocks.astype(BF)
            return
        at = 0
        for out in outs[path * len(KEPT) : (path + 1) * len(KEPT)]:
            for number in range(out.shape[0]):
                spot = at + number
                sent = spot if path == 0 else spot % 4 * 4 + spot // 4
                total_block = blocks[spot] + arrived[sent, first : first + rows].astype(F32)
                out[number, first : first + rows] = total_block.astype(BF)
            at += out.shape[0]

    for start, count, kind, path in kinds:
        used = [refs.pop(0) for _ in range({"plain": 1, "product": 2, "stacked": 3}[kind])]
        if kind == "plain":

            @pl.when((step >= start) & (step < start + count))
            def _():
                rows = used[0].shape[0] // DP
                blocks = [used[0][pl.ds(row_of(i, rows, path), rows), :] for i in range(XS * YS)]
                put(path, 0, rows, jnp.stack(blocks))

            continue
        tokens, rows = used[0].shape[0], used[0].shape[1] // DP
        half = XS * YS * rows

        @pl.when(step == start)
        def _():
            turn(used[0], turned)
            for spot in range(XS * YS):
                chosen[spot * rows : (spot + 1) * rows, :tokens] = turned[
                    pl.ds(row_of(spot, rows, path), rows), :tokens
                ]

        @pl.when((step >= start) & (step < start + count))
        def _():
            for number, right in enumerate(used[1:]):
                product = jnp.dot(chosen[:half, :tokens], right[...], preferred_element_type=F32)
                put(path, number * rows, rows, product.reshape(XS * YS, rows, product.shape[1]))


def outer_blocks(paths, block, arrived=None, after=()):
    x, y, core = coordinates()
    places = jnp.stack([core, x, y]).astype(jnp.int32)
    kinds, operands, specs, ends, at = [], [], {}, [], 0
    for path, pieces in enumerate(paths):
        for piece in pieces:
            kind = ("plain", "product", "stacked")[len(piece) - 1]
            count = piece[-1].shape[1] // block
            kinds.append((at, count, kind, path))
            for number, operand in enumerate(piece):
                if kind == "plain" or number > 0:
                    specs[len(operands)] = pl.BlockSpec(
                        (operand.shape[0], block), lambda i, s, at=at, n=count: (0, jnp.clip(i - at, 0, n - 1))
                    )
                operands.append(operand)
            at += count
        ends.append(at)
    width = paths[0][0][0].shape[1]
    rows = width // DP
    keep = arrived is not None
    if keep:
        specs[len(operands)] = pl.BlockSpec((XS * YS, rows, block), lambda i, s: (0, 0, i))
        operands.append(arrived)
        outs, out_specs = [], {}
        for first, end in ((0, ends[0]), (ends[0], ends[1])):
            for count in KEPT:
                out_specs[len(outs)] = pl.BlockSpec(
                    (count, rows, block), lambda i, s, first=first, end=end: (0, 0, jnp.clip(i, first, end - 1) - first)
                )
                outs.append(((count, rows, (end - first) * block), BF))
    else:
        outs = [((XS * YS, rows, at * block), BF)]
        out_specs = {0: pl.BlockSpec((XS * YS, rows, block), lambda i, s: (0, 0, i))}
    outs = call(
        partial(outer_kernel, keep, kinds),
        outs,
        operands,
        specs=specs,
        out_specs=out_specs,
        grid=(at,),
        scalars=(places,),
        scratch=[pltpu.VMEM((width, 2 * LANES), BF), pltpu.VMEM((width // 2, 2 * LANES), BF)],
        after=after,
    )
    return (outs[: len(KEPT)], outs[len(KEPT) :]) if keep else outs[0]


def step_along(values, along_x, step):
    return fetch(values, step if along_x else 0, 0 if along_x else step, 0)


def half_kernel(*refs):
    for number in range(4):
        arrived, held, out = refs[number], refs[4 + number], refs[8 + number]
        out[...] = (held[...].astype(F32) + arrived[...].astype(F32)).astype(BF)


def both_ways(first_held, last_held):
    arrived, sides, shapes = [], [], []
    for along_x, (_, right, far_right, far_left, left) in ((True, first_held), (False, last_held)):
        arrived += [step_along(far_right, along_x, -1), step_along(far_left, along_x, 1)]
        sides += [right, left]
        shapes += [right.shape] * 2
    specs = [
        pl.BlockSpec((2,) + shape[1:], lambda *_, first=number % 2: (first, 0, 0))
        for number, shape in enumerate(shapes)
    ]
    sides = call(
        half_kernel,
        [(shape, BF) for shape in shapes],
        arrived + sides,
        specs={4 + number: spec for number, spec in enumerate(specs)},
        out_specs=dict(enumerate(specs)),
        aliases={4 + number: number for number in range(4)},
    )
    moved = []
    for along_x, held, (right, left) in ((True, first_held, sides[:2]), (False, last_held, sides[2:])):
        moved.append([held[0], step_along(right, along_x, -1), step_along(left, along_x, 1)])
    return moved


def ring_moves(held, along_x):
    return [held[0]] + [step_along(held[step], along_x, -step) for step in range(1, 4)]


def sum_kernel(*refs):
    for parts, outs in ((refs[:3], refs[6:10]), (refs[3:6], refs[10:])):
        for number in range(4):
            first, second, third = (part[number].astype(F32) for part in parts)
            outs[number][...] = (first + (second + third)).astype(BF)


def last_sum_kernel(*refs):
    mixer_grad, query_grad, source_grad, numbers, spread, gain_grads = refs[8:]
    sums = []
    for parts in (refs[:4], refs[4:8]):
        first, second, third, fourth = (part[...].astype(F32) for part in parts)
        sums.append((first + second) + (third + fourth))
    local = mixer_grad.shape[1]
    mixer_grad[...] = sums[0][:, :local]
    held = sums[0][:, local:]
    numbers[...] = held
    across = jnp.transpose(jnp.concatenate([held, jnp.zeros_like(held)], axis=0))
    gain_grads[...] = across[LANES : LANES + 8, : held.shape[0]]
    lane = lax.broadcasted_iota(jnp.int32, (held.shape[0], LANES), 1)
    means = [held[:, LANES + 4 + i : LANES + 5 + i] for i in range(2)]
    shared = jnp.concatenate([held[:, NL:LANES], jnp.zeros((held.shape[0], LANES - NL), F32)], axis=1)
    for i in range(2):
        shared = jnp.where(lane == NL + i, means[i], shared)
    for device in range(GRP):
        spread[device] = shared
    query_grad[...] = sums[1][:, :local]
    half = sums[1].shape[0] // 2
    for i in range(2):
        source_grad[i] = sums[1][i * half : (i + 1) * half, local:]


def latent_kernel(place, parts, numbers, hat, scale, gain, latents_grad, gain_grad):
    rows = (parts[0] + parts[1]) + (parts[2] + parts[3])
    width = gain.shape[1] * DP
    across = jnp.transpose(jnp.concatenate([rows, jnp.zeros_like(rows)], axis=0))
    direct = jnp.transpose(jnp.concatenate([numbers[...], jnp.zeros_like(numbers)], axis=0))
    hats = jnp.transpose(jnp.concatenate([hat[...], jnp.zeros_like(hat)], axis=0))[:NL, :NL]
    grad = across[:NL, :NL]
    normed = grad * gain[...] - rows[:, NL : NL + 1] / width - hats * (rows[:, NL + 1 : NL + 2] / width)
    latents_grad[...] = direct[:NL, :NL] + scale[:, :1] * normed
    gain_grad[...] = jnp.sum(grad * hats, axis=0, keepdims=True)


def layer_sum_kernel(sums, up_grad, down_grad, in_grad, out_grad):
    wide = up_grad.shape[1]
    local = out_grad.shape[1]
    up_grad[...] = sums[:, :wide].astype(F32)
    down_grad[...] = sums[:, wide : 2 * wide].astype(F32)
    for i in range(3):
        in_grad[i] = sums[:, 2 * wide + i * local : 2 * wide + (i + 1) * local].astype(F32)
    out_grad[...] = sums[:, 2 * wide + 3 * local :].astype(F32)


def sum_over_rings(first_moved, last_moved, after):
    moved = first_moved + last_moved
    shapes = [parts[0].shape[1:] for parts in (first_moved, last_moved)]
    blocks = call(sum_kernel, [(shape, BF) for shape in shapes for _ in range(4)], moved, after=after)
    return ring_moves(blocks[:4], False) + ring_moves(blocks[4:], True), blocks[0]


def last_sums(moved, after):
    rows, local = moved[0].shape[0], moved[4].shape[1] // 2
    outs = [(rows, local), (rows, local), (2, rows // 2, local), (rows, 2 * LANES), (GRP, rows, LANES), (8, rows)]
    return call(last_sum_kernel, [(shape, F32) for shape in outs], moved, after=after)


def grp_gather(values):
    spread = jnp.broadcast_to(values[None], (GRP,) + values.shape)
    return lax.all_to_all(spread, "grp", 0, 0)


def swap(blocks):
    return lax.all_to_all(blocks, "grp", 0, 0)


def total(parts):
    return (parts[0] + parts[1]) + (parts[2] + parts[3])


def row_norm(values):
    center = values - jnp.mean(values, axis=-1, keepdims=True)
    spread = jnp.mean(center * center, axis=-1, keepdims=True)
    scale_rows = lax.rsqrt(spread + EPSILON)
    return center * scale_rows, scale_rows


def row_norm_back(grad_normed, normed, scale_rows, scale_gain):
    grad_hat = grad_normed * scale_gain
    return scale_rows * (
        grad_hat
        - jnp.mean(grad_hat, axis=-1, keepdims=True)
        - normed * jnp.mean(grad_hat * normed, axis=-1, keepdims=True)
    )


def shards(
    caption_token_index,
    lengths,
    slot_image_pair,
    features,
    text_table,
    latents,
    sampler_gain,
    sampler_query,
    sampler_source,
    sampler_mixer,
    norm_gain_one,
    attention_in,
    norm_gain_two,
    attention_out,
    norm_gain_three,
    feed_up,
    norm_gain_four,
    feed_down,
    cotangent,
):
    group = lax.axis_index("grp")
    place = lax.axis_index(DP_AXES)
    width = feed_down.shape[1] * DP
    hidden = feed_down.shape[0] * GRP
    own = width // DP
    local = attention_out.shape[0]
    local_ff = feed_up.shape[1]
    patches, feature_width = features.shape[1:]
    tokens = cotangent.shape[1]
    spans = caption_token_index.shape[1]
    own_rows = tokens // GRP

    quarter = patches // GRP
    place_row = jnp.reshape(group, (1,)).astype(jnp.int32)
    (first_part,) = call(
        pack_kernel,
        [((own, 7 * local + feature_width + LANES), BF)],
        [
            jnp.transpose(attention_in, (1, 0, 2)),
            attention_out.T,
            sampler_mixer.T,
            jnp.transpose(sampler_source, (1, 0, 2)),
            features[0],
            sampler_query,
            latents,
        ],
        specs={4: pl.BlockSpec((quarter, feature_width), lambda i, s: (s[0], 0))},
        scalars=(place_row,),
    )
    second_part = jnp.concatenate([feed_up, feed_down.T], axis=1)
    first_all = lax.all_gather(first_part, DP_AXES, axis=0, tiled=True)
    second_all = lax.all_gather(second_part, DP_AXES, axis=0, tiled=True)

    def first_spec(number, columns):
        return pl.BlockSpec((width, columns), lambda *_: (0, number))

    table_rows_here = text_table.shape[0]
    table_block = lax.all_to_all(text_table, "grp", 1, 0, tiled=True)
    x, y, core = coordinates()
    flat_ids = caption_token_index[0]
    numbers = jnp.stack(
        [
            (flat_ids // 256).astype(BF),
            (flat_ids % 256).astype(BF),
            sampler_gain,
            norm_gain_one,
            norm_gain_three,
            norm_gain_four,
            jnp.pad(norm_gain_two, (0, own - norm_gain_two.shape[0])),
        ]
    )
    numbers = gather_offsets(jnp.pad(numbers, ((0, 16 - numbers.shape[0]), (0, 0))))
    wide_numbers = numbers.astype(F32)
    by_offset = (wide_numbers[:, :, :, 0] * 256 + wide_numbers[:, :, :, 1]).astype(jnp.int32)
    placed = jnp.moveaxis(jnp.roll(wide_numbers[:, :, :, 2:7], (core, x, y), axis=(0, 1, 2)), 0, 2)
    gains = placed
    query_gain, gain_one, gain_three, gain_four, gain_two = (
        gains[:, :, :, i].reshape(1, width) for i in range(5)
    )
    gain_two = gain_two.reshape(DP, own)[:, : norm_gain_two.shape[0]].reshape(1, local)

    def block_rows(ids):
        span = table_rows_here * DP
        held = ids % span // table_rows_here == place
        return jnp.where(held, ids // span * table_rows_here + ids % table_rows_here, -1)

    def one_hot(ids):
        return (block_rows(ids)[:, None] == jnp.arange(GRP * table_rows_here, dtype=jnp.int32)[None]).astype(BF)

    text_places = block_rows(by_offset.reshape(1, -1))
    picked = dot(one_hot(by_offset.reshape(-1)), table_block, 1, 0).astype(BF)
    text_cols = scatter_offsets(picked.reshape(CS, XS, YS, spans, local))
    text_parts = grp_gather(text_cols)

    split_first = first_all.reshape(DP, own, first_all.shape[1])
    (pair_parts,) = call(
        pair_kernel,
        [((GRP, quarter, feature_width), BF)],
        [split_first],
        specs={0: pl.BlockSpec((1, quarter, feature_width), lambda i, s: (s[0], 0, 3))},
        scalars=(slot_image_pair,),
        after=(text_parts,),
    )
    pair_rows = swap(pair_parts).reshape(patches, feature_width)
    small_spec = first_spec(36, LANES)
    mixer_spec = first_spec(4, local)
    vector_rows = width // LANES
    latent_values, latent_hat_t, latent_scale, query_input, query_rows, vectors = call(
        query_kernel,
        [
            ((NL, width), F32),
            ((width, LANES), F32),
            ((NL, LANES), F32),
            ((NL, width), BF),
            ((NL + 16, local), F32),
            ((2 * vector_rows, LANES), F32),
        ],
        [first_all, first_all, query_gain, gain_two, first_all],
        specs={0: small_spec, 1: first_spec(8, local), 4: first_spec(3, local)},
    )
    mixed, sampled, sources, sampler_prob = call(
        sampler_kernel,
        [
            ((GRP, NL // GRP, width), F32),
            ((NL, local), BF),
            ((patches, 2 * local), BF),
            ((local // RHD, NL, patches), F32),
        ],
        [pair_rows, query_rows, split_first, split_first, first_all],
        specs={
            2: pl.BlockSpec((DP, own // 2, local), lambda *_: (0, 0, 5)),
            3: pl.BlockSpec((DP, own // 2, local), lambda *_: (0, 1, 5)),
            4: mixer_spec,
        },
    )
    latent_spec = pl.BlockSpec((NL // GRP, width), lambda i, s: (s[0], 0))
    (images,) = call(
        image_kernel,
        [((GRP, NL // GRP, width), BF)],
        [swap(mixed), latent_values],
        specs={1: latent_spec},
        scalars=(place_row,),
    )
    image_parts = swap(images)

    out_spec = first_spec(3, local)
    in_spec = first_spec(0, 3 * local)
    own_spec = pl.BlockSpec((own_rows, width), lambda i, s: (s[0], 0))
    blocks = ((GRP, own_rows, width), BF)
    wide_blocks = ((GRP, own_rows, width + LANES), BF)
    inputs, first_input, projected, prob, attended, branch_parts = call(
        attention_kernel,
        [
            ((tokens, width), BF),
            ((tokens, width), BF),
            ((tokens, 3 * local), BF),
            ((local // HD, tokens, tokens), F32),
            ((tokens, local), F32),
            ((GRP, own_rows, width + 2 * LANES), BF),
        ],
        [image_parts, text_parts, gain_one, first_all, gain_two, first_all, vectors],
        specs={3: in_spec, 5: out_spec},
        scalars=(lengths,),
    )
    middle, branch, third_input, second_numbers, gain_out = call(
        middle_kernel,
        [
            ((own_rows, width), F32),
            ((own_rows, width), F32),
            blocks,
            ((own_rows, LANES), F32),
            ((1, width), F32),
        ],
        [swap(branch_parts), inputs, gain_three],
        specs={1: own_spec},
        scalars=(place_row,),
    )

    grad_output = cotangent[0]
    hidden_block = 512
    steps = local_ff // hidden_block
    up_spec = pl.BlockSpec((width, hidden_block), lambda i: (0, i))
    down_spec = pl.BlockSpec((width, hidden_block), lambda i: (0, steps + i))
    columns_spec = pl.BlockSpec((tokens, hidden_block), lambda i: (0, i))
    row_spec = pl.BlockSpec((1, hidden_block), lambda i: (0, i))
    wide = ((tokens, local_ff), F32)
    (grad_fourth,) = call(
        grad_fourth_kernel,
        [wide],
        [grad_output, second_all],
        specs={1: down_spec},
        out_specs={0: columns_spec},
        grid=(steps,),
    )
    activated, slope, fourth_stats, third_rows = call(
        hidden_kernel,
        [wide, wide, ((STATS, tokens), F32), ((tokens, width), BF)],
        [swap(third_input), grad_fourth, gain_four, second_all],
        specs={3: up_spec},
        grid=(steps,),
    )
    fourth_stats = [fourth_stats] + [
        lax.ppermute(fourth_stats, "grp", [((i + step) % GRP, i) for i in range(GRP)]) for step in range(1, GRP)
    ]
    fourth_input, grad_up_rows, grad_gain_four, third_parts = call(
        hidden_back_kernel,
        [((tokens, local_ff), BF), ((tokens, local_ff), BF), ((1, local_ff), F32), blocks],
        [*fourth_stats, activated, slope, grad_fourth, gain_four, second_all],
        specs={4: columns_spec, 5: columns_spec, 6: columns_spec, 7: row_spec, 8: up_spec},
        out_specs={0: columns_spec, 1: columns_spec, 2: row_spec},
        grid=(steps,),
        scratch=[pltpu.VMEM((tokens, LANES), F32), pltpu.VMEM((tokens, width), F32)],
    )
    third_parts = swap(third_parts)
    outer_block = 512
    wide_columns = 2 * local_ff + 4 * local
    down_first = local_ff // outer_block
    down_grads = wide_outer([(grad_output, fourth_input)], outer_block, wide_columns, down_first)
    (down_parts,) = call(
        down_kernel,
        [blocks],
        [fourth_input, second_all],
        specs={0: columns_spec, 1: down_spec},
        grid=(steps,),
        scratch=[pltpu.VMEM((tokens, width), F32)],
    )
    grad_middle, branch_low, gain_three_grad = call(
        third_back_kernel,
        [((own_rows, width), F32), wide_blocks, ((1, width), F32)],
        [third_parts, middle, branch, grad_output, gain_three, gain_out, second_numbers],
        specs={3: own_spec},
        scalars=(place_row,),
        after=(down_grads,),
    )

    ff_grads = wide_outer([(third_rows, grad_up_rows)], outer_block, wide_columns, 0, down_grads)

    grad_branch, second_input, grad_projected, grad_gain_two, first_parts = call(
        attention_back_kernel,
        [
            ((tokens, width), BF),
            ((tokens, local), BF),
            ((tokens, 3 * local), BF),
            ((1, local), F32),
            blocks,
        ],
        [swap(branch_low), attended, projected, prob, gain_two, first_all, first_all],
        specs={5: out_spec, 6: in_spec},
        after=(ff_grads,),
    )
    layer_grads = wide_outer(
        [(first_input, grad_projected), (grad_branch, second_input)],
        outer_block,
        wide_columns,
        2 * local_ff // outer_block,
        ff_grads,
    )
    layer_sums = lax.psum_scatter(layer_grads, DP_AXES, scatter_dimension=0, tiled=True)
    (input_low,) = call(
        first_back_kernel,
        [wide_blocks],
        [swap(first_parts), inputs, gain_one, grad_middle, gain_three_grad],
        specs={1: own_spec},
        after=(down_parts,),
        scalars=(place_row,),
        scratch=[pltpu.VMEM((2 * vector_rows, LANES), F32)],
    )
    input_low = swap(input_low)

    per_own = norm_gain_two.shape[0]
    gain_two_row = jnp.pad(grad_gain_two.reshape(DP, per_own), ((0, 0), (0, own - per_own))).reshape(1, width)
    image_low, grad_keys, grad_values, grad_query, extra = call(
        sampler_back_kernel,
        [((NL, width), BF), ((patches, local), BF), ((patches, local), BF), ((NL, local), BF), ((width, 2 * LANES), F32)],
        [input_low, first_all, query_rows, sources, sampler_prob, first_all, grad_gain_four, gain_two_row],
        specs={1: mixer_spec, 5: first_spec(8, local)},
        scratch=[pltpu.VMEM((2 * LANES, width), F32)],
    )

    paths = (
        [(image_low, sampled), (extra,)],
        [(query_input, grad_query), (pair_rows, grad_keys, grad_values)],
    )
    arrived = fetch(outer_blocks(paths, 256), 0, 0, 1)

    (text_low,) = call(
        text_kernel,
        [((spans, local), BF)],
        [input_low],
        specs={0: pl.BlockSpec((2, own_rows, local), lambda i, s: (1, 0, s[0]))},
        scalars=(place_row,),
    )
    text_parts = ring(text_low, 1)
    first_held, last_held = outer_blocks(paths, 256, arrived, text_parts[1:])
    (text_column,) = call(stack_kernel, [((YS, spans, local), BF)], text_parts, after=first_held[:1])
    text_parts = ring(text_column, 0)
    (output_rows,) = call(
        output_kernel, [blocks], [swap(down_parts), middle], after=first_held[:1]
    )
    first_moved, last_moved = both_ways(first_held, last_held)
    (text_same,) = call(
        stack_kernel, [((XS, YS, spans, local), BF)], text_parts, after=(*first_moved[1:], *last_moved[1:], output_rows)
    )
    moved, first_block = sum_over_rings(first_moved, last_moved, ())
    (table_sums,) = call(
        table_kernel,
        [((GRP * table_rows_here, local), BF)],
        [text_places, text_same, fetch(text_same, 0, 0, 1)],
        after=(first_block,),
    )
    table_rows = lax.all_to_all(table_sums, "grp", 0, 1, tiled=True)
    table_grad = table_rows.astype(F32)

    layer_output, input_grad = call(
        widen_kernel, [((tokens, width), F32)] * 2, [swap(output_rows), input_low]
    )
    mixer_grad, query_grad, source_grad, numbers, shared, gain_grads = last_sums(moved, (table_sums,))

    up_grad, down_grad, in_grad, out_grad = call(
        layer_sum_kernel,
        [((own, local_ff), F32), ((own, local_ff), F32), ((3, own, local), F32), ((own, local), F32)],
        [layer_sums],
    )
    latents_grad, sampler_gain_grad = call(
        latent_kernel,
        [((NL, own), F32), ((1, own), F32)],
        [swap(shared), numbers, latent_hat_t, latent_scale, sampler_gain.astype(F32)[None]],
        specs={2: pl.BlockSpec((own, LANES), lambda i, s: (s[0], 0))},
        after=(table_rows, out_grad),
        scalars=(jnp.reshape(place, (1,)).astype(jnp.int32),),
    )
    return (
        layer_output[None],
        input_grad[None],
        table_grad,
        latents_grad,
        sampler_gain_grad[0],
        query_grad,
        jnp.transpose(source_grad, (1, 0, 2)),
        mixer_grad.T,
        gain_grads[0],
        jnp.transpose(in_grad, (1, 0, 2)),
        gain_grads[3, :per_own],
        out_grad.T,
        gain_grads[1],
        up_grad,
        gain_grads[2],
        down_grad.T,
    )


def solution(mesh):
    mesh = Mesh(mesh.devices.reshape(GRP, XS, YS, CS), ("grp",) + DP_AXES)
    return jax.shard_map(
        shards,
        mesh=mesh,
        in_specs=(
            P(DP_AXES, None),
            P(DP_AXES),
            P(DP_AXES),
            P(DP_AXES, None, None),
            P(("grp",) + DP_AXES, None),
            P(None, DP_AXES),
            P(DP_AXES),
            P(DP_AXES, "grp"),
            P(DP_AXES, None, "grp"),
            P("grp", DP_AXES),
            P(DP_AXES),
            P(DP_AXES, None, "grp"),
            P(("grp",) + DP_AXES),
            P("grp", DP_AXES),
            P(DP_AXES),
            P(DP_AXES, "grp"),
            P(("grp",) + DP_AXES),
            P("grp", DP_AXES),
            P(DP_AXES, None, None),
        ),
        out_specs=(
            P(DP_AXES, None, None),
            P(DP_AXES, None, None),
            P(("grp",) + DP_AXES, None),
            P(None, DP_AXES),
            P(DP_AXES),
            P(DP_AXES, "grp"),
            P(DP_AXES, None, "grp"),
            P("grp", DP_AXES),
            P(DP_AXES),
            P(DP_AXES, None, "grp"),
            P(("grp",) + DP_AXES),
            P("grp", DP_AXES),
            P(DP_AXES),
            P(DP_AXES, "grp"),
            P(("grp",) + DP_AXES),
            P("grp", DP_AXES),
        ),
        check_vma=False,
    )
```

```python
from functools import partial

import jax
import jax.numpy as jnp
from jax import lax
from jax.experimental import pallas as pl
from jax.experimental.pallas import tpu as pltpu
from jax.sharding import Mesh, PartitionSpec as P

HD = 64
RHD = 128
NL = 64
EPSILON = 1e-05
NEG_FILL = -1e30
GRP = 4
XS = 4
YS = 4
CS = 2
DP = XS * YS * CS
DP_AXES = ("x", "y", "core")
LANES = 128
STATS = 8
KEPT = (4, 4, 2, 2, 4)
VMEM_LIMIT = 56 * 1024 * 1024
BF = jnp.bfloat16
F32 = jnp.float32


def dot(left, right, left_dims, right_dims):
    return lax.dot_general(
        left, right, (((left_dims,), (right_dims,)), ((), ())), preferred_element_type=F32
    )


def fetch(values, step_x, step_y, step_core):
    pairs = []
    for x in range(XS):
        for y in range(YS):
            for core in range(CS):
                source = (((x + step_x) % XS) * YS + (y + step_y) % YS) * CS + (core ^ step_core)
                pairs.append((source, (x * YS + y) * CS + core))
    return lax.ppermute(values, DP_AXES, pairs)


def coordinates():
    place = lax.axis_index(DP_AXES)
    return place // (YS * CS), place // CS % YS, place % CS


def ring(values, axis):
    steps = [(step, 0) if axis == 0 else (0, step) for step in range(4)]
    return [values] + [fetch(values, *step, 0) for step in steps[1:]]


def gather_offsets(values):
    over_y = jnp.stack(ring(values, 1))
    over_x = jnp.stack(ring(over_y, 0))
    return jnp.stack([over_x, fetch(over_x, 0, 0, 1)])


def dp_total(values):
    values = values + fetch(values, 0, 0, 1)
    for axis in (0, 1):
        parts = ring(values, axis)
        values = (parts[0] + parts[2]) + (parts[1] + parts[3])
    return values


def scatter_offsets(values):
    values = values[0] + fetch(values[1], 0, 0, 1)
    values = values[0] + sum(fetch(values[step], -step, 0, 0) for step in range(1, XS))
    return values[0] + sum(fetch(values[step], 0, -step, 0) for step in range(1, YS))


def call(
    body, outs, operands, specs=None, out_specs=None, grid=(1,), scalars=(), scratch=(), after=(), aliases=None
):
    specs = dict(specs or {})
    out_specs = dict(out_specs or {})

    def whole(shape):
        return pl.BlockSpec(shape, lambda *_: (0,) * len(shape))

    def wrapped(*refs):
        held = len(scalars) + len(operands)
        body(*refs[:held], *refs[held + len(after) :])

    in_specs = [specs.get(i, whole(operand.shape)) for i, operand in enumerate(operands)]
    in_specs += [pl.BlockSpec(memory_space=pl.ANY)] * len(after)
    return pl.pallas_call(
        wrapped,
        grid_spec=pltpu.PrefetchScalarGridSpec(
            num_scalar_prefetch=len(scalars),
            grid=grid,
            in_specs=in_specs,
            out_specs=[out_specs.get(i, whole(shape)) for i, (shape, _) in enumerate(outs)],
            scratch_shapes=list(scratch),
        ),
        out_shape=[jax.ShapeDtypeStruct(shape, dtype) for shape, dtype in outs],
        input_output_aliases={len(scalars) + i: out for i, out in (aliases or {}).items()},
        compiler_params=pltpu.CompilerParams(vmem_limit_bytes=VMEM_LIMIT),
    )(*scalars, *operands, *after)


def pack_kernel(place, projections, out_t, mixer_t, sources, features, query, latents, packed):
    local = query.shape[1]
    half = sources.shape[1]
    for i in range(3):
        packed[:, i * local : (i + 1) * local] = projections[i]
    packed[:, 3 * local : 4 * local] = out_t[...]
    packed[:, 4 * local : 5 * local] = mixer_t[...]
    for i in range(2):
        packed[i * half : (i + 1) * half, 5 * local : 6 * local] = sources[i]
    packed[:, 6 * local : 8 * local] = features[...]
    packed[:, 8 * local : 9 * local] = query[...]
    rows = jnp.concatenate([latents[...].astype(F32), jnp.zeros((NL, LANES - NL), F32)], axis=1)
    across = jnp.transpose(jnp.concatenate([rows, jnp.zeros((LANES - NL, LANES), F32)], axis=0))
    packed[:, 9 * local :] = across[:NL].astype(BF)


def pair_kernel(pair, features, spread):
    for device in range(GRP):
        spread[device] = features[0]


def query_kernel(
    small, query_weight, query_gain, gain_two, out_t,
    latents, latent_hat, latent_scale, query_input, query_rows, vectors,
):
    values = jnp.transpose(small[...].astype(F32))[:NL]
    latents[...] = values
    hat, scale = row_norm(values)
    latent_hat[...] = jnp.transpose(jnp.concatenate([hat, jnp.zeros_like(hat)], axis=0))
    latent_scale[...] = jnp.broadcast_to(scale, latent_scale.shape)
    gain = query_gain[...]
    normed = (hat * gain).astype(BF)
    query_input[...] = normed
    query_rows[:NL, :] = jnp.dot(normed, query_weight[...], preferred_element_type=F32)
    query_rows[NL:, :] = jnp.dot(
        jnp.broadcast_to(gain, (16, gain.shape[1])).astype(BF), query_weight[...], preferred_element_type=F32
    )
    gains = jnp.broadcast_to(gain_two[...], (16, gain_two.shape[1])).astype(BF)
    products = dot(gains, out_t[...], 1, 1)[:1]
    for number, vector in enumerate(in_pairs([products])):
        put_vector(vectors, number * (vector.shape[1] // LANES), vector)


def sampler_kernel(pair, query_rows, key_weight, value_weight, mixer, mixed, sampled, sources, prob):
    width = query_rows.shape[1]
    query = query_rows[:NL, :].astype(BF)
    rows = pair[...]
    keys, values = (
        jnp.dot(rows, weight[...].reshape(rows.shape[1], width), preferred_element_type=F32).astype(BF)
        for weight in (key_weight, value_weight)
    )
    sources[:, :width] = keys
    sources[:, width:] = values
    for head in range(width // RHD):
        columns = slice(head * RHD, (head + 1) * RHD)
        scores = dot(query[:, columns], keys[:, columns], 1, 1) * RHD ** (-0.5)
        exponent = jnp.exp(scores - jnp.max(scores, axis=-1, keepdims=True))
        weights = exponent / jnp.sum(exponent, axis=-1, keepdims=True)
        prob[head] = weights
        sampled[:, columns] = jnp.dot(
            weights.astype(BF), values[:, columns], preferred_element_type=F32
        ).astype(BF)
    mixed[...] = dot(sampled[...], mixer[...], 1, 1).reshape(mixed.shape)


def image_kernel(place, parts, latents, images):
    mixed = (parts[0] + parts[1]) + (parts[2] + parts[3])
    rows = (latents[...] + mixed).astype(BF)
    for device in range(GRP):
        images[device] = rows


def lanes_of(numbers, dtype):
    rows = numbers[0].shape[0]
    lane = lax.broadcasted_iota(jnp.int32, (rows, LANES), 1)
    held = jnp.zeros((rows, LANES), F32)
    for number, column in enumerate(numbers):
        held = jnp.where(lane == number, column, held)
    return held.astype(dtype)


def in_pairs(numbers):
    pairs = []
    for number in numbers:
        high = number.astype(BF).astype(F32)
        pairs += [high, number - high]
    return pairs


def from_pairs(lanes, number):
    wide = lanes.astype(F32)
    return wide[:, 2 * number : 2 * number + 1] + wide[:, 2 * number + 1 : 2 * number + 2]


def put_rows(columns):
    tokens = columns[0].shape[0]
    lane = lax.broadcasted_iota(jnp.int32, (tokens, tokens), 1)
    held = jnp.zeros((tokens, tokens), F32)
    for number, column in enumerate(columns):
        held = jnp.where(lane == number, column, held)
    return jnp.transpose(held)[:STATS]


def take_columns(stats):
    return jnp.transpose(jnp.concatenate([rows[...] for rows in stats], axis=0))


def put_vector(small, first, vector):
    for i in range(vector.shape[1] // LANES):
        small[first + i : first + i + 1, :] = vector[:, i * LANES : (i + 1) * LANES]


def attention_kernel(
    length, image, text, gain_one, in_weight, gain_two, out_t, vectors,
    inputs, first_input, projected, prob, attended, parts,
):
    images = NL
    inputs[:images, :] = image[...].reshape(images, inputs.shape[1])
    local = gain_two.shape[1]
    for device in range(GRP):
        inputs[images:, device * local : (device + 1) * local] = text[device]
    hat, _ = row_norm(inputs[...].astype(F32))
    first_input[...] = (hat * gain_one[...]).astype(BF)
    projected[...] = dot(first_input[...], in_weight[...], 1, 0).astype(BF)
    tokens = inputs.shape[0]
    query = lax.broadcasted_iota(jnp.int32, (tokens, tokens), 0)
    key = lax.broadcasted_iota(jnp.int32, (tokens, tokens), 1)
    allowed = (key <= query) & (key < NL + length[0])
    for head in range(local // HD):
        query_head, key_head, value_head = (
            projected[:, i * local + head * HD : i * local + (head + 1) * HD] for i in range(3)
        )
        scores = jnp.where(allowed, dot(query_head, key_head, 1, 1) * HD ** (-0.5), NEG_FILL)
        exponent = jnp.exp(scores - jnp.max(scores, axis=-1, keepdims=True))
        weights = exponent / jnp.sum(exponent, axis=-1, keepdims=True)
        prob[head] = weights
        attended[:, head * HD : (head + 1) * HD] = jnp.dot(
            weights.astype(BF), value_head, preferred_element_type=F32
        )
    values = attended[...]
    mean = jnp.mean(values, axis=-1, keepdims=True)
    center = values - mean
    square = jnp.sum(center * center, axis=-1, keepdims=True)
    gains = gain_two[...]
    width = inputs.shape[1]
    blocks = dot((center * gains).astype(BF), out_t[...], 1, 1).astype(BF)
    parts[:, :, :width] = blocks.reshape(GRP, tokens // GRP, width)
    numbers = lanes_of(in_pairs([mean, square]), BF)
    parts[:, :, width : width + LANES] = numbers.reshape(GRP, tokens // GRP, LANES)
    for device in range(GRP):
        parts[device, :, width + LANES :] = vectors[...].astype(BF)


def joined_stats(means, squares, own, full):
    mean = ((means[0] + means[1]) + (means[2] + means[3])) / GRP
    shifts = [part - mean for part in means]
    square = sum(squares[i] + own * shifts[i] * shifts[i] for i in range(GRP))
    return mean, lax.rsqrt(square / full + EPSILON), shifts


def middle_kernel(place, parts, inputs, gain_three, middle, branch, third_input, numbers, gain_out):
    own_rows, width = inputs.shape
    count = width // LANES
    lanes = [parts[i, :, width : width + LANES] for i in range(GRP)]
    mean, scale, shifts = joined_stats(
        [from_pairs(lane, 0) for lane in lanes], [from_pairs(lane, 1) for lane in lanes], width // GRP, width
    )
    vectors = []
    for device in range(GRP):
        pairs = parts[device, :, width + LANES :].astype(F32)
        rows = pairs[:count] + pairs[count:]
        vectors.append(jnp.concatenate([rows[i : i + 1] for i in range(count)], axis=1))
    gain_out[...] = (vectors[0] + vectors[1]) + (vectors[2] + vectors[3])
    gathered = sum(parts[i, :, :width].astype(F32) + shifts[i] * vectors[i] for i in range(GRP))
    added = scale * gathered
    branch[...] = added
    rows = inputs[...].astype(F32) + added
    middle[...] = rows
    numbers[...] = lanes_of([mean, scale], F32)
    hat, _ = row_norm(rows)
    low = (hat * gain_three[...]).astype(BF)
    for device in range(GRP):
        third_input[device] = low


def grad_fourth_kernel(cotangent, down_t, grad_fourth):
    grad_fourth[...] = dot(cotangent[...], down_t[...], 1, 0)


def hidden_kernel(third_input, grad_fourth, gain_four, up_weight, activated, slope, stats, third_rows):
    step = pl.program_id(0)
    block = up_weight.shape[1]
    rows = third_input[...].reshape(third_rows.shape)
    columns = pl.ds(step * block, block)
    values = dot(rows, up_weight[...], 1, 0)
    normal = 0.5 * (1.0 + lax.erf(values * (0.5**0.5)))
    activated[:, columns] = values * normal
    slope[:, columns] = normal + values * jnp.exp(-0.5 * values * values) * 0.3989422804014327

    @pl.when(step == pl.num_programs(0) - 1)
    def _():
        third_rows[...] = rows
        active = activated[...]
        grad_hat = grad_fourth[...] * gain_four[...]
        mean = jnp.mean(active, axis=-1, keepdims=True)
        center = active - mean
        stats[...] = put_rows(
            [
                mean,
                jnp.sum(center * center, axis=-1, keepdims=True),
                jnp.sum(grad_hat, axis=-1, keepdims=True),
                jnp.sum(grad_hat * center, axis=-1, keepdims=True),
            ]
        )


def hidden_back_kernel(
    first_stats, second_stats, third_stats, fourth_stats, activated, slope, grad_fourth, gain_four, up_weight,
    fourth_input, grad_up, grad_gain, parts, held, summed,
):
    step = pl.program_id(0)
    block = up_weight.shape[1]
    own = block * pl.num_programs(0)
    full = own * GRP

    @pl.when(step == 0)
    def _():
        columns = take_columns([first_stats, second_stats, third_stats, fourth_stats])
        means, squares = ([columns[:, STATS * i + n : STATS * i + n + 1] for i in range(GRP)] for n in (0, 1))
        mean, scale, shifts = joined_stats(means, squares, own, full)
        sums = [columns[:, STATS * i + 2 : STATS * i + 3] for i in range(GRP)]
        crosses = [columns[:, STATS * i + 3 : STATS * i + 4] + shifts[i] * sums[i] for i in range(GRP)]
        lane = lax.broadcasted_iota(jnp.int32, held.shape, 1)
        numbers = [
            mean,
            scale,
            ((sums[0] + sums[1]) + (sums[2] + sums[3])) / full,
            scale * ((crosses[0] + crosses[1]) + (crosses[2] + crosses[3])) / full,
        ]
        kept = jnp.zeros(held.shape, F32)
        for number, column in enumerate(numbers):
            kept = jnp.where(lane == number, column, kept)
        held[...] = kept
        summed[...] = jnp.zeros_like(summed)

    mean, scale, sum_grad, sum_cross = (held[:, i : i + 1] for i in range(4))
    gains = gain_four[...]
    hat = (activated[...] - mean) * scale
    fourth_input[...] = (hat * gains).astype(BF)
    grads = grad_fourth[...]
    grad_gain[...] = jnp.sum(grads * hat, axis=0, keepdims=True)
    low = (scale * (grads * gains - sum_grad - hat * sum_cross) * slope[...]).astype(BF)
    grad_up[...] = low
    summed[...] += dot(low, up_weight[...], 1, 1)

    @pl.when(step == pl.num_programs(0) - 1)
    def _():
        parts[...] = summed[...].astype(BF).reshape(parts.shape)


def down_kernel(fourth_input, down_t, parts, summed):
    step = pl.program_id(0)

    @pl.when(step == 0)
    def _():
        summed[...] = jnp.zeros_like(summed)

    summed[...] += dot(fourth_input[...], down_t[...], 1, 1)

    @pl.when(step == pl.num_programs(0) - 1)
    def _():
        parts[...] = summed[...].astype(BF).reshape(parts.shape)


def output_kernel(parts, middle, rows):
    total_rows = (parts[0].astype(F32) + parts[1].astype(F32)) + (parts[2].astype(F32) + parts[3].astype(F32))
    low = (middle[...] + total_rows).astype(BF)
    for device in range(GRP):
        rows[device] = low


def widen_kernel(output_rows, grad_rows, layer_output, input_grad):
    width = layer_output.shape[1]
    layer_output[...] = output_rows[...].astype(F32).reshape(layer_output.shape)
    input_grad[...] = grad_rows[:, :, :width].astype(F32).reshape(input_grad.shape)


def stack_kernel(*refs):
    for number, part in enumerate(refs[:-1]):
        refs[-1][number] = part[...]


def table_kernel(places, same, other, out):
    count, width = out.shape
    total_rows = jnp.zeros((count, width), F32)
    at = 0
    for rows in (same, other):
        held = rows[...].reshape(-1, width)
        ids = places[:, at : at + held.shape[0]]
        row = lax.broadcasted_iota(jnp.int32, (count, held.shape[0]), 0)
        chosen = jnp.where(row == ids, 1.0, 0.0).astype(BF)
        total_rows = total_rows + jnp.dot(chosen, held, preferred_element_type=F32)
        at += held.shape[0]
    out[...] = total_rows.astype(BF)


def text_kernel(place, rows, text):
    text[...] = rows[...].reshape(text.shape)


def third_back_kernel(
    place, parts, middle, branch, cotangent, gain_three, gain_out, numbers, grad_middle, low, gain_grad
):
    width = middle.shape[1]
    grads = (parts[0].astype(F32) + parts[1].astype(F32)) + (parts[2].astype(F32) + parts[3].astype(F32))
    hat, scale = row_norm(middle[...])
    total_rows = cotangent[...].astype(F32) + row_norm_back(grads, hat, scale, gain_three[...])
    grad_middle[...] = total_rows
    rounded = total_rows.astype(BF)
    wide = rounded.astype(F32)
    sum_grad = jnp.sum(wide * gain_out[...], axis=-1, keepdims=True) / width
    sum_cross = jnp.sum(wide * branch[...], axis=-1, keepdims=True) / width
    lanes = lanes_of(in_pairs([numbers[:, 0:1], numbers[:, 1:2], sum_grad, sum_cross]), BF)
    gain_grad[...] = jnp.sum(grads * hat, axis=0, keepdims=True)
    for device in range(GRP):
        low[device, :, :width] = rounded
        low[device, :, width:] = lanes


def attention_back_kernel(
    grad_rows, attended, projected, prob, gain_two, out_t, in_weight,
    grad_branch, second_input, grad_projected, grad_gain_two, parts,
):
    tokens, local = attended.shape
    width = grad_branch.shape[1]
    grad_branch[...] = grad_rows[:, :, :width].reshape(tokens, width)
    lanes = grad_rows[:, :, width:].reshape(tokens, LANES)
    mean, scale, sum_grad, sum_cross = (from_pairs(lanes, i) for i in range(4))
    hat = (attended[...] - mean) * scale
    gains = gain_two[...]
    second_input[...] = (hat * gains).astype(BF)
    grad_second = dot(grad_branch[...], out_t[...], 1, 0)
    grad_gain_two[...] = jnp.sum(grad_second * hat, axis=0, keepdims=True)
    grad_attended = (scale * (grad_second * gains - sum_grad - hat * sum_cross)).astype(BF)
    for head in range(local // HD):
        columns = [slice(i * local + head * HD, i * local + (head + 1) * HD) for i in range(3)]
        query_head, key_head, value_head = (projected[:, column] for column in columns)
        grad_head = grad_attended[:, head * HD : (head + 1) * HD]
        weights = prob[head]
        grad_weights = dot(grad_head, value_head, 1, 1)
        grad_scores = weights * (
            grad_weights - jnp.sum(weights * grad_weights, axis=-1, keepdims=True)
        )
        grad_scores = grad_scores.astype(BF)
        factor = HD ** (-0.5)
        grad_projected[:, columns[0]] = (dot(grad_scores, key_head, 1, 0) * factor).astype(BF)
        grad_projected[:, columns[1]] = (dot(grad_scores, query_head, 0, 0) * factor).astype(BF)
        grad_projected[:, columns[2]] = dot(weights.astype(BF), grad_head, 0, 0).astype(BF)
    parts[...] = dot(grad_projected[...], in_weight[...], 1, 1).astype(BF).reshape(parts.shape)


def first_back_kernel(
    place, parts, inputs, gain_one, grad_middle, gain_three_grad, low, gain_grads
):
    grads = (parts[0].astype(F32) + parts[1].astype(F32)) + (parts[2].astype(F32) + parts[3].astype(F32))
    hat, scale = row_norm(inputs[...].astype(F32))
    rows = grad_middle[...] + row_norm_back(grads, hat, scale, gain_one[...])
    rounded = rows.astype(BF)
    gain_grad = jnp.sum(grads * hat, axis=0, keepdims=True)
    width = gain_grad.shape[1]
    put_vector(gain_grads, 0, gain_grad)
    put_vector(gain_grads, width // LANES, gain_three_grad[...])
    for device in range(GRP):
        low[device, :, :width] = rounded
        low[device, :, width:] = gain_grads[...].astype(BF)


def sampler_back_kernel(
    grad_rows, mixer, query_rows, sources, prob, query_weight, gain_four_grad, gain_two_grad,
    grad_image, grad_keys, grad_values, grad_query, extra, across,
):
    width = query_rows.shape[1]
    full = grad_image.shape[1]
    query = query_rows[:NL, :].astype(BF)
    grad_image[...] = grad_rows[:2, :, :full].reshape(grad_image.shape)
    grad_sampled = dot(grad_image[...], mixer[...], 1, 0).astype(BF)
    for head in range(width // RHD):
        columns = slice(head * RHD, (head + 1) * RHD)
        value_columns = slice(width + head * RHD, width + (head + 1) * RHD)
        keys, values = sources[:, columns], sources[:, value_columns]
        grad_head = grad_sampled[:, columns]
        weights = prob[head]
        grad_weights = dot(grad_head, values, 1, 1)
        grad_scores = weights * (
            grad_weights - jnp.sum(weights * grad_weights, axis=-1, keepdims=True)
        )
        grad_scores = grad_scores.astype(BF)
        factor = RHD ** (-0.5)
        grad_query[:, columns] = (dot(grad_scores, keys, 1, 0) * factor).astype(BF)
        grad_keys[:, columns] = (dot(grad_scores, query[:, columns], 0, 0) * factor).astype(BF)
        grad_values[:, columns] = dot(weights.astype(BF), grad_head, 0, 0).astype(BF)
    low = grad_query[...]
    wide = low.astype(F32)
    sums = [
        jnp.sum(wide * query_rows[NL : NL + 1, :], axis=-1, keepdims=True),
        jnp.sum(wide * query_rows[:NL, :], axis=-1, keepdims=True),
    ]
    across[...] = jnp.zeros_like(across)
    across[:NL, :] = grad_image[...].astype(F32)
    across[NL : 2 * NL, :] = dot(low, query_weight[...], 1, 1)
    lanes = [grad_rows[i, :, full:].astype(F32) for i in range(GRP)]
    lanes = (lanes[0] + lanes[1]) + (lanes[2] + lanes[3])
    count = full // LANES
    for number in range(2):
        vector = [lanes[number * count + i : number * count + i + 1, :] for i in range(count)]
        across[LANES + number : LANES + number + 1, :] = jnp.concatenate(vector, axis=1)
    across[LANES + 2 : LANES + 3, :] = gain_four_grad[...]
    across[LANES + 3 : LANES + 4, :] = gain_two_grad[...]
    held = jnp.transpose(across[...])
    lane = lax.broadcasted_iota(jnp.int32, held.shape, 1)
    for number, column in enumerate(sums):
        held = jnp.where(lane == LANES + 4 + number, jnp.concatenate([column] * DP, axis=0), held)
    extra[...] = held


def turn(left, turned):
    tokens, columns = left.shape
    for at in range(0, columns, LANES):
        block = left[:, at : at + LANES].astype(F32)
        turned[at : at + LANES, :tokens] = jnp.transpose(block).astype(BF)


def wide_outer_kernel(count, *refs):
    step = pl.program_id(0)
    out, turned = refs[-2:]
    start = 0
    for piece in range(len(count)):
        left, right = refs[2 * piece], refs[2 * piece + 1]

        @pl.when(step == start)
        def _():
            turn(left, turned)

        @pl.when((step >= start) & (step < start + count[piece]))
        def _():
            out[...] = jnp.dot(turned[...], right[...], preferred_element_type=F32).astype(BF)

        start += count[piece]


def wide_outer(pieces, block, full, first, held=None):
    count, operands, specs, at = [], [], {}, 0
    for left, right in pieces:
        count.append(right.shape[1] // block)
        specs[len(operands) + 1] = pl.BlockSpec(
            (right.shape[0], block), lambda i, at=at, n=count[-1]: (0, jnp.clip(i - at, 0, n - 1))
        )
        operands += [left, right]
        at += count[-1]
    tokens, width = pieces[0][0].shape
    aliases = None
    if held is not None:
        specs[len(operands)] = pl.BlockSpec(memory_space=pl.ANY)
        aliases = {len(operands): 0}
        operands.append(held)

    def body(*refs):
        wide_outer_kernel(count, *refs[: 2 * len(pieces)], *refs[-2:])

    (out,) = call(
        body,
        [((width, full), BF)],
        operands,
        specs=specs,
        out_specs={0: pl.BlockSpec((width, block), lambda i: (0, first + i))},
        grid=(at,),
        scratch=[pltpu.VMEM((width, tokens), BF)],
        aliases=aliases,
    )
    return out


def outer_kernel(keep, kinds, places, *refs):
    step = pl.program_id(0)
    core, x, y = places[0], places[1], places[2]
    turned, chosen = refs[-2:]
    refs = list(refs[:-2])
    outs = [refs.pop() for _ in range(2 * len(KEPT) if keep else 1)][::-1]
    arrived = refs.pop() if keep else None
    side = core if keep else 1 - core

    def row_of(spot, rows, path):
        first, second = spot // 4, spot % 4
        off_x, off_y = (first, second) if path == 0 or not keep else (second, first)
        chip = (x + off_x) % XS * YS + (y + off_y) % YS
        return pl.multiple_of((2 * chip + side) * rows, rows)

    def put(path, first, rows, blocks):
        if not keep:
            outs[0][:, first : first + rows] = blocks.astype(BF)
            return
        at = 0
        for out in outs[path * len(KEPT) : (path + 1) * len(KEPT)]:
            for number in range(out.shape[0]):
                spot = at + number
                sent = spot if path == 0 else spot % 4 * 4 + spot // 4
                total_block = blocks[spot] + arrived[sent, first : first + rows].astype(F32)
                out[number, first : first + rows] = total_block.astype(BF)
            at += out.shape[0]

    for start, count, kind, path in kinds:
        used = [refs.pop(0) for _ in range({"plain": 1, "product": 2, "stacked": 3}[kind])]
        if kind == "plain":

            @pl.when((step >= start) & (step < start + count))
            def _():
                rows = used[0].shape[0] // DP
                blocks = [used[0][pl.ds(row_of(i, rows, path), rows), :] for i in range(XS * YS)]
                put(path, 0, rows, jnp.stack(blocks))

            continue
        tokens, rows = used[0].shape[0], used[0].shape[1] // DP
        half = XS * YS * rows

        @pl.when(step == start)
        def _():
            turn(used[0], turned)
            for spot in range(XS * YS):
                chosen[spot * rows : (spot + 1) * rows, :tokens] = turned[
                    pl.ds(row_of(spot, rows, path), rows), :tokens
                ]

        @pl.when((step >= start) & (step < start + count))
        def _():
            for number, right in enumerate(used[1:]):
                product = jnp.dot(chosen[:half, :tokens], right[...], preferred_element_type=F32)
                put(path, number * rows, rows, product.reshape(XS * YS, rows, product.shape[1]))


def outer_blocks(paths, block, arrived=None, after=()):
    x, y, core = coordinates()
    places = jnp.stack([core, x, y]).astype(jnp.int32)
    kinds, operands, specs, ends, at = [], [], {}, [], 0
    for path, pieces in enumerate(paths):
        for piece in pieces:
            kind = ("plain", "product", "stacked")[len(piece) - 1]
            count = piece[-1].shape[1] // block
            kinds.append((at, count, kind, path))
            for number, operand in enumerate(piece):
                if kind == "plain" or number > 0:
                    specs[len(operands)] = pl.BlockSpec(
                        (operand.shape[0], block), lambda i, s, at=at, n=count: (0, jnp.clip(i - at, 0, n - 1))
                    )
                operands.append(operand)
            at += count
        ends.append(at)
    width = paths[0][0][0].shape[1]
    rows = width // DP
    keep = arrived is not None
    if keep:
        specs[len(operands)] = pl.BlockSpec((XS * YS, rows, block), lambda i, s: (0, 0, i))
        operands.append(arrived)
        outs, out_specs = [], {}
        for first, end in ((0, ends[0]), (ends[0], ends[1])):
            for count in KEPT:
                out_specs[len(outs)] = pl.BlockSpec(
                    (count, rows, block), lambda i, s, first=first, end=end: (0, 0, jnp.clip(i, first, end - 1) - first)
                )
                outs.append(((count, rows, (end - first) * block), BF))
    else:
        outs = [((XS * YS, rows, at * block), BF)]
        out_specs = {0: pl.BlockSpec((XS * YS, rows, block), lambda i, s: (0, 0, i))}
    outs = call(
        partial(outer_kernel, keep, kinds),
        outs,
        operands,
        specs=specs,
        out_specs=out_specs,
        grid=(at,),
        scalars=(places,),
        scratch=[pltpu.VMEM((width, 2 * LANES), BF), pltpu.VMEM((width // 2, 2 * LANES), BF)],
        after=after,
    )
    return (outs[: len(KEPT)], outs[len(KEPT) :]) if keep else outs[0]


def step_along(values, along_x, step):
    return fetch(values, step if along_x else 0, 0 if along_x else step, 0)


def half_kernel(*refs):
    for number in range(4):
        arrived, held, out = refs[number], refs[4 + number], refs[8 + number]
        out[...] = (held[...].astype(F32) + arrived[...].astype(F32)).astype(BF)


def both_ways(first_held, last_held):
    arrived, sides, shapes = [], [], []
    for along_x, (_, right, far_right, far_left, left) in ((True, first_held), (False, last_held)):
        arrived += [step_along(far_right, along_x, -1), step_along(far_left, along_x, 1)]
        sides += [right, left]
        shapes += [right.shape] * 2
    specs = [
        pl.BlockSpec((2,) + shape[1:], lambda *_, first=number % 2: (first, 0, 0))
        for number, shape in enumerate(shapes)
    ]
    sides = call(
        half_kernel,
        [(shape, BF) for shape in shapes],
        arrived + sides,
        specs={4 + number: spec for number, spec in enumerate(specs)},
        out_specs=dict(enumerate(specs)),
        aliases={4 + number: number for number in range(4)},
    )
    moved = []
    for along_x, held, (right, left) in ((True, first_held, sides[:2]), (False, last_held, sides[2:])):
        moved.append([held[0], step_along(right, along_x, -1), step_along(left, along_x, 1)])
    return moved


def ring_moves(held, along_x):
    return [held[0]] + [step_along(held[step], along_x, -step) for step in range(1, 4)]


def sum_kernel(*refs):
    for parts, outs in ((refs[:3], refs[6:10]), (refs[3:6], refs[10:])):
        for number in range(4):
            first, second, third = (part[number].astype(F32) for part in parts)
            outs[number][...] = (first + (second + third)).astype(BF)


def last_sum_kernel(*refs):
    mixer_grad, query_grad, source_grad, numbers, spread, gain_grads = refs[8:]
    sums = []
    for parts in (refs[:4], refs[4:8]):
        first, second, third, fourth = (part[...].astype(F32) for part in parts)
        sums.append((first + second) + (third + fourth))
    local = mixer_grad.shape[1]
    mixer_grad[...] = sums[0][:, :local]
    held = sums[0][:, local:]
    numbers[...] = held
    across = jnp.transpose(jnp.concatenate([held, jnp.zeros_like(held)], axis=0))
    gain_grads[...] = across[LANES : LANES + 8, : held.shape[0]]
    lane = lax.broadcasted_iota(jnp.int32, (held.shape[0], LANES), 1)
    means = [held[:, LANES + 4 + i : LANES + 5 + i] for i in range(2)]
    shared = jnp.concatenate([held[:, NL:LANES], jnp.zeros((held.shape[0], LANES - NL), F32)], axis=1)
    for i in range(2):
        shared = jnp.where(lane == NL + i, means[i], shared)
    for device in range(GRP):
        spread[device] = shared
    query_grad[...] = sums[1][:, :local]
    half = sums[1].shape[0] // 2
    for i in range(2):
        source_grad[i] = sums[1][i * half : (i + 1) * half, local:]


def latent_kernel(place, parts, numbers, hat, scale, gain, latents_grad, gain_grad):
    rows = (parts[0] + parts[1]) + (parts[2] + parts[3])
    width = gain.shape[1] * DP
    across = jnp.transpose(jnp.concatenate([rows, jnp.zeros_like(rows)], axis=0))
    direct = jnp.transpose(jnp.concatenate([numbers[...], jnp.zeros_like(numbers)], axis=0))
    hats = jnp.transpose(jnp.concatenate([hat[...], jnp.zeros_like(hat)], axis=0))[:NL, :NL]
    grad = across[:NL, :NL]
    normed = grad * gain[...] - rows[:, NL : NL + 1] / width - hats * (rows[:, NL + 1 : NL + 2] / width)
    latents_grad[...] = direct[:NL, :NL] + scale[:, :1] * normed
    gain_grad[...] = jnp.sum(grad * hats, axis=0, keepdims=True)


def layer_sum_kernel(sums, up_grad, down_grad, in_grad, out_grad):
    wide = up_grad.shape[1]
    local = out_grad.shape[1]
    up_grad[...] = sums[:, :wide].astype(F32)
    down_grad[...] = sums[:, wide : 2 * wide].astype(F32)
    for i in range(3):
        in_grad[i] = sums[:, 2 * wide + i * local : 2 * wide + (i + 1) * local].astype(F32)
    out_grad[...] = sums[:, 2 * wide + 3 * local :].astype(F32)


def sum_over_rings(first_moved, last_moved, after):
    moved = first_moved + last_moved
    shapes = [parts[0].shape[1:] for parts in (first_moved, last_moved)]
    blocks = call(sum_kernel, [(shape, BF) for shape in shapes for _ in range(4)], moved, after=after)
    return ring_moves(blocks[:4], False) + ring_moves(blocks[4:], True), blocks[0]


def last_sums(moved, after):
    rows, local = moved[0].shape[0], moved[4].shape[1] // 2
    outs = [(rows, local), (rows, local), (2, rows // 2, local), (rows, 2 * LANES), (GRP, rows, LANES), (8, rows)]
    return call(last_sum_kernel, [(shape, F32) for shape in outs], moved, after=after)


def grp_gather(values):
    spread = jnp.broadcast_to(values[None], (GRP,) + values.shape)
    return lax.all_to_all(spread, "grp", 0, 0)


def swap(blocks):
    return lax.all_to_all(blocks, "grp", 0, 0)


def total(parts):
    return (parts[0] + parts[1]) + (parts[2] + parts[3])


def row_norm(values):
    center = values - jnp.mean(values, axis=-1, keepdims=True)
    spread = jnp.mean(center * center, axis=-1, keepdims=True)
    scale_rows = lax.rsqrt(spread + EPSILON)
    return center * scale_rows, scale_rows


def row_norm_back(grad_normed, normed, scale_rows, scale_gain):
    grad_hat = grad_normed * scale_gain
    return scale_rows * (
        grad_hat
        - jnp.mean(grad_hat, axis=-1, keepdims=True)
        - normed * jnp.mean(grad_hat * normed, axis=-1, keepdims=True)
    )


def shards(
    caption_token_index,
    lengths,
    slot_image_pair,
    features,
    text_table,
    latents,
    sampler_gain,
    sampler_query,
    sampler_source,
    sampler_mixer,
    norm_gain_one,
    attention_in,
    norm_gain_two,
    attention_out,
    norm_gain_three,
    feed_up,
    norm_gain_four,
    feed_down,
    cotangent,
):
    group = lax.axis_index("grp")
    place = lax.axis_index(DP_AXES)
    width = feed_down.shape[1] * DP
    hidden = feed_down.shape[0] * GRP
    own = width // DP
    local = attention_out.shape[0]
    local_ff = feed_up.shape[1]
    patches, feature_width = features.shape[1:]
    tokens = cotangent.shape[1]
    spans = caption_token_index.shape[1]
    own_rows = tokens // GRP

    quarter = patches // GRP
    place_row = jnp.reshape(group, (1,)).astype(jnp.int32)
    (first_part,) = call(
        pack_kernel,
        [((own, 7 * local + feature_width + LANES), BF)],
        [
            jnp.transpose(attention_in, (1, 0, 2)),
            attention_out.T,
            sampler_mixer.T,
            jnp.transpose(sampler_source, (1, 0, 2)),
            features[0],
            sampler_query,
            latents,
        ],
        specs={4: pl.BlockSpec((quarter, feature_width), lambda i, s: (s[0], 0))},
        scalars=(place_row,),
    )
    second_part = jnp.concatenate([feed_up, feed_down.T], axis=1)
    first_all = lax.all_gather(first_part, DP_AXES, axis=0, tiled=True)
    second_all = lax.all_gather(second_part, DP_AXES, axis=0, tiled=True)

    def first_spec(number, columns):
        return pl.BlockSpec((width, columns), lambda *_: (0, number))

    table_rows_here = text_table.shape[0]
    table_block = lax.all_to_all(text_table, "grp", 1, 0, tiled=True)
    x, y, core = coordinates()
    flat_ids = caption_token_index[0]
    numbers = jnp.stack(
        [
            (flat_ids // 256).astype(BF),
            (flat_ids % 256).astype(BF),
            sampler_gain,
            norm_gain_one,
            norm_gain_three,
            norm_gain_four,
            jnp.pad(norm_gain_two, (0, own - norm_gain_two.shape[0])),
        ]
    )
    numbers = gather_offsets(jnp.pad(numbers, ((0, 16 - numbers.shape[0]), (0, 0))))
    wide_numbers = numbers.astype(F32)
    by_offset = (wide_numbers[:, :, :, 0] * 256 + wide_numbers[:, :, :, 1]).astype(jnp.int32)
    placed = jnp.moveaxis(jnp.roll(wide_numbers[:, :, :, 2:7], (core, x, y), axis=(0, 1, 2)), 0, 2)
    gains = placed
    query_gain, gain_one, gain_three, gain_four, gain_two = (
        gains[:, :, :, i].reshape(1, width) for i in range(5)
    )
    gain_two = gain_two.reshape(DP, own)[:, : norm_gain_two.shape[0]].reshape(1, local)

    def block_rows(ids):
        span = table_rows_here * DP
        held = ids % span // table_rows_here == place
        return jnp.where(held, ids // span * table_rows_here + ids % table_rows_here, -1)

    def one_hot(ids):
        return (block_rows(ids)[:, None] == jnp.arange(GRP * table_rows_here, dtype=jnp.int32)[None]).astype(BF)

    text_places = block_rows(by_offset.reshape(1, -1))
    picked = dot(one_hot(by_offset.reshape(-1)), table_block, 1, 0).astype(BF)
    text_cols = scatter_offsets(picked.reshape(CS, XS, YS, spans, local))
    text_parts = grp_gather(text_cols)

    split_first = first_all.reshape(DP, own, first_all.shape[1])
    (pair_parts,) = call(
        pair_kernel,
        [((GRP, quarter, feature_width), BF)],
        [split_first],
        specs={0: pl.BlockSpec((1, quarter, feature_width), lambda i, s: (s[0], 0, 3))},
        scalars=(slot_image_pair,),
        after=(text_parts,),
    )
    pair_rows = swap(pair_parts).reshape(patches, feature_width)
    small_spec = first_spec(36, LANES)
    mixer_spec = first_spec(4, local)
    vector_rows = width // LANES
    latent_values, latent_hat_t, latent_scale, query_input, query_rows, vectors = call(
        query_kernel,
        [
            ((NL, width), F32),
            ((width, LANES), F32),
            ((NL, LANES), F32),
            ((NL, width), BF),
            ((NL + 16, local), F32),
            ((2 * vector_rows, LANES), F32),
        ],
        [first_all, first_all, query_gain, gain_two, first_all],
        specs={0: small_spec, 1: first_spec(8, local), 4: first_spec(3, local)},
    )
    mixed, sampled, sources, sampler_prob = call(
        sampler_kernel,
        [
            ((GRP, NL // GRP, width), F32),
            ((NL, local), BF),
            ((patches, 2 * local), BF),
            ((local // RHD, NL, patches), F32),
        ],
        [pair_rows, query_rows, split_first, split_first, first_all],
        specs={
            2: pl.BlockSpec((DP, own // 2, local), lambda *_: (0, 0, 5)),
            3: pl.BlockSpec((DP, own // 2, local), lambda *_: (0, 1, 5)),
            4: mixer_spec,
        },
    )
    latent_spec = pl.BlockSpec((NL // GRP, width), lambda i, s: (s[0], 0))
    (images,) = call(
        image_kernel,
        [((GRP, NL // GRP, width), BF)],
        [swap(mixed), latent_values],
        specs={1: latent_spec},
        scalars=(place_row,),
    )
    image_parts = swap(images)

    out_spec = first_spec(3, local)
    in_spec = first_spec(0, 3 * local)
    own_spec = pl.BlockSpec((own_rows, width), lambda i, s: (s[0], 0))
    blocks = ((GRP, own_rows, width), BF)
    wide_blocks = ((GRP, own_rows, width + LANES), BF)
    inputs, first_input, projected, prob, attended, branch_parts = call(
        attention_kernel,
        [
            ((tokens, width), BF),
            ((tokens, width), BF),
            ((tokens, 3 * local), BF),
            ((local // HD, tokens, tokens), F32),
            ((tokens, local), F32),
            ((GRP, own_rows, width + 2 * LANES), BF),
        ],
        [image_parts, text_parts, gain_one, first_all, gain_two, first_all, vectors],
        specs={3: in_spec, 5: out_spec},
        scalars=(lengths,),
    )
    middle, branch, third_input, second_numbers, gain_out = call(
        middle_kernel,
        [
            ((own_rows, width), F32),
            ((own_rows, width), F32),
            blocks,
            ((own_rows, LANES), F32),
            ((1, width), F32),
        ],
        [swap(branch_parts), inputs, gain_three],
        specs={1: own_spec},
        scalars=(place_row,),
    )

    grad_output = cotangent[0]
    hidden_block = 1024
    steps = local_ff // hidden_block
    up_spec = pl.BlockSpec((width, hidden_block), lambda i: (0, i))
    down_spec = pl.BlockSpec((width, hidden_block), lambda i: (0, steps + i))
    columns_spec = pl.BlockSpec((tokens, hidden_block), lambda i: (0, i))
    row_spec = pl.BlockSpec((1, hidden_block), lambda i: (0, i))
    wide = ((tokens, local_ff), F32)
    (grad_fourth,) = call(
        grad_fourth_kernel,
        [wide],
        [grad_output, second_all],
        specs={1: down_spec},
        out_specs={0: columns_spec},
        grid=(steps,),
    )
    activated, slope, fourth_stats, third_rows = call(
        hidden_kernel,
        [wide, wide, ((STATS, tokens), F32), ((tokens, width), BF)],
        [swap(third_input), grad_fourth, gain_four, second_all],
        specs={3: up_spec},
        grid=(steps,),
    )
    fourth_stats = [fourth_stats] + [
        lax.ppermute(fourth_stats, "grp", [((i + step) % GRP, i) for i in range(GRP)]) for step in range(1, GRP)
    ]
    fourth_input, grad_up_rows, grad_gain_four, third_parts = call(
        hidden_back_kernel,
        [((tokens, local_ff), BF), ((tokens, local_ff), BF), ((1, local_ff), F32), blocks],
        [*fourth_stats, activated, slope, grad_fourth, gain_four, second_all],
        specs={4: columns_spec, 5: columns_spec, 6: columns_spec, 7: row_spec, 8: up_spec},
        out_specs={0: columns_spec, 1: columns_spec, 2: row_spec},
        grid=(steps,),
        scratch=[pltpu.VMEM((tokens, LANES), F32), pltpu.VMEM((tokens, width), F32)],
    )
    third_parts = swap(third_parts)
    outer_block = 512
    wide_columns = 2 * local_ff + 4 * local
    down_first = local_ff // outer_block
    down_grads = wide_outer([(grad_output, fourth_input)], outer_block, wide_columns, down_first)
    (down_parts,) = call(
        down_kernel,
        [blocks],
        [fourth_input, second_all],
        specs={0: columns_spec, 1: down_spec},
        grid=(steps,),
        scratch=[pltpu.VMEM((tokens, width), F32)],
    )
    grad_middle, branch_low, gain_three_grad = call(
        third_back_kernel,
        [((own_rows, width), F32), wide_blocks, ((1, width), F32)],
        [third_parts, middle, branch, grad_output, gain_three, gain_out, second_numbers],
        specs={3: own_spec},
        scalars=(place_row,),
        after=(down_grads,),
    )

    ff_grads = wide_outer([(third_rows, grad_up_rows)], outer_block, wide_columns, 0, down_grads)

    grad_branch, second_input, grad_projected, grad_gain_two, first_parts = call(
        attention_back_kernel,
        [
            ((tokens, width), BF),
            ((tokens, local), BF),
            ((tokens, 3 * local), BF),
            ((1, local), F32),
            blocks,
        ],
        [swap(branch_low), attended, projected, prob, gain_two, first_all, first_all],
        specs={5: out_spec, 6: in_spec},
        after=(ff_grads,),
    )
    layer_grads = wide_outer(
        [(first_input, grad_projected), (grad_branch, second_input)],
        outer_block,
        wide_columns,
        2 * local_ff // outer_block,
        ff_grads,
    )
    layer_sums = lax.psum_scatter(layer_grads, DP_AXES, scatter_dimension=0, tiled=True)
    (input_low,) = call(
        first_back_kernel,
        [wide_blocks],
        [swap(first_parts), inputs, gain_one, grad_middle, gain_three_grad],
        specs={1: own_spec},
        after=(down_parts,),
        scalars=(place_row,),
        scratch=[pltpu.VMEM((2 * vector_rows, LANES), F32)],
    )
    input_low = swap(input_low)

    per_own = norm_gain_two.shape[0]
    gain_two_row = jnp.pad(grad_gain_two.reshape(DP, per_own), ((0, 0), (0, own - per_own))).reshape(1, width)
    image_low, grad_keys, grad_values, grad_query, extra = call(
        sampler_back_kernel,
        [((NL, width), BF), ((patches, local), BF), ((patches, local), BF), ((NL, local), BF), ((width, 2 * LANES), F32)],
        [input_low, first_all, query_rows, sources, sampler_prob, first_all, grad_gain_four, gain_two_row],
        specs={1: mixer_spec, 5: first_spec(8, local)},
        scratch=[pltpu.VMEM((2 * LANES, width), F32)],
    )

    paths = (
        [(image_low, sampled), (extra,)],
        [(query_input, grad_query), (pair_rows, grad_keys, grad_values)],
    )
    arrived = fetch(outer_blocks(paths, 256), 0, 0, 1)

    (text_low,) = call(
        text_kernel,
        [((spans, local), BF)],
        [input_low],
        specs={0: pl.BlockSpec((2, own_rows, local), lambda i, s: (1, 0, s[0]))},
        scalars=(place_row,),
    )
    text_parts = ring(text_low, 1)
    first_held, last_held = outer_blocks(paths, 256, arrived, text_parts[1:])
    (text_column,) = call(stack_kernel, [((YS, spans, local), BF)], text_parts, after=first_held[:1])
    text_parts = ring(text_column, 0)
    (output_rows,) = call(
        output_kernel, [blocks], [swap(down_parts), middle], after=first_held[:1]
    )
    first_moved, last_moved = both_ways(first_held, last_held)
    (text_same,) = call(
        stack_kernel, [((XS, YS, spans, local), BF)], text_parts, after=(*first_moved[1:], *last_moved[1:], output_rows)
    )
    moved, first_block = sum_over_rings(first_moved, last_moved, ())
    (table_sums,) = call(
        table_kernel,
        [((GRP * table_rows_here, local), BF)],
        [text_places, text_same, fetch(text_same, 0, 0, 1)],
        after=(first_block,),
    )
    table_rows = lax.all_to_all(table_sums, "grp", 0, 1, tiled=True)
    table_grad = table_rows.astype(F32)

    layer_output, input_grad = call(
        widen_kernel, [((tokens, width), F32)] * 2, [swap(output_rows), input_low]
    )
    mixer_grad, query_grad, source_grad, numbers, shared, gain_grads = last_sums(moved, (table_sums,))

    up_grad, down_grad, in_grad, out_grad = call(
        layer_sum_kernel,
        [((own, local_ff), F32), ((own, local_ff), F32), ((3, own, local), F32), ((own, local), F32)],
        [layer_sums],
    )
    latents_grad, sampler_gain_grad = call(
        latent_kernel,
        [((NL, own), F32), ((1, own), F32)],
        [swap(shared), numbers, latent_hat_t, latent_scale, sampler_gain.astype(F32)[None]],
        specs={2: pl.BlockSpec((own, LANES), lambda i, s: (s[0], 0))},
        after=(table_rows, out_grad),
        scalars=(jnp.reshape(place, (1,)).astype(jnp.int32),),
    )
    return (
        layer_output[None],
        input_grad[None],
        table_grad,
        latents_grad,
        sampler_gain_grad[0],
        query_grad,
        jnp.transpose(source_grad, (1, 0, 2)),
        mixer_grad.T,
        gain_grads[0],
        jnp.transpose(in_grad, (1, 0, 2)),
        gain_grads[3, :per_own],
        out_grad.T,
        gain_grads[1],
        up_grad,
        gain_grads[2],
        down_grad.T,
    )


def solution(mesh):
    mesh = Mesh(mesh.devices.reshape(GRP, XS, YS, CS), ("grp",) + DP_AXES)
    return jax.shard_map(
        shards,
        mesh=mesh,
        in_specs=(
            P(DP_AXES, None),
            P(DP_AXES),
            P(DP_AXES),
            P(DP_AXES, None, None),
            P(("grp",) + DP_AXES, None),
            P(None, DP_AXES),
            P(DP_AXES),
            P(DP_AXES, "grp"),
            P(DP_AXES, None, "grp"),
            P("grp", DP_AXES),
            P(DP_AXES),
            P(DP_AXES, None, "grp"),
            P(("grp",) + DP_AXES),
            P("grp", DP_AXES),
            P(DP_AXES),
            P(DP_AXES, "grp"),
            P(("grp",) + DP_AXES),
            P("grp", DP_AXES),
            P(DP_AXES, None, None),
        ),
        out_specs=(
            P(DP_AXES, None, None),
            P(DP_AXES, None, None),
            P(("grp",) + DP_AXES, None),
            P(None, DP_AXES),
            P(DP_AXES),
            P(DP_AXES, "grp"),
            P(DP_AXES, None, "grp"),
            P("grp", DP_AXES),
            P(DP_AXES),
            P(DP_AXES, None, "grp"),
            P(("grp",) + DP_AXES),
            P("grp", DP_AXES),
            P(DP_AXES),
            P(DP_AXES, "grp"),
            P(("grp",) + DP_AXES),
            P("grp", DP_AXES),
        ),
        check_vma=False,
    )
```
